32 devices in a mesh: bucket: 4 (over x, core), ctx: 8 (over z, y).
Axes of the slice: x: 2, y: 2, z: 4, core: 2. Of those that a mesh axis runs over, the one named last changes fastest.
Arguments:
- hidden_in: bfloat16 [4, 1, 1024, 1024], P('bucket', None, 'ctx'), may hold values from -6 to 6
- lengths: int32 [4, 1, 8], P('bucket'), may hold values from 0 to 1024, as said below
- w_query: bfloat16 [1024, 1024], P(('bucket', 'ctx')), may hold values from -0.1875 to 0.1875
- w_key: bfloat16 [1024, 1024], P(('bucket', 'ctx')), may hold values from -0.1875 to 0.1875
- w_value: bfloat16 [1024, 1024], P(('bucket', 'ctx')), may hold values from -0.1875 to 0.1875
- b_query: bfloat16 [1024], P(('bucket', 'ctx')), may hold values from -3 to 3
- b_value: bfloat16 [1024], P(('bucket', 'ctx')), may hold values from -0.119628906 to 0.119628906
- w_out: bfloat16 [1024, 1024], P(('bucket', 'ctx')), may hold values from -2 to 2
- b_out: bfloat16 [1024], P(('bucket', 'ctx')), may hold values from -3 to 3
- first_gain: bfloat16 [1024], P(('bucket', 'ctx')), may hold values from 0.5 to 1.5
- first_shift: bfloat16 [1024], P(('bucket', 'ctx')), may hold values from -3 to 3
- w_up: bfloat16 [1024, 4096], P(('bucket', 'ctx')), may hold values from -0.1875 to 0.1875
- b_up: bfloat16 [4096], P(('bucket', 'ctx')), may hold values from -3 to 3
- w_down: bfloat16 [4096, 1024], P(('bucket', 'ctx')), may hold values from -0.09375 to 0.09375
- b_down: bfloat16 [1024], P(('bucket', 'ctx')), may hold values from -3 to 3
- second_gain: bfloat16 [1024], P(('bucket', 'ctx')), may hold values from 0.5 to 1.5
- second_shift: bfloat16 [1024], P(('bucket', 'ctx')), may hold values from -3 to 3
- cotangent: bfloat16 [4, 1, 1024, 1024], P('bucket', None, 'ctx'), may hold values from -6 to 6
Outputs:
- hidden_out: bfloat16 [4, 1, 1024, 1024], P('bucket', None, 'ctx')
- grad_in: float32 [4, 1, 1024, 1024], P('bucket', None, 'ctx')
- grad_w_query: float32 [1024, 1024], P(('bucket', 'ctx'))
- grad_w_key: float32 [1024, 1024], P(('bucket', 'ctx'))
- grad_w_value: float32 [1024, 1024], P(('bucket', 'ctx'))
- grad_b_query: float32 [1024], P(('bucket', 'ctx'))
- grad_b_value: float32 [1024], P(('bucket', 'ctx'))
- grad_w_out: float32 [1024, 1024], P(('bucket', 'ctx'))
- grad_b_out: float32 [1024], P(('bucket', 'ctx'))
- grad_first_gain: float32 [1024], P(('bucket', 'ctx'))
- grad_first_shift: float32 [1024], P(('bucket', 'ctx'))
- grad_w_up: float32 [1024, 4096], P(('bucket', 'ctx'))
- grad_b_up: float32 [4096], P(('bucket', 'ctx'))
- grad_w_down: float32 [4096, 1024], P(('bucket', 'ctx'))
- grad_b_down: float32 [1024], P(('bucket', 'ctx'))
- grad_second_gain: float32 [1024], P(('bucket', 'ctx'))
- grad_second_shift: float32 [1024], P(('bucket', 'ctx'))
The draws below stay inside these ranges and needn't reach their ends.
Inputs may be any that keep to these rules, and one draw needn't show every extreme that they name: `lengths`: in length group b (counting from 0) with slot = 1024 // (8 >> b), entries 0 to (8 >> b) - 1 of each pack lie from slot - slot // 4 to slot, and one of them in each pack is exactly slot; the later entries are 0. The single sequence of the last group fills all 1024 slots.
All inputs are finite; a program needn't handle non-finite values.
Results may differ from the reference program's by a relative error of at most 0.018.
Values may be sent and summed in bfloat16 or wider, within the bound.
A program may use at most 192 MiB of HBM per device.

```python
import math
import jax
import jax.numpy as jnp
from jax import lax

D = 1024
HEADS = 16
HEAD_DIM = 64
FF = 4096
SEQS = 1
BUCKETS = 4
MAX_SEQS = 8
SEQ_LEN = 1024


def draw_lengths(key, part):
    key = jax.random.fold_in(key, 11)
    group_ids = jnp.arange(BUCKETS, dtype=jnp.int32)[:, None, None]
    counts = jnp.right_shift(jnp.int32(MAX_SEQS), group_ids)
    slots = SEQ_LEN // counts
    least = slots - slots // 4
    drawn = jax.random.randint(jax.random.fold_in(key, 1), (BUCKETS, SEQS, MAX_SEQS), least, slots + 1, dtype=jnp.int32)
    full_pick = jax.random.randint(jax.random.fold_in(key, 2), (BUCKETS, SEQS, 1), 0, counts, dtype=jnp.int32)
    entry = jnp.arange(MAX_SEQS, dtype=jnp.int32)[None, None, :]
    drawn = jnp.where(entry == full_pick, slots, drawn)
    return jnp.where(entry < counts, drawn, 0).astype(jnp.int32)


def with_spikes(values, key, source, target, blocks, factor):
    def block_of(dim):
        return (jnp.arange(values.shape[dim]) // (values.shape[dim] // blocks)).reshape((-1,) + (1,) * (values.ndim - 1 - dim))

    near = jax.random.permutation(key, blocks)[block_of(target)]
    other_side = (block_of(target) + blocks // 2) % blocks
    return jnp.where((block_of(source) == near) | (block_of(source) == other_side), factor * values, values)


def level_of(own_key, shape, cuts, low, top_value):
    gain = 1.0
    for position, parts in cuts:
        heights = jax.random.uniform(jax.random.fold_in(jax.random.fold_in(own_key, 6), position), (parts,), jnp.float32, low / len(cuts), top_value / len(cuts))
        gain = gain * jnp.repeat(jnp.exp(heights), shape[position] // parts).reshape((-1,) + (1,) * (len(shape) - 1 - position))
    return gain


def scatter_about(key, extent, width, reach, split=(), kind=jnp.bfloat16):
    level = level_of(key, extent, split, -0.22, 0.18) if split else 1.0
    values = jax.random.normal(key, extent, jnp.float32) * width * level
    return jnp.minimum(jnp.maximum(values, -reach), reach).astype(kind)


def heavy_noise(key, shape, scale, most, split, heavy, held_as=jnp.bfloat16):
    array = scale * jax.random.normal(key, shape, jnp.float32)
    if split:
        array = array * level_of(key, shape, split, -0.22, 0.18)
    return jnp.clip(with_spikes(array, jax.random.fold_in(key, 3), *heavy), -most, most).astype(held_as)


def setup_inputs(seed: int = 0) -> dict:
    splits = jax.random.split(jax.random.key(seed), 19)
    hidden_in = heavy_noise(splits[0], (BUCKETS, SEQS, SEQ_LEN, D), 1.0, 6.0, ((0, 4), (2, 8)), (2, 3, 8, 2.0))
    lengths = draw_lengths(jax.random.fold_in(splits[18], 71), 0)
    w_query = scatter_about(splits[2], (D, D), D ** -0.5, 0.1875, ((0, 32),))
    w_key = scatter_about(splits[3], (D, D), D ** -0.5, 0.1875, ((0, 32),))
    w_value = scatter_about(splits[4], (D, D), D ** -0.5, 0.1875, ((0, 32),))
    b_query = scatter_about(splits[5], (D,), 0.5, 3.0, ((0, 32),))
    b_value = scatter_about(splits[6], (D,), 0.02, 0.119628906, ((0, 32),))
    w_out = scatter_about(splits[7], (D, D), (max(1, 8 * D // SEQ_LEN)) ** -0.5, 2.0, ((0, 32),))
    b_out = scatter_about(splits[8], (D,), 0.5, 3.0, ((0, 32),))
    first_gain = jnp.clip(1.0 + 0.1 * jax.random.normal(splits[9], (D,), jnp.float32), 0.5, 1.5).astype(jnp.bfloat16)
    first_shift = scatter_about(splits[10], (D,), 0.5, 3.0, ((0, 32),))
    w_up = scatter_about(splits[11], (D, FF), D ** -0.5, 0.1875, ((0, 32),))
    b_up = scatter_about(splits[12], (FF,), 0.5, 3.0, ((0, 32),))
    w_down = scatter_about(splits[13], (FF, D), FF ** -0.5, 0.09375, ((0, 32),))
    b_down = scatter_about(splits[14], (D,), 0.5, 3.0, ((0, 32),))
    second_gain = jnp.clip(1.0 + 0.1 * jax.random.normal(splits[15], (D,), jnp.float32), 0.5, 1.5).astype(jnp.bfloat16)
    second_shift = scatter_about(splits[16], (D,), 0.5, 3.0, ((0, 32),))
    cotangent = scatter_about(splits[17], (BUCKETS, SEQS, SEQ_LEN, D), 1.0, 6.0, ((0, 4), (2, 8)))
    return dict(hidden_in=hidden_in, lengths=lengths, w_query=w_query, w_key=w_key, w_value=w_value, b_query=b_query, b_value=b_value, w_out=w_out, b_out=b_out, first_gain=first_gain, first_shift=first_shift, w_up=w_up, b_up=b_up, w_down=w_down, b_down=b_down, second_gain=second_gain, second_shift=second_shift, cotangent=cotangent)


EPSILON = 1e-05
NEG_FILL = -1e+30
HIGHEST_MODE = lax.Precision.HIGHEST

@jax.custom_vjp
def low(v):
    return lax.optimization_barrier(v.astype(jnp.bfloat16)).astype(jnp.float32)

@jax.custom_vjp
def low_back(v):
    return v

def low_keep(v):
    return (low(v), None)

def low_pass(kept, grad):
    return (grad,)

def back_keep(v):
    return (v, None)

def back_low(kept, grad):
    return (low(grad),)
low.defvjp(low_keep, low_pass)
low_back.defvjp(back_keep, back_low)

def both_ways(values):
    return low(low_back(values))

def product(left, right):
    return jnp.dot(left, right, preferred_element_type=jnp.float32, precision=HIGHEST_MODE)

def layer_norm(summed, gain_vec, shift_vec):
    average = lax.optimization_barrier(jnp.mean(summed, axis=-1, keepdims=True))
    centred = summed - average
    variance = lax.optimization_barrier(jnp.mean(centred * centred, axis=-1, keepdims=True))
    return centred * lax.rsqrt(variance + EPSILON) * gain_vec + shift_vec

def gelu_value(values):
    return 0.5 * values * (1.0 + jax.scipy.special.erf(values * 0.7071067811865476))

def attend(query_block, key_heads, value_heads, allowed):
    raw = jnp.einsum('qhd,khd->hqk', query_block, key_heads, precision=HIGHEST_MODE)
    scores = low_back(raw * HEAD_DIM ** (-0.5))
    scores = jnp.where(allowed[None, None, :], scores, NEG_FILL)
    largest = lax.optimization_barrier(jnp.max(scores, axis=-1, keepdims=True))
    raised = jnp.exp(scores - largest)
    probs = raised / lax.optimization_barrier(jnp.sum(raised, axis=-1, keepdims=True))
    return jnp.einsum('hqk,khd->qhd', low(probs), value_heads, precision=HIGHEST_MODE)

def layer(tokens, length, params):
    query_mat, key_mat, value_mat, query_bias, value_bias, out_mat, out_bias, gain_one, shift_one, up_mat, up_bias, down_mat, down_bias, gain_two, shift_two = params
    query = both_ways(product(tokens, query_mat) + query_bias)
    keys = both_ways(product(tokens, key_mat))
    values = both_ways(product(tokens, value_mat) + value_bias)
    seq_len = tokens.shape[0]
    block_rows = math.gcd(seq_len, 512)
    allowed = jnp.arange(seq_len, dtype=jnp.int32) < length
    key_heads = keys.reshape(seq_len, HEADS, HEAD_DIM)
    value_heads = values.reshape(seq_len, HEADS, HEAD_DIM)
    query_blocks = query.reshape(seq_len // block_rows, block_rows, HEADS, HEAD_DIM)
    blockwise = jax.checkpoint(attend)
    attended_all = lax.map(lambda query_block: blockwise(query_block, key_heads, value_heads, allowed), query_blocks)
    attended = both_ways(attended_all.reshape(seq_len, D))
    branch = low_back(product(attended, out_mat) + out_bias)
    middle = layer_norm(tokens + branch, gain_one, shift_one)
    pre_act = low_back(product(both_ways(middle), up_mat) + up_bias)
    activated = both_ways(gelu_value(pre_act))
    ffn_out = low_back(product(activated, down_mat) + down_bias)
    return layer_norm(middle + ffn_out, gain_two, shift_two)

def reference(hidden_in, lengths, w_query, w_key, w_value, b_query, b_value, w_out, b_out, first_gain, first_shift, w_up, b_up, w_down, b_down, second_gain, second_shift, cotangent):
    params = tuple((argument.astype(jnp.float32) for argument in (w_query, w_key, w_value, b_query, b_value, w_out, b_out, first_gain, first_shift, w_up, b_up, w_down, b_down, second_gain, second_shift)))
    packs = hidden_in.astype(jnp.float32)
    seq_lengths = lengths.astype(jnp.int32)
    checked = jax.checkpoint(layer)

    def whole(inputs, weights):
        results = []
        for group in range(BUCKETS):
            count = MAX_SEQS >> group
            slot = SEQ_LEN // count
            group_seqs = inputs[group].reshape(SEQS * count, slot, D)
            group_lens = seq_lengths[group, :, :count].reshape(SEQS * count)
            mapped = lax.map(lambda entries: checked(entries[0], entries[1], weights), (group_seqs, group_lens))
            results.append(mapped.reshape(SEQS, SEQ_LEN, D))
        return jnp.stack(results)
    outputs, pullback = jax.vjp(whole, packs, params)
    grad_inputs, grad_params = pullback(cotangent.astype(jnp.float32))
    grad_w_query, grad_w_key, grad_w_value, grad_b_query, grad_b_value, grad_w_out, grad_b_out, grad_first_gain, grad_first_shift, grad_w_up, grad_b_up, grad_w_down, grad_b_down, grad_second_gain, grad_second_shift = grad_params
    return (outputs.astype(jnp.bfloat16), grad_inputs, grad_w_query, grad_w_key, grad_w_value, grad_b_query, grad_b_value, grad_w_out, grad_b_out, grad_first_gain, grad_first_shift, grad_w_up, grad_b_up, grad_w_down, grad_b_down, grad_second_gain, grad_second_shift)
```

```python
import functools
import math

import jax
import jax.numpy as jnp
from jax import lax
from jax.experimental import pallas as pl
from jax.experimental.pallas import tpu as pltpu
from jax.sharding import PartitionSpec as P

HEAD_DIM = 64
EPSILON = 1e-05
NEG_FILL = -1e30
MESH_ID = pl.DeviceIdType.MESH
F32, BF16 = jnp.float32, jnp.bfloat16
ROWS = 32
PIECES = 12
VMEM_LIMIT = 62 * 2**20


def when(condition):
    return pl.when(condition)


def place():
    bucket, ctx = lax.axis_index("bucket"), lax.axis_index("ctx")
    return bucket // 2, ctx % 2, ctx // 2, bucket % 2


def device(x, y, z, core):
    return (x * 2 + core, z * 2 + y)


def owner(x, y, z, core):
    return (x * 2 + core) * 8 + z * 2 + y


def remote(src, dst, send_sem, recv_sem, target):
    return pltpu.make_async_remote_copy(
        src_ref=src, dst_ref=dst, send_sem=send_sem, recv_sem=recv_sem,
        device_id=target, device_id_type=MESH_ID,
    )


def bytes_of(ref, sem):
    return pltpu.make_async_copy(ref, ref, sem)


class Route:
    def __init__(self):
        self.x, self.y, self.z, self.core = x, y, z, core = place()
        self.ax, self.ay = jnp.where(core == 0, 1 - x, x), jnp.where(core == 0, y, 1 - y)
        self.bx, self.by = jnp.where(core == 1, 1 - x, x), jnp.where(core == 1, y, 1 - y)
        self.a = device(self.ax, self.ay, z, core)
        self.b = device(self.bx, self.by, z, core)
        self.sibling = device(x, y, z, 1 - core)
        self.up = device(x, y, jnp.minimum(z + 1, 3), core)
        self.down = device(x, y, jnp.maximum(z - 1, 0), core)

    def greet(self):
        z = self.z
        barrier = pltpu.get_barrier_semaphore()
        for target in (self.a, self.b, self.sibling):
            pl.semaphore_signal(barrier, inc=1, device_id=target, device_id_type=MESH_ID)

        @when(z < 3)
        def _():
            pl.semaphore_signal(barrier, inc=1, device_id=self.up, device_id_type=MESH_ID)

        @when(z > 0)
        def _():
            pl.semaphore_signal(barrier, inc=1, device_id=self.down, device_id_type=MESH_ID)

        pl.semaphore_wait(barrier, 3 + (z < 3).astype(jnp.int32) + (z > 0).astype(jnp.int32))


class Gatherer:
    stages = 7

    def __init__(self, route, count, own, block, span, sems):
        self.rt, self.count, self.own, self.block, self.span = route, count, own, block, span
        (self.zs, self.zr, self.ps, self.ar, self.br, self.dr, self.ls) = sems

    def spread(self, c, src, j, jz, to_a, to_b, z_dirs):
        rt, dst = self.rt, self.block(c, j)
        if "up" in z_dirs:

            @when(rt.z < 3)
            def _():
                remote(src, dst, self.zs.at[0, c, jz], self.zr.at[c, jz], rt.up).start()

        if "down" in z_dirs:

            @when(rt.z > 0)
            def _():
                remote(src, dst, self.zs.at[1, c, jz], self.zr.at[c, jz], rt.down).start()

        if to_a:
            remote(src, dst, self.ps, self.ar.at[c, jz], rt.a).start()
        if to_b is not None:
            remote(src, dst, self.ps, self.br.at[c, to_b * 4 + jz], rt.b).start()
        remote(src, dst, self.ps, self.dr.at[c], rt.sibling).start()

    def near(self, k, action):
        for sign in (0,) if k == 0 else (-1, 1):
            zz = self.rt.z + sign * k

            @when((zz >= 0) & (zz <= 3))
            def _():
                action(zz, "up" if sign < 0 else "down")

    def own_stage(self, c):
        rt = self.rt
        j = owner(rt.x, rt.y, rt.z, rt.core)
        pltpu.make_async_copy(self.own(c), self.block(c, j), self.ls).start()
        self.spread(c, self.own(c), j, rt.z, True, 0, ("up", "down"))

    def z_stage(self, c, k):
        rt = self.rt

        def action(zz, direction):
            j = owner(rt.x, rt.y, zz, rt.core)
            bytes_of(self.block(c, j), self.zr.at[c, zz]).wait()
            self.spread(c, self.block(c, j), j, zz, True, 0, (direction,))

        self.near(k, action)

    def a_stage(self, c, k):
        rt = self.rt

        def action(zz, _):
            j = owner(rt.ax, rt.ay, zz, rt.core)
            bytes_of(self.block(c, j), self.ar.at[c, zz]).wait()
            self.spread(c, self.block(c, j), j, zz, False, 1, ())

        self.near(k, action)

    def b_stage(self, c, k):
        rt = self.rt

        def action(zz, _):
            for which, (xx, yy) in enumerate(((rt.bx, rt.by), (1 - rt.x, 1 - rt.y))):
                j = owner(xx, yy, zz, rt.core)
                bytes_of(self.block(c, j), self.br.at[c, which * 4 + zz]).wait()
                self.spread(c, self.block(c, j), j, zz, False, None, ())

        self.near(k, action)

    def stage(self, s, c):
        if s == 0:
            self.own_stage(c)
        if 1 <= s <= 3:
            self.z_stage(c, s)
        if 2 <= s <= 5:
            self.a_stage(c, s - 2)
        if 3 <= s <= 6:
            self.b_stage(c, s - 3)

    def arrived(self, c):
        bytes_of(self.span(16), self.dr.at[c]).wait()

    def finish(self):
        bytes_of(self.span(28 * self.count), self.ps).wait()
        bytes_of(self.span(self.count), self.ls).wait()

    def finish_z(self, c):
        rt = self.rt
        for zz in range(4):

            @when((rt.z < 3) & (rt.z >= zz))
            def _():
                bytes_of(self.span(1), self.zs.at[0, c, zz]).wait()

            @when((rt.z > 0) & (rt.z <= zz))
            def _():
                bytes_of(self.span(1), self.zs.at[1, c, zz]).wait()


def gather_sems(count):
    dma = pltpu.SemaphoreType.DMA
    return [dma((2, count, 4)), dma((count, 4)), dma(()), dma((count, 4)), dma((count, 8)), dma((count,)), dma(())]


def piece_row(c, j):
    return pl.multiple_of(jnp.where(c < 8, c * 1024 + ROWS * j, 8192 + 128 * j + ROWS * (c - 8)), ROWS)


def gather_kernel(x_ref, v_ref, w_ref, t_ref, *sems):
    rt = Route()
    main = Gatherer(
        rt, PIECES,
        lambda c: x_ref.at[pl.ds(pl.multiple_of(c * ROWS, ROWS), ROWS)],
        lambda c, j: w_ref.at[pl.ds(piece_row(c, j), ROWS)],
        lambda n: w_ref.at[pl.ds(0, n * ROWS)],
        sems[:7],
    )
    small = Gatherer(rt, 1, lambda c: v_ref, lambda c, j: t_ref.at[j], lambda n: t_ref.at[pl.ds(0, n)], sems[7:])
    rt.greet()

    def step(t, _):
        for s in range(Gatherer.stages):
            c = t - s

            @when(c == 0)
            def _():
                small.stage(s, 0)

            @when((c >= 0) & (c < PIECES))
            def _():
                main.stage(s, c)

        return 0

    lax.fori_loop(0, PIECES + Gatherer.stages - 1, step, 0)
    small.arrived(0)
    small.finish()
    small.finish_z(0)

    def last(c, _):
        main.arrived(c)
        main.finish_z(c)
        return 0

    lax.fori_loop(0, PIECES, last, 0)
    main.finish()


def gather_weights(shards, small):
    vmem, anywhere = pl.BlockSpec(memory_space=pltpu.VMEM), pl.BlockSpec(memory_space=pl.ANY)
    return pl.pallas_call(
        gather_kernel,
        out_shape=(
            jax.ShapeDtypeStruct((PIECES * 1024, 1024), BF16),
            jax.ShapeDtypeStruct((32, 16, 128), BF16),
        ),
        in_specs=[vmem, vmem],
        out_specs=(anywhere, vmem),
        scratch_shapes=gather_sems(PIECES) + gather_sems(1),
        compiler_params=pltpu.CompilerParams(collective_id=0, has_side_effects=True, vmem_limit_bytes=VMEM_LIMIT),
    )(shards, small)


def add_f32(left, right):
    return left.astype(F32) + right.astype(F32)


class Reducer:
    stages = 7

    def __init__(self, route, bufs, sems):
        self.rt = route
        (self.own, self.sib, self.rd, self.rb, self.ra, self.ru, self.rn, self.out) = bufs
        (self.sd_s, self.sd_r, self.sb_s, self.sb_r, self.sa_s, self.sa_r, self.sz_s, self.su_r, self.sn_r) = sems

    @staticmethod
    def slot(xx, yy, zz):
        return xx * 8 + zz * 2 + yy

    def add(self, c, k, other):
        self.own[c, k] = add_f32(self.own[c, k], other).astype(self.own.dtype)

    def to_sibling(self, c):
        remote(self.sib.at[c], self.rd.at[c], self.sd_s.at[c], self.sd_r.at[c], self.rt.sibling).start()

    def to_b(self, c):
        rt = self.rt
        bytes_of(self.rd.at[c], self.sd_r.at[c]).wait()
        for same_a in (0, 1):
            for zz in range(4):
                xx, yy = (rt.bx, rt.by) if same_a else (1 - rt.x, 1 - rt.y)
                k = self.slot(xx, yy, zz)
                self.add(c, k, self.rd[c, k])
                remote(self.own.at[c, k], self.rb.at[c, same_a * 4 + zz], self.sb_s.at[c], self.sb_r.at[c], rt.b).start()
        for same_a in (0, 1):
            for zz in range(4):
                xx, yy = (rt.x, rt.y) if same_a else (rt.ax, rt.ay)
                k = self.slot(xx, yy, zz)
                self.add(c, k, self.rd[c, k])

    def to_a(self, c):
        rt = self.rt
        bytes_of(self.rb.at[c], self.sb_r.at[c]).wait()
        for zz in range(4):
            k = self.slot(rt.ax, rt.ay, zz)
            self.add(c, k, self.rb[c, zz])
            remote(self.own.at[c, k], self.ra.at[c, zz], self.sa_s.at[c], self.sa_r.at[c], rt.a).start()
        for zz in range(4):
            self.add(c, self.slot(rt.x, rt.y, zz), self.rb[c, 4 + zz])

    def from_a(self, c):
        rt = self.rt
        bytes_of(self.ra.at[c], self.sa_r.at[c]).wait()
        for zz in range(4):
            self.add(c, self.slot(rt.x, rt.y, zz), self.ra[c, zz])

    def along_z(self, c, hop):
        rt = self.rt
        x, y = rt.x, rt.y

        @when(rt.z == hop)
        def _():
            for d in range(3, hop, -1):
                k = self.slot(x, y, d)
                if hop > 0:
                    bytes_of(self.ru.at[c, d - 1], self.su_r.at[c, d - 1]).wait()
                    self.add(c, k, self.ru[c, d - 1])
                remote(self.own.at[c, k], self.ru.at[c, d - 1], self.sz_s.at[c, d], self.su_r.at[c, d - 1], rt.up).start()
            if hop > 0:
                bytes_of(self.ru.at[c, hop - 1], self.su_r.at[c, hop - 1]).wait()

        at = 3 - hop

        @when(rt.z == at)
        def _():
            for d in range(at):
                k = self.slot(x, y, d)
                if at < 3:
                    bytes_of(self.rn.at[c, d], self.sn_r.at[c, d]).wait()
                    self.add(c, k, self.rn[c, d])
                remote(self.own.at[c, k], self.rn.at[c, d], self.sz_s.at[c, d], self.sn_r.at[c, d], rt.down).start()
            if at < 3:
                bytes_of(self.rn.at[c, at], self.sn_r.at[c, at]).wait()

    def total(self, c):
        rt = self.rt
        k = self.slot(rt.x, rt.y, rt.z)

        @when(rt.z == 0)
        def _():
            self.out[c] = add_f32(self.own[c, k], self.rn[c, 0])

        @when(rt.z == 3)
        def _():
            self.out[c] = add_f32(self.own[c, k], self.ru[c, 2])

        for at in (1, 2):

            @when(rt.z == at)
            def _():
                self.out[c] = add_f32(self.own[c, k], self.ru[c, at - 1]) + self.rn[c, at].astype(F32)

    def stage(self, s, c):
        if s == 0:
            self.to_sibling(c)
        if s == 1:
            self.to_b(c)
        if s == 2:
            self.to_a(c)
        if s == 3:
            self.from_a(c)
        if s >= 3:
            self.along_z(c, s - 3)
        if s == 6:
            self.total(c)

    def finish(self, c):
        rt = self.rt
        bytes_of(self.sib.at[c], self.sd_s.at[c]).wait()
        bytes_of(self.rb.at[c], self.sb_s.at[c]).wait()
        bytes_of(self.ra.at[c], self.sa_s.at[c]).wait()
        for d in range(4):

            @when(rt.z != d)
            def _():
                bytes_of(self.ra.at[c, 0], self.sz_s.at[c, d]).wait()


def reducer_bufs(count, block, dtype):
    sizes = (16, 16, 16, 8, 4, 3, 3)
    return [pltpu.VMEM((count, n) + block, dtype) for n in sizes] + [pltpu.VMEM((count,) + block, F32)]


def reducer_sems(count):
    dma = pltpu.SemaphoreType.DMA
    return [dma((count,))] * 6 + [dma((count, 4)), dma((count, 3)), dma((count, 3))]


def outer(left, right):
    return lax.dot_general(left, right, (((0,), (0,)), ((), ())), preferred_element_type=F32)


def inner(left, right):
    return lax.dot_general(left, right, (((1,), (1,)), ((), ())), preferred_element_type=F32)


def dense(left, right):
    return jnp.dot(left, right, preferred_element_type=F32)


def reduce_kernel(jobs, *refs):
    n_in = 2 * len(jobs) + 2
    ins, outs, rest = refs[:n_in], refs[n_in:n_in + 2], refs[n_in + 2:]
    count = sum(n for _, n in jobs)
    m_bufs, m_sems, v_bufs, v_sems = rest[:8], rest[8:17], rest[17:25], rest[25:34]
    rt = Route()
    main, small = Reducer(rt, m_bufs, m_sems), Reducer(rt, v_bufs, v_sems)
    own, sib = m_bufs[0], m_bufs[1]
    halves = ((sib, 1 - rt.core), (own, rt.core))

    def tall(left, right, first):
        def one(i, _):
            for buf, core in halves:
                j = (i // 8) * 16 + core * 8 + i % 8
                part = left[:, pl.ds(pl.multiple_of(j * 128, 128), 128)]
                grad = outer(part, right[...]).astype(BF16)
                for q in range(4):
                    buf[first + q, i] = grad[q * ROWS:(q + 1) * ROWS]
            return 0

        lax.fori_loop(0, 16, one, 0)

    def square(left, right, c):
        for buf, core in halves:
            for xx in range(2):
                part = left[:, pl.ds(pl.multiple_of((xx * 2 + core) * 256, 256), 256)]
                buf[c, xx * 8:xx * 8 + 8] = outer(part, right).astype(BF16).reshape(8, ROWS, 1024)

    def compute(c):
        first = 0
        for i, (kind, n) in enumerate(jobs):
            left, right = ins[2 * i], ins[2 * i + 1]
            if kind == "tall":

                @when(c == first)
                def _():
                    tall(left, right, first)

            else:

                @when((c >= first) & (c < first + n))
                def _():
                    square(left, right[:, pl.ds(pl.multiple_of((c - first) * 1024, 1024), 1024)], c)

            first += n

    def compute_small():
        rows8, up8 = ins[-2], ins[-1]

        def one(i, _):
            for buf, core in ((v_bufs[1], 1 - rt.core), (v_bufs[0], rt.core)):
                j = (i // 8) * 16 + core * 8 + i % 8
                buf[0, i, 0:8] = rows8[:, pl.ds(pl.multiple_of((j // 4) * 128, 128), 128)]
                buf[0, i, 8:16] = up8[:, pl.ds(pl.multiple_of(j * 128, 128), 128)]
            return 0

        lax.fori_loop(0, 16, one, 0)

    rt.greet()

    def step(t, _):
        for s in range(Reducer.stages):
            c = t - s

            @when((c >= 0) & (c < count))
            def _():
                if s == 0:
                    compute(c)
                main.stage(s, c)

            @when(c == count)
            def _():
                if s == 0:
                    compute_small()
                small.stage(s, 0)

        return 0

    lax.fori_loop(0, count + Reducer.stages, step, 0)

    def last(c, _):
        main.finish(c)
        return 0

    lax.fori_loop(0, count, last, 0)
    small.finish(0)
    outs[0][...] = m_bufs[7][...]
    mine = v_bufs[7][0]
    quarter = owner(rt.x, rt.y, rt.z, rt.core) % 4
    picked = jnp.zeros((16, 32), F32)
    for q in range(4):
        picked = jnp.where(quarter == q, mine[:, q * 32:(q + 1) * 32], picked)
    outs[1][:, 0:128] = mine
    outs[1][:, 128:160] = picked


def reduce_gradients(jobs, ins, rows8, up8):
    count = sum(n for _, n in jobs)
    vmem = pl.BlockSpec(memory_space=pltpu.VMEM)
    return pl.pallas_call(
        functools.partial(reduce_kernel, jobs),
        out_shape=(jax.ShapeDtypeStruct((count, ROWS, 1024), F32), jax.ShapeDtypeStruct((16, 256), F32)),
        in_specs=[vmem] * (len(ins) + 2),
        out_specs=(vmem, vmem),
        scratch_shapes=reducer_bufs(count, (ROWS, 1024), BF16) + reducer_sems(count)
        + reducer_bufs(1, (16, 128), F32) + reducer_sems(1),
        compiler_params=pltpu.CompilerParams(collective_id=1, has_side_effects=True, vmem_limit_bytes=VMEM_LIMIT),
    )(*ins, rows8, up8)


def head_mask(shape, head):
    lane = lax.broadcasted_iota(jnp.int32, shape, len(shape) - 1)
    return (lane // HEAD_DIM) == head


def only_head(values, head):
    return jnp.where(head_mask(values.shape, head), values, jnp.zeros_like(values))


def key_sequences(len_ref, shift, keys):
    pos = lax.broadcasted_iota(jnp.int32, (keys, 128), 0)
    seq = lax.shift_right_logical(pos, shift)
    at = pos - lax.shift_left(seq, shift)
    limit = jnp.zeros((keys, 128), jnp.int32)
    for s in range(8):
        limit = jnp.where(seq == s, len_ref[s], limit)
    return jnp.where(at < limit, seq, -1)


def key_bias(kseq, shift, start, width):
    keys = kseq.shape[0]
    qseq = lax.shift_right_logical(start + lax.broadcasted_iota(jnp.int32, (1, 128), 1), shift)
    parts = []
    for w in range(width // 128):
        qs = lax.shift_right_logical(start + w * 128 + lax.broadcasted_iota(jnp.int32, (1, 128), 1), shift)
        parts.append(jnp.where(kseq == qs, 0.0, NEG_FILL))
    return jnp.concatenate(parts, axis=1)


class Swap:
    def __init__(self):
        self.bucket, self.me = lax.axis_index("bucket"), lax.axis_index("ctx")

    def greet(self):
        barrier = pltpu.get_barrier_semaphore()
        for off in range(1, 8):
            target = (self.bucket, (self.me + off) % 8)
            pl.semaphore_signal(barrier, inc=1, device_id=target, device_id_type=MESH_ID)
        pl.semaphore_wait(barrier, 7)

    def heads_out(self, tokens, heads, send_sem, recv_sem, local_sem):
        rows = pl.ds(pl.multiple_of(self.me * 128, 128), 128)
        for off in (4, 3, 5, 2, 6, 1, 7):
            d = (self.me + off) % 8
            remote(tokens.at[:, pl.ds(pl.multiple_of(d * 128, 128), 128)], heads.at[rows], send_sem, recv_sem, (self.bucket, d)).start()
        pltpu.make_async_copy(tokens.at[:, pl.ds(pl.multiple_of(self.me * 128, 128), 128)], heads.at[rows], local_sem).start()

    def heads_back(self, heads, tokens, send_sem, recv_sem, local_sem):
        cols = pl.ds(pl.multiple_of(self.me * 128, 128), 128)
        for off in (4, 3, 5, 2, 6, 1, 7):
            d = (self.me + off) % 8
            remote(heads.at[pl.ds(pl.multiple_of(d * 128, 128), 128)], tokens.at[:, cols], send_sem, recv_sem, (self.bucket, d)).start()
        pltpu.make_async_copy(heads.at[pl.ds(pl.multiple_of(self.me * 128, 128), 128)], tokens.at[:, cols], local_sem).start()

    def wait(self, heads, send_sem, recv_sem, local_sem):
        seven = heads.at[pl.ds(0, 7 * 128)]
        bytes_of(seven, recv_sem).wait()
        bytes_of(seven, send_sem).wait()
        bytes_of(heads.at[pl.ds(0, 128)], local_sem).wait()


Q_BLOCK = 256


def attend_block(i, shift, kseq, q, k, v, o_ref, lse_ref):
    start = i * Q_BLOCK
    rows = pl.ds(pl.multiple_of(start, Q_BLOCK), Q_BLOCK)
    bias = key_bias(kseq[...], shift, start, Q_BLOCK)
    scaled = q[rows] * jnp.asarray(HEAD_DIM ** (-0.5), BF16)
    result = []
    for h in range(2):
        s = inner(k[...], only_head(scaled, h)) + bias
        m = jnp.max(s, axis=0, keepdims=True)
        e = jnp.exp(s - m)
        total = jnp.sum(e, axis=0, keepdims=True)
        w = (e * (1.0 / total)).astype(BF16)
        lse_ref[h:h + 1, rows] = m + jnp.log(total)
        o = outer(v[...], w)
        result.append(o[h * HEAD_DIM:(h + 1) * HEAD_DIM])
    o_ref[rows] = jnp.concatenate(result, axis=0).T.astype(BF16)


def attend_kernel(x_ref, w_ref, t_ref, len_ref, att_ref, qh, kh, vh, lse, qkv, oh, kseq, wbuf, wsem, sems):
    swap = Swap()
    shift = 7 + swap.bucket
    copies = [pltpu.make_async_copy(w_ref.at[pl.ds(i * 1024, 1024)], wbuf.at[i], wsem.at[i]) for i in range(3)]
    for c in copies:
        c.start()
    swap.greet()
    x = x_ref[...]
    table = table_of(t_ref)
    for i, (dst, row) in enumerate(((qh, 0), (kh, None), (vh, 1))):
        copies[i].wait()
        val = dense(x, wbuf[i])
        if row is not None:
            val = val + table[row:row + 1]
        qkv[i] = val.astype(BF16)
        swap.heads_out(qkv.at[i], dst, sems.at[3 * i], sems.at[3 * i + 1], sems.at[3 * i + 2])
    kseq[...] = key_sequences(len_ref, shift, kseq.shape[0])
    for i, dst in enumerate((qh, kh, vh)):
        swap.wait(dst, sems.at[3 * i], sems.at[3 * i + 1], sems.at[3 * i + 2])

    def block(i, _):
        attend_block(i, shift, kseq, qh, kh, vh, oh, lse)
        return 0

    lax.fori_loop(0, qh.shape[0] // Q_BLOCK, block, 0)
    swap.heads_back(oh, att_ref, sems.at[9], sems.at[10], sems.at[11])
    swap.wait(oh, sems.at[9], sems.at[10], sems.at[11])


def table_of(t_ref):
    groups = []
    for g in range(8):
        groups.append(sum(t_ref[4 * g + i].astype(F32) for i in range(4)))
    return jnp.concatenate(groups, axis=1)


def attend(tokens, weights, table, lens):
    vmem, anywhere = pl.BlockSpec(memory_space=pltpu.VMEM), pl.BlockSpec(memory_space=pl.ANY)
    hs = jax.ShapeDtypeStruct((1024, 128), BF16)
    return pl.pallas_call(
        attend_kernel,
        out_shape=(jax.ShapeDtypeStruct((128, 1024), BF16), hs, hs, hs, jax.ShapeDtypeStruct((2, 1024), F32)),
        in_specs=[vmem, anywhere, vmem, pl.BlockSpec(memory_space=pltpu.SMEM)],
        out_specs=(vmem,) * 5,
        scratch_shapes=[
            pltpu.VMEM((3, 128, 1024), BF16), pltpu.VMEM((1024, 128), BF16), pltpu.VMEM((1024, 128), jnp.int32),
            pltpu.VMEM((3, 1024, 1024), BF16), pltpu.SemaphoreType.DMA((3,)), pltpu.SemaphoreType.DMA((12,)),
        ],
        compiler_params=pltpu.CompilerParams(collective_id=2, has_side_effects=True, vmem_limit_bytes=VMEM_LIMIT),
    )(tokens, weights, table, lens)


def attend_back_block(i, shift, kseq, q, k, v, do, lse, dq, dk, dv):
    start = i * Q_BLOCK
    rows = pl.ds(pl.multiple_of(start, Q_BLOCK), Q_BLOCK)
    bias = key_bias(kseq[...], shift, start, Q_BLOCK)
    scaled = q[rows] * jnp.asarray(HEAD_DIM ** (-0.5), BF16)
    back = do[rows]
    result = []
    for h in range(2):
        qm, dm = only_head(scaled, h), only_head(back, h)
        p = jnp.exp(inner(k[...], qm) + bias - lse[h:h + 1, rows])
        slope = inner(v[...], dm)
        product = p * slope
        delta = jnp.sum(product, axis=0, keepdims=True)
        ds = (product - p * delta).astype(BF16)
        dv[...] += dense(p.astype(BF16), dm)
        dk[...] += dense(ds, qm)
        g = outer(k[...], ds) * (HEAD_DIM ** (-0.5))
        result.append(g[h * HEAD_DIM:(h + 1) * HEAD_DIM])
    dq[rows] = jnp.concatenate(result, axis=0).T.astype(BF16)


def attend_back_kernel(g_ref, qh, kh, vh, lse, len_ref, dq_t, dk_t, dv_t, doh, dqh, dk, dv, dkh, dvh, kseq, sems):
    swap = Swap()
    shift = 7 + swap.bucket
    swap.greet()
    swap.heads_out(g_ref, doh, sems.at[0], sems.at[1], sems.at[2])
    kseq[...] = key_sequences(len_ref, shift, kseq.shape[0])
    dk[...] = jnp.zeros_like(dk)
    dv[...] = jnp.zeros_like(dv)
    swap.wait(doh, sems.at[0], sems.at[1], sems.at[2])

    def block(i, _):
        attend_back_block(i, shift, kseq, qh, kh, vh, doh, lse, dqh, dk, dv)
        return 0

    lax.fori_loop(0, qh.shape[0] // Q_BLOCK, block, 0)
    dkh[...] = dk[...].astype(BF16)
    dvh[...] = dv[...].astype(BF16)
    trio = ((dqh, dq_t), (dkh, dk_t), (dvh, dv_t))
    for i, (src, dst) in enumerate(trio):
        swap.heads_back(src, dst, sems.at[3 * i + 3], sems.at[3 * i + 4], sems.at[3 * i + 5])
    for i, (src, dst) in enumerate(trio):
        swap.wait(src, sems.at[3 * i + 3], sems.at[3 * i + 4], sems.at[3 * i + 5])


def attend_back(grad_att, qh, kh, vh, lse, lens):
    vmem = pl.BlockSpec(memory_space=pltpu.VMEM)
    ts = jax.ShapeDtypeStruct((128, 1024), BF16)
    half, full = pltpu.VMEM((1024, 128), BF16), pltpu.VMEM((1024, 128), F32)
    return pl.pallas_call(
        attend_back_kernel,
        out_shape=(ts, ts, ts),
        in_specs=[vmem] * 5 + [pl.BlockSpec(memory_space=pltpu.SMEM)],
        out_specs=(vmem,) * 3,
        scratch_shapes=[half, half, full, full, half, half, pltpu.VMEM((1024, 128), jnp.int32), pltpu.SemaphoreType.DMA((12,))],
        compiler_params=pltpu.CompilerParams(collective_id=3, has_side_effects=True, vmem_limit_bytes=VMEM_LIMIT),
    )(grad_att, qh, kh, vh, lse, lens)


def gelu_value(values):
    return 0.5 * values * (1.0 + lax.erf(values * 0.7071067811865476))


def gelu_slope(values):
    return 0.5 * (1.0 + lax.erf(values * 0.7071067811865476)) + values * jnp.exp(-0.5 * values * values) * 0.3989422804014327


def row_mean(values):
    return jnp.mean(values, axis=-1, keepdims=True)


def column_sum(values):
    return jnp.sum(values, axis=0, keepdims=True)


def norm_parts(summed):
    centred = summed - row_mean(summed)
    inv_std = lax.rsqrt(row_mean(centred * centred) + EPSILON)
    return centred * inv_std, inv_std


def norm_back(incoming, normed, inv_std, gain):
    scaled = incoming * gain
    return inv_std * (scaled - row_mean(scaled) - normed * row_mean(scaled * normed))


V_QUERY, V_VALUE, V_OUT, V_GAIN1, V_SHIFT1, V_DOWN, V_GAIN2, V_SHIFT2 = range(8)


def middle_kernel(x_ref, att_ref, w_ref, t_ref, cot_ref,
                  hid_ref, act_ref, gffn_ref, mid_ref, gpre_ref, gbr_ref, gone_ref, gatt_ref, rows_ref, up_ref,
                  wbuf, pre, wsem):
    order = [3, 4, 8, 5, 9, 6, 10, 7, 11]
    copies = {i: pltpu.make_async_copy(w_ref.at[pl.ds(i * 1024, 1024)], wbuf.at[i - 3], wsem.at[i - 3]) for i in order}
    for i in order:
        copies[i].start()
    table = table_of(t_ref)

    def vec(row):
        return table[row:row + 1]

    x = x_ref[...].astype(F32)
    copies[3].wait()
    normed1, inv1 = norm_parts(x + (dense(att_ref[...], wbuf[0]) + vec(V_OUT)))
    middle = normed1 * vec(V_GAIN1) + vec(V_SHIFT1)
    mid_ref[...] = middle.astype(BF16)
    ffn = jnp.zeros(x.shape, F32)
    for i in range(4):
        copies[4 + i].wait()
        b_up = jnp.concatenate([t_ref[8 * i + j][8:9].astype(F32) for j in range(8)], axis=1)
        value = dense(mid_ref[...], wbuf[1 + i]) + b_up
        pre[i] = value
        act = gelu_value(value).astype(BF16)
        act_ref[:, i * 1024:(i + 1) * 1024] = act
        copies[8 + i].wait()
        ffn = ffn + dense(act, wbuf[5 + i])
    normed2, inv2 = norm_parts(middle + (ffn + vec(V_DOWN)))
    hid_ref[...] = (normed2 * vec(V_GAIN2) + vec(V_SHIFT2)).astype(BF16)
    g = cot_ref[...].astype(F32)
    rows_ref[...] = jnp.zeros_like(rows_ref)
    rows_ref[V_GAIN2:V_GAIN2 + 1] = column_sum(g * normed2)
    rows_ref[V_SHIFT2:V_SHIFT2 + 1] = column_sum(g)
    gtwo = norm_back(g, normed2, inv2, vec(V_GAIN2))
    gffn = gtwo.astype(BF16)
    gffn_ref[...] = gffn
    rows_ref[V_DOWN:V_DOWN + 1] = column_sum(gffn.astype(F32))
    back = jnp.zeros(x.shape, F32)
    up_ref[...] = jnp.zeros_like(up_ref)
    for i in range(4):
        gact = inner(gffn_ref[...], wbuf[5 + i]).astype(BF16).astype(F32)
        gpre = (gact * gelu_slope(pre[i])).astype(BF16)
        gpre_ref[:, i * 1024:(i + 1) * 1024] = gpre
        up_ref[0:1, i * 1024:(i + 1) * 1024] = column_sum(gpre.astype(F32))
        back = back + inner(gpre, wbuf[1 + i])
    gmid = gtwo + back.astype(BF16).astype(F32)
    rows_ref[V_GAIN1:V_GAIN1 + 1] = column_sum(gmid * normed1)
    rows_ref[V_SHIFT1:V_SHIFT1 + 1] = column_sum(gmid)
    gone = norm_back(gmid, normed1, inv1, vec(V_GAIN1))
    gone_ref[...] = gone
    gbr = gone.astype(BF16)
    gbr_ref[...] = gbr
    rows_ref[V_OUT:V_OUT + 1] = column_sum(gbr.astype(F32))
    gatt_ref[...] = inner(gbr, wbuf[0]).astype(BF16)


def middle_layer(tokens, attended, weights, table, cotangent):
    vmem, anywhere = pl.BlockSpec(memory_space=pltpu.VMEM), pl.BlockSpec(memory_space=pl.ANY)

    def s(shape, dtype):
        return jax.ShapeDtypeStruct(shape, dtype)

    narrow, wide = (128, 1024), (128, 4096)
    return pl.pallas_call(
        middle_kernel,
        out_shape=(
            s(narrow, BF16), s(wide, BF16), s(narrow, BF16), s(narrow, BF16), s(wide, BF16),
            s(narrow, BF16), s(narrow, F32), s(narrow, BF16), s((8, 1024), F32), s((8, 4096), F32),
        ),
        in_specs=[vmem, vmem, anywhere, vmem, vmem],
        out_specs=(vmem,) * 10,
        scratch_shapes=[pltpu.VMEM((9, 1024, 1024), BF16), pltpu.VMEM((4, 128, 1024), F32), pltpu.SemaphoreType.DMA((9,))],
        compiler_params=pltpu.CompilerParams(vmem_limit_bytes=VMEM_LIMIT),
    )(tokens, attended, weights, table, cotangent)


def fast_body(hidden_in, lengths, w_query, w_key, w_value, b_query, b_value, w_out, b_out, first_gain, first_shift,
              w_up, b_up, w_down, b_down, second_gain, second_shift, cotangent):
    tokens = hidden_in.reshape(128, 1024)
    shards = jnp.concatenate(
        [w_query, w_key, w_value, w_out] + [w_up[:, i * 1024:(i + 1) * 1024] for i in range(4)] + [w_down], axis=0
    )
    me = lax.axis_index("bucket") * 8 + lax.axis_index("ctx")
    rows = jnp.stack([b_query, b_value, b_out, first_gain, first_shift, b_down, second_gain, second_shift])
    spread = jnp.concatenate([jnp.where(me % 4 == q, rows, jnp.zeros_like(rows)) for q in range(4)], axis=1)
    small = jnp.concatenate([spread, b_up[None], jnp.zeros((7, 128), BF16)], axis=0)
    weights, table = gather_weights(shards, small)
    lens = lengths.reshape(8)
    attended, qh, kh, vh, lse = attend(tokens, weights, table, lens)
    (hidden_out, act, gffn, mid, gpre, gbr, gone, gatt, rows8, up8) = middle_layer(
        tokens, attended, weights, table, cotangent.reshape(128, 1024)
    )
    dq, dk, dv = attend_back(gatt, qh, kh, vh, lse, lens)
    grad_in = gone + inner(dq, weights[0:1024]) + inner(dk, weights[1024:2048]) + inner(dv, weights[2048:3072])
    more = jnp.stack([jnp.sum(dq.astype(F32), axis=0), jnp.sum(dv.astype(F32), axis=0)])
    rows8 = jnp.concatenate([more, rows8[2:]], axis=0)
    jobs = (("tall", 4), ("square", 4), ("square", 1), ("square", 1), ("square", 1), ("square", 1))
    sums, small_sums = reduce_gradients(
        jobs, (act, gffn, mid, gpre, attended, gbr, tokens, dq, tokens, dk, tokens, dv), rows8, up8
    )
    g_down = sums[:4].reshape(128, 1024)
    g_up = jnp.concatenate([sums[4 + i] for i in range(4)], axis=1)
    row = lambda r: small_sums[r, 128:160]
    return (
        hidden_out.reshape(hidden_in.shape), grad_in.reshape(hidden_in.shape), sums[9], sums[10], sums[11],
        row(0), row(1), sums[8], row(2), row(3), row(4), g_up, small_sums[8, 0:128], g_down, row(5), row(6), row(7),
    )


def matmul(left, right):
    return jnp.dot(left, right, preferred_element_type=jnp.float32)


def row_inner(left, right):
    return lax.dot_general(
        left, right, (((0,), (0,)), ((), ())), preferred_element_type=jnp.float32
    )


def right_inner(left, right):
    return lax.dot_general(
        left, right, (((1,), (1,)), ((), ())), preferred_element_type=jnp.float32
    )


def rounded(values):
    return values.astype(jnp.bfloat16)


def widened(values):
    return values.astype(jnp.float32)


def norm_forward(summed, gain_vec, shift_vec):
    average = jnp.mean(summed, axis=-1, keepdims=True)
    centred = summed - average
    variance = jnp.mean(centred * centred, axis=-1, keepdims=True)
    inv_std = lax.rsqrt(variance + EPSILON)
    normed = centred * inv_std
    return (normed * gain_vec + shift_vec, normed, inv_std)


def norm_backward(incoming, normed, inv_std, gain_vec):
    scaled = incoming * gain_vec
    inner = (
        scaled
        - jnp.mean(scaled, axis=-1, keepdims=True)
        - normed * jnp.mean(scaled * normed, axis=-1, keepdims=True)
    )
    return (inv_std * inner, jnp.sum(incoming * normed, axis=0), jnp.sum(incoming, axis=0))


def plain_gelu_value(values):
    return 0.5 * values * (1.0 + jax.scipy.special.erf(values * 0.7071067811865476))


def plain_gelu_slope(values):
    return (
        0.5 * (1.0 + jax.scipy.special.erf(values * 0.7071067811865476))
        + values * jnp.exp(-0.5 * values * values) * 0.3989422804014327
    )


def split_heads(values):
    return values.reshape(values.shape[0], values.shape[1], values.shape[2] // HEAD_DIM, HEAD_DIM)


def seq_mask(seq_info, query_pos, key_pos):
    seq_lens, slot_len = seq_info
    query_seq = query_pos // slot_len
    key_seq = key_pos // slot_len
    seq_ids = jnp.arange(seq_lens.shape[1], dtype=jnp.int32)
    picked = (key_seq[:, None] == seq_ids[None, :]).astype(jnp.int32)
    key_limit = jnp.sum(picked[None, :, :] * seq_lens[:, None, :], axis=-1)
    key_valid = (key_pos - key_seq * slot_len)[None, :] < key_limit
    same_seq = query_seq[:, None] == key_seq[None, :]
    return (same_seq[None, :, :] & key_valid[:, None, :])[:, None, :, :]


def score_block(query4, key4, query_start, key_start, seq_info):
    raw = jnp.einsum(
        "sqhd,skhd->shqk", query4, key4, preferred_element_type=jnp.float32
    ) * HEAD_DIM ** (-0.5)
    query_pos = query_start + jnp.arange(query4.shape[1], dtype=jnp.int32)
    key_pos = key_start + jnp.arange(key4.shape[1], dtype=jnp.int32)
    allowed = seq_mask(seq_info, query_pos, key_pos)
    return (jnp.where(allowed, raw, NEG_FILL), allowed)


def over_blocks(block_step, running, pieces):
    length_here = pieces[0].shape[1]
    block_len = math.gcd(length_here, 512)
    turn_count = length_here // block_len

    def advance(turn_no, current):
        offset = turn_no * block_len
        sliced = tuple(
            (lax.dynamic_slice_in_dim(piece_arr, offset, block_len, 1) for piece_arr in pieces)
        )
        return block_step(current, sliced, offset)

    return lax.fori_loop(0, turn_count, advance, running)


def general_body(
    hidden_in,
    lengths,
    w_query,
    w_key,
    w_value,
    b_query,
    b_value,
    w_out,
    b_out,
    first_gain,
    first_shift,
    w_up,
    b_up,
    w_down,
    b_down,
    second_gain,
    second_shift,
    cotangent,
):
    shards = (
        w_query,
        w_key,
        w_value,
        b_query,
        b_value,
        w_out,
        b_out,
        first_gain,
        first_shift,
        w_up,
        b_up,
        w_down,
        b_down,
        second_gain,
        second_shift,
    )
    gathered = (
        lax.all_gather(shards[0], ("bucket", "ctx"), axis=0, tiled=True),
        lax.all_gather(shards[1], ("bucket", "ctx"), axis=0, tiled=True),
        lax.all_gather(shards[2], ("bucket", "ctx"), axis=0, tiled=True),
        lax.all_gather(shards[3], ("bucket", "ctx"), axis=0, tiled=True),
        lax.all_gather(shards[4], ("bucket", "ctx"), axis=0, tiled=True),
        lax.all_gather(shards[5], ("bucket", "ctx"), axis=0, tiled=True),
        lax.all_gather(shards[6], ("bucket", "ctx"), axis=0, tiled=True),
        lax.all_gather(shards[7], ("bucket", "ctx"), axis=0, tiled=True),
        lax.all_gather(shards[8], ("bucket", "ctx"), axis=0, tiled=True),
        lax.all_gather(shards[9], ("bucket", "ctx"), axis=0, tiled=True),
        lax.all_gather(shards[10], ("bucket", "ctx"), axis=0, tiled=True),
        lax.all_gather(shards[11], ("bucket", "ctx"), axis=0, tiled=True),
        lax.all_gather(shards[12], ("bucket", "ctx"), axis=0, tiled=True),
        lax.all_gather(shards[13], ("bucket", "ctx"), axis=0, tiled=True),
        lax.all_gather(shards[14], ("bucket", "ctx"), axis=0, tiled=True),
    )
    (
        query_mat,
        key_mat,
        value_mat,
        query_bias,
        value_bias,
        out_mat,
        out_bias,
        gain_one,
        shift_one,
        up_mat,
        up_bias,
        down_mat,
        down_bias,
        gain_two,
        shift_two,
    ) = gathered
    seq_count = hidden_in.shape[1]
    local_rows = hidden_in.shape[2]
    model_width = hidden_in.shape[3]
    head_count = model_width // HEAD_DIM
    total_rows = seq_count * local_rows
    block_shape = (seq_count, local_rows, model_width)
    score_scale = HEAD_DIM ** (-0.5)
    seq_total = local_rows * lax.axis_size("ctx")
    group_index = lax.axis_index("bucket")
    seq_slots = jnp.right_shift(jnp.int32(lengths.shape[2]), group_index)
    slot_len = jnp.int32(seq_total) // seq_slots
    seq_info = (lengths[0], slot_len)
    own_start = lax.axis_index("ctx") * local_rows
    tokens = hidden_in.reshape(total_rows, model_width)
    query_low = rounded(matmul(tokens, query_mat) + widened(query_bias))
    key_low = rounded(matmul(tokens, key_mat))
    value_low = rounded(matmul(tokens, value_mat) + widened(value_bias))
    query_heads = split_heads(query_low.reshape(block_shape))
    key_rows = key_low.reshape(block_shape)
    value_rows = value_low.reshape(block_shape)

    def stats_step(running, sliced, anchor):
        scores, allowed = score_block(
            query_heads, split_heads(sliced[0]), own_start, anchor, seq_info
        )
        run_max, run_total = running
        new_max = jnp.maximum(run_max, jnp.max(scores, axis=-1))
        raised = jnp.where(allowed, jnp.exp(scores - new_max[..., None]), 0.0)
        return (new_max, run_total * jnp.exp(run_max - new_max) + jnp.sum(raised, axis=-1))

    stat_shape = (seq_count, head_count, local_rows)
    stats_start = (jnp.full(stat_shape, NEG_FILL, jnp.float32), jnp.zeros(stat_shape, jnp.float32))
    run_max, run_total = over_blocks(
        stats_step, stats_start, (lax.all_gather(key_rows, "ctx", axis=1, tiled=True),)
    )
    log_total = run_max + jnp.log(run_total)

    def output_step(running, sliced, anchor):
        key4 = split_heads(sliced[0])
        value4 = split_heads(sliced[1])
        scores, allowed = score_block(query_heads, key4, own_start, anchor, seq_info)
        probs_low = rounded(jnp.where(allowed, jnp.exp(scores - log_total[..., None]), 0.0))
        return running + jnp.einsum(
            "shqk,skhd->sqhd", probs_low, value4, preferred_element_type=jnp.float32
        )

    attended_f32 = over_blocks(
        output_step,
        jnp.zeros(query_heads.shape, jnp.float32),
        (
            lax.all_gather(key_rows, "ctx", axis=1, tiled=True),
            lax.all_gather(value_rows, "ctx", axis=1, tiled=True),
        ),
    )
    attended_low = rounded(attended_f32.reshape(total_rows, model_width))
    branch = matmul(attended_low, out_mat) + widened(out_bias)
    middle, normed_one, inv_one = norm_forward(
        widened(tokens) + branch, widened(gain_one), widened(shift_one)
    )
    middle_low = rounded(middle)
    pre_act = matmul(middle_low, up_mat) + widened(up_bias)
    activated = rounded(plain_gelu_value(pre_act))
    ffn_out = matmul(activated, down_mat) + widened(down_bias)
    result, normed_two, inv_two = norm_forward(
        middle + ffn_out, widened(gain_two), widened(shift_two)
    )
    hidden_out = rounded(result).reshape(hidden_in.shape)
    gathered = (
        lax.all_gather(shards[0], ("bucket", "ctx"), axis=0, tiled=True),
        lax.all_gather(shards[1], ("bucket", "ctx"), axis=0, tiled=True),
        lax.all_gather(shards[2], ("bucket", "ctx"), axis=0, tiled=True),
        lax.all_gather(shards[3], ("bucket", "ctx"), axis=0, tiled=True),
        lax.all_gather(shards[4], ("bucket", "ctx"), axis=0, tiled=True),
        lax.all_gather(shards[5], ("bucket", "ctx"), axis=0, tiled=True),
        lax.all_gather(shards[6], ("bucket", "ctx"), axis=0, tiled=True),
        lax.all_gather(shards[7], ("bucket", "ctx"), axis=0, tiled=True),
        lax.all_gather(shards[8], ("bucket", "ctx"), axis=0, tiled=True),
        lax.all_gather(shards[9], ("bucket", "ctx"), axis=0, tiled=True),
        lax.all_gather(shards[10], ("bucket", "ctx"), axis=0, tiled=True),
        lax.all_gather(shards[11], ("bucket", "ctx"), axis=0, tiled=True),
        lax.all_gather(shards[12], ("bucket", "ctx"), axis=0, tiled=True),
        lax.all_gather(shards[13], ("bucket", "ctx"), axis=0, tiled=True),
        lax.all_gather(shards[14], ("bucket", "ctx"), axis=0, tiled=True),
    )
    query_mat = gathered[0]
    key_mat = gathered[1]
    value_mat = gathered[2]
    out_mat = gathered[5]
    gain_one = gathered[7]
    up_mat = gathered[9]
    down_mat = gathered[11]
    gain_two = gathered[13]
    incoming = widened(cotangent.reshape(total_rows, model_width))
    grad_two_sum, grad_second_gain, grad_second_shift = norm_backward(
        incoming, normed_two, inv_two, widened(gain_two)
    )
    grad_ffn = rounded(grad_two_sum)
    grad_b_down = jnp.sum(widened(grad_ffn), axis=0)
    grad_w_down = row_inner(activated, grad_ffn)
    grad_act = widened(rounded(right_inner(grad_ffn, down_mat)))
    grad_pre = rounded(grad_act * plain_gelu_slope(pre_act))
    grad_b_up = jnp.sum(widened(grad_pre), axis=0)
    grad_w_up = row_inner(middle_low, grad_pre)
    grad_middle = grad_two_sum + widened(rounded(right_inner(grad_pre, up_mat)))
    grad_one_sum, grad_first_gain, grad_first_shift = norm_backward(
        grad_middle, normed_one, inv_one, widened(gain_one)
    )
    grad_branch = rounded(grad_one_sum)
    grad_b_out = jnp.sum(widened(grad_branch), axis=0)
    grad_w_out = row_inner(attended_low, grad_branch)
    grad_att = rounded(right_inner(grad_branch, out_mat)).reshape(block_shape)
    grad_att_heads = split_heads(grad_att)
    delta = jnp.einsum("sqhd,sqhd->shq", widened(grad_att_heads), attended_f32)

    def grad_terms(query4, key4, value4, att4, row_log, row_delta, query_start, key_start):
        scores, allowed = score_block(query4, key4, query_start, key_start, seq_info)
        probs = jnp.where(allowed, jnp.exp(scores - row_log[..., None]), 0.0)
        slope = jnp.einsum("sqhd,skhd->shqk", att4, value4, preferred_element_type=jnp.float32)
        return (rounded(probs), rounded(probs * (slope - row_delta[..., None])))

    def query_step(running, sliced, anchor):
        key4 = split_heads(sliced[0])
        value4 = split_heads(sliced[1])
        probs_low, score_grad = grad_terms(
            query_heads, key4, value4, grad_att_heads, log_total, delta, own_start, anchor
        )
        return (
            running
            + jnp.einsum("shqk,skhd->sqhd", score_grad, key4, preferred_element_type=jnp.float32)
            * score_scale
        )

    grad_q = over_blocks(
        query_step,
        jnp.zeros(query_heads.shape, jnp.float32),
        (
            lax.all_gather(key_rows, "ctx", axis=1, tiled=True),
            lax.all_gather(value_rows, "ctx", axis=1, tiled=True),
        ),
    )
    log_all, delta_all = (
        lax.all_gather(log_total, "ctx", axis=2, tiled=True),
        lax.all_gather(delta, "ctx", axis=2, tiled=True),
    )
    own_keys = split_heads(key_rows)
    own_values = split_heads(value_rows)

    def owner_step(running, sliced, anchor):
        query4 = split_heads(sliced[0])
        att4 = split_heads(sliced[1])
        count_here = sliced[0].shape[1]
        row_log = lax.dynamic_slice_in_dim(log_all, anchor, count_here, 2)
        row_delta = lax.dynamic_slice_in_dim(delta_all, anchor, count_here, 2)
        probs_low, score_grad = grad_terms(
            query4, own_keys, own_values, att4, row_log, row_delta, anchor, own_start
        )
        grad_k, grad_v = running
        grad_k = (
            grad_k
            + jnp.einsum("shqk,sqhd->skhd", score_grad, query4, preferred_element_type=jnp.float32)
            * score_scale
        )
        grad_v = grad_v + jnp.einsum(
            "shqk,sqhd->skhd", probs_low, att4, preferred_element_type=jnp.float32
        )
        return (grad_k, grad_v)

    owner_start = (jnp.zeros(own_keys.shape, jnp.float32), jnp.zeros(own_keys.shape, jnp.float32))
    grad_k_own, grad_v_own = over_blocks(
        owner_step,
        owner_start,
        (
            lax.all_gather(query_low.reshape(block_shape), "ctx", axis=1, tiled=True),
            lax.all_gather(grad_att, "ctx", axis=1, tiled=True),
        ),
    )
    grad_q_low = rounded(grad_q.reshape(total_rows, model_width))
    grad_k_low = rounded(grad_k_own.reshape(total_rows, model_width))
    grad_v_low = rounded(grad_v_own.reshape(total_rows, model_width))
    grad_w_query = row_inner(tokens, grad_q_low)
    grad_b_query = jnp.sum(widened(grad_q_low), axis=0)
    grad_w_key = row_inner(tokens, grad_k_low)
    grad_w_value = row_inner(tokens, grad_v_low)
    grad_b_value = jnp.sum(widened(grad_v_low), axis=0)
    grad_in = (
        grad_one_sum
        + right_inner(grad_q_low, query_mat)
        + right_inner(grad_k_low, key_mat)
        + right_inner(grad_v_low, value_mat)
    )
    owned = (
        lax.psum_scatter(grad_w_query, ("bucket", "ctx"), scatter_dimension=0, tiled=True),
        lax.psum_scatter(grad_w_key, ("bucket", "ctx"), scatter_dimension=0, tiled=True),
        lax.psum_scatter(grad_w_value, ("bucket", "ctx"), scatter_dimension=0, tiled=True),
        lax.psum_scatter(grad_b_query, ("bucket", "ctx"), scatter_dimension=0, tiled=True),
        lax.psum_scatter(grad_b_value, ("bucket", "ctx"), scatter_dimension=0, tiled=True),
        lax.psum_scatter(grad_w_out, ("bucket", "ctx"), scatter_dimension=0, tiled=True),
        lax.psum_scatter(grad_b_out, ("bucket", "ctx"), scatter_dimension=0, tiled=True),
        lax.psum_scatter(grad_first_gain, ("bucket", "ctx"), scatter_dimension=0, tiled=True),
        lax.psum_scatter(grad_first_shift, ("bucket", "ctx"), scatter_dimension=0, tiled=True),
        lax.psum_scatter(grad_w_up, ("bucket", "ctx"), scatter_dimension=0, tiled=True),
        lax.psum_scatter(grad_b_up, ("bucket", "ctx"), scatter_dimension=0, tiled=True),
        lax.psum_scatter(grad_w_down, ("bucket", "ctx"), scatter_dimension=0, tiled=True),
        lax.psum_scatter(grad_b_down, ("bucket", "ctx"), scatter_dimension=0, tiled=True),
        lax.psum_scatter(grad_second_gain, ("bucket", "ctx"), scatter_dimension=0, tiled=True),
        lax.psum_scatter(grad_second_shift, ("bucket", "ctx"), scatter_dimension=0, tiled=True),
    )
    return (hidden_out, grad_in.reshape(hidden_in.shape)) + tuple(owned)


def solution(mesh):
    placed = (
        P("bucket", None, "ctx", None),
        P("bucket", None, None),
        P(("bucket", "ctx"), None),
        P(("bucket", "ctx"), None),
        P(("bucket", "ctx"), None),
        P(("bucket", "ctx")),
        P(("bucket", "ctx")),
        P(("bucket", "ctx"), None),
        P(("bucket", "ctx")),
        P(("bucket", "ctx")),
        P(("bucket", "ctx")),
        P(("bucket", "ctx"), None),
        P(("bucket", "ctx")),
        P(("bucket", "ctx"), None),
        P(("bucket", "ctx")),
        P(("bucket", "ctx")),
        P(("bucket", "ctx")),
        P("bucket", None, "ctx", None),
    )
    def body(*arguments):
        here = dict(mesh.shape) == {"bucket": 4, "ctx": 8}
        shapes = arguments[0].shape == (1, 1, 128, 1024) and arguments[11].shape == (32, 4096)
        return (fast_body if here and shapes else general_body)(*arguments)

    return jax.shard_map(
        body,
        mesh=mesh,
        in_specs=placed,
        out_specs=(
            P("bucket", None, "ctx", None),
            P("bucket", None, "ctx", None),
            P(("bucket", "ctx"), None),
            P(("bucket", "ctx"), None),
            P(("bucket", "ctx"), None),
            P(("bucket", "ctx")),
            P(("bucket", "ctx")),
            P(("bucket", "ctx"), None),
            P(("bucket", "ctx")),
            P(("bucket", "ctx")),
            P(("bucket", "ctx")),
            P(("bucket", "ctx"), None),
            P(("bucket", "ctx")),
            P(("bucket", "ctx"), None),
            P(("bucket", "ctx")),
            P(("bucket", "ctx")),
            P(("bucket", "ctx")),
        ),
        check_vma=False,
    )
```

```python
import math

import jax
import jax.numpy as jnp
from jax import lax
from jax.experimental import pallas as pl
from jax.experimental.pallas import tpu as pltpu
from jax.sharding import PartitionSpec as P

HEAD_DIM = 64
EPSILON = 1e-05
NEG_FILL = -1e30
MESH_ID = pl.DeviceIdType.MESH
F32, BF16 = jnp.float32, jnp.bfloat16
ROWS = 32
PIECES = 12
VMEM_LIMIT = 62 * 2**20


def when(condition):
    return pl.when(condition)


def place():
    bucket, ctx = lax.axis_index("bucket"), lax.axis_index("ctx")
    return bucket // 2, ctx % 2, ctx // 2, bucket % 2


def device(x, y, z, core):
    return (x * 2 + core, z * 2 + y)


def owner(x, y, z, core):
    return (x * 2 + core) * 8 + z * 2 + y


def remote(src, dst, send_sem, recv_sem, target):
    return pltpu.make_async_remote_copy(
        src_ref=src, dst_ref=dst, send_sem=send_sem, recv_sem=recv_sem,
        device_id=target, device_id_type=MESH_ID,
    )


def bytes_of(ref, sem):
    return pltpu.make_async_copy(ref, ref, sem)


class Route:
    def __init__(self):
        self.x, self.y, self.z, self.core = x, y, z, core = place()
        self.ax, self.ay = jnp.where(core == 0, 1 - x, x), jnp.where(core == 0, y, 1 - y)
        self.bx, self.by = jnp.where(core == 1, 1 - x, x), jnp.where(core == 1, y, 1 - y)
        self.a = device(self.ax, self.ay, z, core)
        self.b = device(self.bx, self.by, z, core)
        self.sibling = device(x, y, z, 1 - core)
        self.up = device(x, y, jnp.minimum(z + 1, 3), core)
        self.down = device(x, y, jnp.maximum(z - 1, 0), core)

    def greet(self):
        z = self.z
        bucket, ctx = lax.axis_index("bucket"), lax.axis_index("ctx")
        barrier = pltpu.get_barrier_semaphore()
        pack = [(bucket, (ctx + off) % 8) for off in range(1, 8)]
        for target in [self.a, self.b, self.sibling] + pack:
            pl.semaphore_signal(barrier, inc=1, device_id=target, device_id_type=MESH_ID)

        @when(z < 3)
        def _():
            pl.semaphore_signal(barrier, inc=1, device_id=self.up, device_id_type=MESH_ID)

        @when(z > 0)
        def _():
            pl.semaphore_signal(barrier, inc=1, device_id=self.down, device_id_type=MESH_ID)

        pl.semaphore_wait(barrier, 10 + (z < 3).astype(jnp.int32) + (z > 0).astype(jnp.int32))


class Gatherer:
    stages = 7

    def __init__(self, route, count, own, block, span, sems):
        self.rt, self.count, self.own, self.block, self.span = route, count, own, block, span
        (self.zs, self.zr, self.ps, self.ar, self.br, self.dr, self.ls) = sems

    def spread(self, c, src, j, jz, to_a, to_b, z_dirs):
        rt, dst = self.rt, self.block(c, j)
        if "up" in z_dirs:

            @when(rt.z < 3)
            def _():
                remote(src, dst, self.zs.at[0, c, jz], self.zr.at[c, jz], rt.up).start()

        if "down" in z_dirs:

            @when(rt.z > 0)
            def _():
                remote(src, dst, self.zs.at[1, c, jz], self.zr.at[c, jz], rt.down).start()

        if to_a:
            remote(src, dst, self.ps, self.ar.at[c, jz], rt.a).start()
        if to_b is not None:
            remote(src, dst, self.ps, self.br.at[c, to_b * 4 + jz], rt.b).start()
        remote(src, dst, self.ps, self.dr.at[c], rt.sibling).start()

    def near(self, k, action):
        for sign in (0,) if k == 0 else (-1, 1):
            zz = self.rt.z + sign * k

            @when((zz >= 0) & (zz <= 3))
            def _():
                action(zz, "up" if sign < 0 else "down")

    def own_stage(self, c):
        rt = self.rt
        j = owner(rt.x, rt.y, rt.z, rt.core)
        pltpu.make_async_copy(self.own(c), self.block(c, j), self.ls.at[c]).start()
        self.spread(c, self.own(c), j, rt.z, True, 0, ("up", "down"))

    def z_stage(self, c, k):
        rt = self.rt

        def action(zz, direction):
            j = owner(rt.x, rt.y, zz, rt.core)
            bytes_of(self.block(c, j), self.zr.at[c, zz]).wait()
            self.spread(c, self.block(c, j), j, zz, True, 0, (direction,))

        self.near(k, action)

    def a_stage(self, c, k):
        rt = self.rt

        def action(zz, _):
            j = owner(rt.ax, rt.ay, zz, rt.core)
            bytes_of(self.block(c, j), self.ar.at[c, zz]).wait()
            self.spread(c, self.block(c, j), j, zz, False, 1, ())

        self.near(k, action)

    def b_stage(self, c, k):
        rt = self.rt

        def action(zz, _):
            for which, (xx, yy) in enumerate(((rt.bx, rt.by), (1 - rt.x, 1 - rt.y))):
                j = owner(xx, yy, zz, rt.core)
                bytes_of(self.block(c, j), self.br.at[c, which * 4 + zz]).wait()
                self.spread(c, self.block(c, j), j, zz, False, None, ())

        self.near(k, action)

    def stage(self, s, c):
        if s == 0:
            self.own_stage(c)
        if 1 <= s <= 3:
            self.z_stage(c, s)
        if 2 <= s <= 5:
            self.a_stage(c, s - 2)
        if 3 <= s <= 6:
            self.b_stage(c, s - 3)

    def arrived(self, c):
        bytes_of(self.span(16), self.dr.at[c]).wait()
        bytes_of(self.span(1), self.ls.at[c]).wait()

    def finish(self):
        bytes_of(self.span(28 * self.count), self.ps).wait()

    def finish_z(self, c):
        rt = self.rt
        for zz in range(4):

            @when((rt.z < 3) & (rt.z >= zz))
            def _():
                bytes_of(self.span(1), self.zs.at[0, c, zz]).wait()

            @when((rt.z > 0) & (rt.z <= zz))
            def _():
                bytes_of(self.span(1), self.zs.at[1, c, zz]).wait()


def gather_sems(count):
    dma = pltpu.SemaphoreType.DMA
    return [dma((2, count, 4)), dma((count, 4)), dma(()), dma((count, 4)), dma((count, 8)), dma((count,)), dma((count,))]


def outer(left, right):
    return lax.dot_general(left, right, (((0,), (0,)), ((), ())), preferred_element_type=F32)


def inner(left, right):
    return lax.dot_general(left, right, (((1,), (1,)), ((), ())), preferred_element_type=F32)


def dense(left, right):
    return jnp.dot(left, right, preferred_element_type=F32)


def head_mask(shape, head):
    lane = lax.broadcasted_iota(jnp.int32, shape, len(shape) - 1)
    return (lane // HEAD_DIM) == head


def only_head(values, head):
    return jnp.where(head_mask(values.shape, head), values, jnp.zeros_like(values))


def key_sequences(len_ref, shift, keys):
    pos = lax.broadcasted_iota(jnp.int32, (keys, 128), 0)
    seq = lax.shift_right_logical(pos, shift)
    at = pos - lax.shift_left(seq, shift)
    limit = jnp.zeros((keys, 128), jnp.int32)
    for s in range(8):
        limit = jnp.where(seq == s, len_ref[s], limit)
    return jnp.where(at < limit, seq, -1)


def key_bias(kseq, shift, start, width):
    keys = kseq.shape[0]
    qseq = lax.shift_right_logical(start + lax.broadcasted_iota(jnp.int32, (1, 128), 1), shift)
    parts = []
    for w in range(width // 128):
        qs = lax.shift_right_logical(start + w * 128 + lax.broadcasted_iota(jnp.int32, (1, 128), 1), shift)
        parts.append(jnp.where(kseq == qs, 0.0, NEG_FILL))
    return jnp.concatenate(parts, axis=1)


class Swap:
    def __init__(self):
        self.bucket, self.me = lax.axis_index("bucket"), lax.axis_index("ctx")

    def heads_out(self, tokens, heads, send_sem, recv_sem, local_sem):
        rows = pl.ds(pl.multiple_of(self.me * 128, 128), 128)
        for off in (4, 3, 5, 2, 6, 1, 7):
            d = (self.me + off) % 8
            remote(tokens.at[:, pl.ds(pl.multiple_of(d * 128, 128), 128)], heads.at[rows], send_sem, recv_sem, (self.bucket, d)).start()
        pltpu.make_async_copy(tokens.at[:, pl.ds(pl.multiple_of(self.me * 128, 128), 128)], heads.at[rows], local_sem).start()

    def heads_back(self, heads, tokens, send_sem, recv_sem, local_sem):
        cols = pl.ds(pl.multiple_of(self.me * 128, 128), 128)
        for off in (4, 3, 5, 2, 6, 1, 7):
            d = (self.me + off) % 8
            remote(heads.at[pl.ds(pl.multiple_of(d * 128, 128), 128)], tokens.at[:, cols], send_sem, recv_sem, (self.bucket, d)).start()
        pltpu.make_async_copy(heads.at[pl.ds(pl.multiple_of(self.me * 128, 128), 128)], tokens.at[:, cols], local_sem).start()

    def wait(self, heads, send_sem, recv_sem, local_sem):
        seven = heads.at[pl.ds(0, 7 * 128)]
        bytes_of(seven, recv_sem).wait()
        bytes_of(seven, send_sem).wait()
        bytes_of(heads.at[pl.ds(0, 128)], local_sem).wait()


Q_BLOCK = 256


def attend_block(i, shift, kseq, q, k, v, o_ref, lse_ref):
    start = i * Q_BLOCK
    rows = pl.ds(pl.multiple_of(start, Q_BLOCK), Q_BLOCK)
    bias = key_bias(kseq[...], shift, start, Q_BLOCK)
    scaled = q[rows] * jnp.asarray(HEAD_DIM ** (-0.5), BF16)
    result = []
    for h in range(2):
        s = inner(k[...], only_head(scaled, h)) + bias
        m = jnp.max(s, axis=0, keepdims=True)
        e = jnp.exp(s - m)
        total = jnp.sum(e, axis=0, keepdims=True)
        w = (e * (1.0 / total)).astype(BF16)
        lse_ref[h:h + 1, rows] = m + jnp.log(total)
        o = outer(v[...], w)
        result.append(o[h * HEAD_DIM:(h + 1) * HEAD_DIM])
    o_ref[rows] = jnp.concatenate(result, axis=0).T.astype(BF16)


def attend_back_block(i, shift, kseq, q, k, v, do, lse, dq, dk, dv):
    start = i * Q_BLOCK
    rows = pl.ds(pl.multiple_of(start, Q_BLOCK), Q_BLOCK)
    bias = key_bias(kseq[...], shift, start, Q_BLOCK)
    scaled = q[rows] * jnp.asarray(HEAD_DIM ** (-0.5), BF16)
    back = do[rows]
    result = []
    for h in range(2):
        qm, dm = only_head(scaled, h), only_head(back, h)
        p = jnp.exp(inner(k[...], qm) + bias - lse[h:h + 1, rows])
        slope = inner(v[...], dm)
        product = p * slope
        delta = jnp.sum(product, axis=0, keepdims=True)
        ds = (product - p * delta).astype(BF16)
        dv[...] += dense(p.astype(BF16), dm)
        dk[...] += dense(ds, qm)
        g = outer(k[...], ds) * (HEAD_DIM ** (-0.5))
        result.append(g[h * HEAD_DIM:(h + 1) * HEAD_DIM])
    dq[rows] = jnp.concatenate(result, axis=0).T.astype(BF16)


def table_of(t_ref):
    groups = []
    for g in range(8):
        groups.append(sum(t_ref[4 * g + i].astype(F32) for i in range(4)))
    return jnp.concatenate(groups, axis=1)


def gelu_value(values):
    return 0.5 * values * (1.0 + lax.erf(values * 0.7071067811865476))


def gelu_slope(values):
    return 0.5 * (1.0 + lax.erf(values * 0.7071067811865476)) + values * jnp.exp(-0.5 * values * values) * 0.3989422804014327


def row_mean(values):
    return jnp.mean(values, axis=-1, keepdims=True)


def column_sum(values):
    return jnp.sum(values, axis=0, keepdims=True)


def norm_parts(summed):
    centred = summed - row_mean(summed)
    inv_std = lax.rsqrt(row_mean(centred * centred) + EPSILON)
    return centred * inv_std, inv_std


def norm_back(incoming, normed, inv_std, gain):
    scaled = incoming * gain
    return inv_std * (scaled - row_mean(scaled) - normed * row_mean(scaled * normed))


V_QUERY, V_VALUE, V_OUT, V_GAIN1, V_SHIFT1, V_DOWN, V_GAIN2, V_SHIFT2 = range(8)
V_UP = 8
W_DOWN, W_UP = 4096, 8192


def piece_row(c, j):
    tall = (c >= 4) & (c < 8)
    return pl.multiple_of(jnp.where(tall, W_DOWN + 128 * j + ROWS * (c - 4), c * 1024 + ROWS * j), ROWS)


def forward_kernel(x_ref, cot_ref, v_ref, len_ref, wq, wk, wv, wo, wu, wd,
                   w_out, att, qh, kh, vh, lse, hid, act, pre, mid, nor1, inv1, gtwo, gffn, rows, table,
                   w, own, tiles, qkv, oh, kseq, own_sems, out_sems, swap_sems, *sems):
    rt, swap = Route(), Swap()
    shift = 7 + swap.bucket
    loads = [pltpu.make_async_copy(ref, own.at[pl.ds(i * ROWS, ROWS)], own_sems.at[i]) for i, ref in enumerate((wq, wk, wv, wo))]
    loads.append(pltpu.make_async_copy(wd, own.at[pl.ds(4 * ROWS, 4 * ROWS)], own_sems.at[4]))
    for i in range(4):
        loads.append(pltpu.make_async_copy(wu.at[:, pl.ds(i * 1024, 1024)], own.at[pl.ds((8 + i) * ROWS, ROWS)], own_sems.at[5 + i]))
    for load in loads:
        load.start()
    main = Gatherer(
        rt, PIECES,
        lambda c: own.at[pl.ds(pl.multiple_of(c * ROWS, ROWS), ROWS)],
        lambda c, j: w.at[pl.ds(piece_row(c, j), ROWS)],
        lambda n: w.at[pl.ds(0, n * ROWS)],
        sems[:7],
    )
    small = Gatherer(rt, 1, lambda c: v_ref, lambda c, j: tiles.at[j], lambda n: tiles.at[pl.ds(0, n)], sems[7:])
    for load in loads:
        load.wait()
    rt.greet()

    def vec(row):
        return table[row:row + 1]

    def project(i):
        value = dense(x_ref[...], w[i * 1024:(i + 1) * 1024])
        if i != 1:
            value = value + vec(V_QUERY if i == 0 else V_VALUE)
        qkv[i] = value.astype(BF16)
        swap.heads_out(qkv.at[i], (qh, kh, vh)[i], *(swap_sems.at[3 * i + n] for n in range(3)))

    def start():
        small.arrived(0)
        table[0:16] = table_of(tiles)
        for i in range(4):
            table[V_UP + i:V_UP + i + 1] = jnp.concatenate([tiles[8 * i + j][8:9].astype(F32) for j in range(8)], axis=1)
        kseq[...] = key_sequences(len_ref, shift, kseq.shape[0])
        project(0)

    def score(first):
        if first == 0:
            for i, ref in enumerate((qh, kh, vh)):
                swap.wait(ref, *(swap_sems.at[3 * i + n] for n in range(3)))

        def block(i, _):
            attend_block(i, shift, kseq, qh, kh, vh, oh, lse)
            return 0

        lax.fori_loop(first, first + 2, block, 0)
        if first == 2:
            swap.heads_back(oh, att, *(swap_sems.at[9 + n] for n in range(3)))

    def first_norm():
        swap.wait(oh, *(swap_sems.at[9 + n] for n in range(3)))
        normed, inv = norm_parts(x_ref[...].astype(F32) + (dense(att[...], w[3072:4096]) + vec(V_OUT)))
        nor1[...] = normed
        inv1[...] = inv
        mid[...] = (normed * vec(V_GAIN1) + vec(V_SHIFT1)).astype(BF16)
        gtwo[...] = jnp.zeros_like(gtwo)

    def up(i):
        value = dense(mid[...], w[W_UP + i * 1024:W_UP + (i + 1) * 1024]) + vec(V_UP + i)
        pre[i] = value
        now = gelu_value(value).astype(BF16)
        act[:, i * 1024:(i + 1) * 1024] = now
        gtwo[...] += dense(now, w[W_DOWN + i * 1024:W_DOWN + (i + 1) * 1024])

    items = {
        7: start, 8: lambda: project(1), 9: lambda: project(2), 10: lambda: score(0), 11: lambda: score(2), 13: first_norm,
        15: lambda: up(0), 16: lambda: up(1), 17: lambda: up(2), 18: lambda: up(3),
    }

    def save(i):
        rows_of = pl.ds(pl.multiple_of(i * 1024, 1024), 1024)
        return pltpu.make_async_copy(w.at[rows_of], w_out.at[rows_of], out_sems.at[i])

    def step(t, _):
        for s in range(Gatherer.stages):
            c = t - s

            @when(c == 0)
            def _():
                small.stage(s, 0)

            @when((c >= 0) & (c < PIECES))
            def _():
                main.stage(s, c)

        c = t - Gatherer.stages

        @when(c >= 0)
        def _():
            main.arrived(c)

            @when((c < 4) | (c >= 8))
            def _():
                save(c).start()

            @when(c == 7)
            def _():
                for i in range(4, 8):
                    save(i).start()

        for k, item in items.items():

            @when(t == k)
            def _():
                item()

        return 0

    lax.fori_loop(0, PIECES + Gatherer.stages, step, 0)
    middle = nor1[...] * vec(V_GAIN1) + vec(V_SHIFT1)
    normed2, inv2 = norm_parts(middle + (gtwo[...] + vec(V_DOWN)))
    hid[...] = (normed2 * vec(V_GAIN2) + vec(V_SHIFT2)).astype(BF16)
    g = cot_ref[...].astype(F32)
    rows[...] = jnp.zeros_like(rows)
    rows[V_GAIN2:V_GAIN2 + 1] = column_sum(g * normed2)
    rows[V_SHIFT2:V_SHIFT2 + 1] = column_sum(g)
    back = norm_back(g, normed2, inv2, vec(V_GAIN2))
    gtwo[...] = back
    low = back.astype(BF16)
    gffn[...] = low
    rows[V_DOWN:V_DOWN + 1] = column_sum(low.astype(F32))
    small.finish()
    small.finish_z(0)

    def last(c, _):
        main.finish_z(c)
        save(c).wait()
        return 0

    lax.fori_loop(0, PIECES, last, 0)
    main.finish()


def shaped(shape, dtype):
    return jax.ShapeDtypeStruct(shape, dtype)


def forward(tokens, cotangent, small, lens, weights):
    vmem, anywhere = pl.BlockSpec(memory_space=pltpu.VMEM), pl.BlockSpec(memory_space=pl.ANY)
    dma = pltpu.SemaphoreType.DMA
    narrow, wide, heads = (128, 1024), (128, 4096), (1024, 128)
    return pl.pallas_call(
        forward_kernel,
        out_shape=(
            shaped((PIECES * 1024, 1024), BF16), shaped(narrow, BF16), shaped(heads, BF16), shaped(heads, BF16),
            shaped(heads, BF16), shaped((2, 1024), F32), shaped(narrow, BF16), shaped(wide, BF16),
            shaped((4,) + narrow, F32), shaped(narrow, BF16), shaped(narrow, F32), shaped((128, 1), F32),
            shaped(narrow, F32), shaped(narrow, BF16), shaped((16, 1024), F32), shaped((16, 1024), F32),
        ),
        in_specs=[vmem, vmem, vmem, pl.BlockSpec(memory_space=pltpu.SMEM)] + [anywhere] * 6,
        out_specs=(anywhere,) + (vmem,) * 15,
        scratch_shapes=[
            pltpu.VMEM((PIECES * 1024, 1024), BF16), pltpu.VMEM((PIECES * ROWS, 1024), BF16), pltpu.VMEM((32, 16, 128), BF16),
            pltpu.VMEM((3, 128, 1024), BF16), pltpu.VMEM(heads, BF16), pltpu.VMEM(heads, jnp.int32),
            dma((9,)), dma((PIECES,)), dma((12,)),
        ] + gather_sems(PIECES) + gather_sems(1),
        compiler_params=pltpu.CompilerParams(collective_id=0, has_side_effects=True, vmem_limit_bytes=VMEM_LIMIT),
    )(tokens, cotangent, small, lens, *weights)


def add_f32(left, right):
    return left.astype(F32) + right.astype(F32)


class Reducer:
    stages = 7

    def __init__(self, route, bufs, sems):
        self.rt = route
        (self.own, self.rb, self.ra, self.ru, self.rn, self.out) = bufs
        (self.sb_s, self.sb_r, self.sa_s, self.sa_r, self.sz_s, self.su_r, self.sn_r) = sems

    @staticmethod
    def slot(xx, yy, zz):
        return xx * 8 + zz * 2 + yy

    def add(self, c, k, other):
        self.own[c, k] = add_f32(self.own[c, k], other).astype(self.own.dtype)

    def to_b(self, c):
        rt = self.rt
        for same_a in (0, 1):
            for zz in range(4):
                xx, yy = (rt.bx, rt.by) if same_a else (1 - rt.x, 1 - rt.y)
                k = self.slot(xx, yy, zz)
                remote(self.own.at[c, k], self.rb.at[c, same_a * 4 + zz], self.sb_s.at[c], self.sb_r.at[c], rt.b).start()

    def to_a(self, c):
        rt = self.rt
        bytes_of(self.rb.at[c], self.sb_r.at[c]).wait()
        for zz in range(4):
            k = self.slot(rt.ax, rt.ay, zz)
            self.add(c, k, self.rb[c, zz])
            remote(self.own.at[c, k], self.ra.at[c, zz], self.sa_s.at[c], self.sa_r.at[c], rt.a).start()
        for zz in range(4):
            self.add(c, self.slot(rt.x, rt.y, zz), self.rb[c, 4 + zz])

    def from_a(self, c):
        rt = self.rt
        bytes_of(self.ra.at[c], self.sa_r.at[c]).wait()
        for zz in range(4):
            self.add(c, self.slot(rt.x, rt.y, zz), self.ra[c, zz])

    def along_z(self, c, hop):
        rt = self.rt
        x, y = rt.x, rt.y

        @when(rt.z == hop)
        def _():
            for d in range(3, hop, -1):
                k = self.slot(x, y, d)
                if hop > 0:
                    bytes_of(self.ru.at[c, d - 1], self.su_r.at[c, d - 1]).wait()
                    self.add(c, k, self.ru[c, d - 1])
                remote(self.own.at[c, k], self.ru.at[c, d - 1], self.sz_s.at[c, d], self.su_r.at[c, d - 1], rt.up).start()
            if hop > 0:
                bytes_of(self.ru.at[c, hop - 1], self.su_r.at[c, hop - 1]).wait()

        at = 3 - hop

        @when(rt.z == at)
        def _():
            for d in range(at):
                k = self.slot(x, y, d)
                if at < 3:
                    bytes_of(self.rn.at[c, d], self.sn_r.at[c, d]).wait()
                    self.add(c, k, self.rn[c, d])
                remote(self.own.at[c, k], self.rn.at[c, d], self.sz_s.at[c, d], self.sn_r.at[c, d], rt.down).start()
            if at < 3:
                bytes_of(self.rn.at[c, at], self.sn_r.at[c, at]).wait()

    def total(self, c):
        rt = self.rt
        k = self.slot(rt.x, rt.y, rt.z)

        @when(rt.z == 0)
        def _():
            self.out[c] = add_f32(self.own[c, k], self.rn[c, 0])

        @when(rt.z == 3)
        def _():
            self.out[c] = add_f32(self.own[c, k], self.ru[c, 2])

        for at in (1, 2):

            @when(rt.z == at)
            def _():
                self.out[c] = add_f32(self.own[c, k], self.ru[c, at - 1]) + self.rn[c, at].astype(F32)

    def stage(self, s, c):
        if s == 0:
            self.to_b(c)
        if s == 2:
            self.to_a(c)
        if s == 3:
            self.from_a(c)
        if s >= 3:
            self.along_z(c, s - 3)
        if s == 6:
            self.total(c)

    def finish(self, c):
        rt = self.rt
        bytes_of(self.rb.at[c], self.sb_s.at[c]).wait()
        bytes_of(self.ra.at[c], self.sa_s.at[c]).wait()
        for d in range(4):

            @when(rt.z != d)
            def _():
                bytes_of(self.ra.at[c, 0], self.sz_s.at[c, d]).wait()


def reducer_bufs(count, block, dtype):
    return [pltpu.VMEM((count, n) + block, dtype) for n in (16, 8, 4, 3, 3)] + [pltpu.VMEM((count,) + block, F32)]


def reducer_sems(count):
    dma = pltpu.SemaphoreType.DMA
    return [dma((count,))] * 4 + [dma((count, 4)), dma((count, 3)), dma((count, 3))]


class Shared:
    def __init__(self, route, ref, sems, at):
        self.rt, self.ref, self.send, self.recv = route, ref, sems.at[2 * at], sems.at[2 * at + 1]

    def give(self):
        remote(self.ref.at[pl.ds(0, 128)], self.ref.at[pl.ds(128, 128)], self.send, self.recv, self.rt.sibling).start()

    def wait(self):
        bytes_of(self.ref.at[pl.ds(0, 128)], self.recv).wait()

    def sent(self):
        bytes_of(self.ref.at[pl.ds(0, 128)], self.send).wait()


def backward_kernel(x_ref, att, qh, kh, vh, lse, act, pre, mid, nor1, inv1, gtwo, gffn, rows_in, table, len_ref, w,
                    gin, sums, small_out,
                    x2, att2, mid2, act2, gffn2, gpre2, gbr2, dq2, dk2, dv2, rows2, wbuf, gatt, doh, dqh, dk, dv, dkh, dvh,
                    kseq, acc, w_sems, swap_sems, shared_sems, *rest):
    rt, swap = Route(), Swap()
    shift = 7 + swap.bucket
    m_bufs, m_sems, v_bufs, v_sems = rest[:6], rest[6:13], rest[13:19], rest[19:26]
    main, small = Reducer(rt, m_bufs, m_sems), Reducer(rt, v_bufs, v_sems)
    own = m_bufs[0]
    pairs = (x2, att2, mid2, act2, gffn2, gpre2, gbr2, dq2, dk2, dv2)
    sx, satt, smid, sact, sgffn, sgpre, sgbr, sdq, sdk, sdv = (Shared(rt, ref, shared_sems, i) for i, ref in enumerate(pairs))

    order = [4, 8, 5, 9, 6, 10, 7, 11, 3, 0, 1, 2]
    slots = wbuf.shape[0]

    def load(n):
        return pltpu.make_async_copy(w.at[pl.ds(order[n] * 1024, 1024)], wbuf.at[n % slots], w_sems.at[n])

    for n in range(slots):
        load(n).start()
    for ref, value in ((x2, x_ref), (att2, att), (mid2, mid), (act2, act), (gffn2, gffn)):
        ref[0:128] = value[...]
    rt.greet()
    for one in (sgffn, sact, smid, satt, sx):
        one.give()

    def used(n):
        if n + slots < PIECES:
            load(n + slots).start()

    def tall(left, right, first):
        def one(i, _):
            j = (i // 8) * 16 + rt.core * 8 + i % 8
            part = left[:, pl.ds(pl.multiple_of(j * 128, 128), 128)]
            grad = outer(part, right[...]).astype(BF16)
            for q in range(4):
                own[first + q, i] = grad[q * ROWS:(q + 1) * ROWS]
            return 0

        lax.fori_loop(0, 16, one, 0)

    def square(left, right, c):
        for xx in range(2):
            part = left[:, pl.ds(pl.multiple_of((xx * 2 + rt.core) * 256, 256), 256)]
            own[c, xx * 8:xx * 8 + 8] = outer(part, right).astype(BF16).reshape(8, ROWS, 1024)

    def compute(c):
        @when(c == 0)
        def _():
            sgffn.wait()
            sact.wait()
            tall(act2, gffn2, 0)

        @when(c == 4)
        def _():
            sgpre.wait()
            smid.wait()

        @when((c >= 4) & (c < 8))
        def _():
            square(mid2, gpre2[:, pl.ds(pl.multiple_of((c - 4) * 1024, 1024), 1024)], c)

        for k, (left, right, lw, rw) in enumerate(
            ((att2, gbr2, satt, sgbr), (x2, dq2, sx, sdq), (x2, dk2, None, sdk), (x2, dv2, None, sdv))
        ):

            @when(c == 8 + k)
            def _():
                if lw is not None:
                    lw.wait()
                rw.wait()
                square(left, right[...], c)

    def compute_small():
        bytes_of(rows2.at[1], shared_sems.at[21]).wait()
        both = rows2[0] + rows2[1]
        rows2[0] = both

        def one(i, _):
            j = (i // 8) * 16 + rt.core * 8 + i % 8
            v_bufs[0][0, i, 0:8] = rows2[0, 0:8, pl.ds(pl.multiple_of((j // 4) * 128, 128), 128)]
            ups = rows2[0, 8:16, pl.ds(pl.multiple_of((j % 8) * 128, 128), 128)]
            row = lax.broadcasted_iota(jnp.int32, (8, 128), 0)
            v_bufs[0][0, i, 8:16] = jnp.where(row == j // 8, ups, 0.0)
            return 0

        lax.fori_loop(0, 16, one, 0)

    rows2[0] = rows_in[...]

    def ffn_back(i):
        load(2 * i).wait()
        gact = inner(gffn2[0:128], wbuf[(2 * i) % slots]).astype(BF16).astype(F32)
        used(2 * i)
        gpre = (gact * gelu_slope(pre[i])).astype(BF16)
        gpre2[0:128, i * 1024:(i + 1) * 1024] = gpre
        rows2[0, V_UP + i:V_UP + i + 1] = column_sum(gpre.astype(F32))
        load(2 * i + 1).wait()
        part = inner(gpre, wbuf[(2 * i + 1) % slots])
        used(2 * i + 1)
        if i == 0:
            acc[...] = part
        else:
            acc[...] += part

    def ffn_end():
        sgpre.give()
        gmid = gtwo[...] + acc[...].astype(BF16).astype(F32)
        normed1 = nor1[...]
        rows2[0, V_GAIN1:V_GAIN1 + 1] = column_sum(gmid * normed1)
        rows2[0, V_SHIFT1:V_SHIFT1 + 1] = column_sum(gmid)
        gone = norm_back(gmid, normed1, inv1[...], table[V_GAIN1:V_GAIN1 + 1])
        acc[...] = gone
        gbr = gone.astype(BF16)
        gbr2[0:128] = gbr
        sgbr.give()
        rows2[0, V_OUT:V_OUT + 1] = column_sum(gbr.astype(F32))
        load(8).wait()
        gatt[...] = inner(gbr, wbuf[8 % slots]).astype(BF16)
        used(8)
        swap.heads_out(gatt, doh, *(swap_sems.at[n] for n in range(3)))
        kseq[...] = key_sequences(len_ref, shift, kseq.shape[0])
        dk[...] = jnp.zeros_like(dk)
        dv[...] = jnp.zeros_like(dv)

    def score_back(first, count):
        if first == 0:
            swap.wait(doh, *(swap_sems.at[n] for n in range(3)))

        def block(i, _):
            attend_back_block(i, shift, kseq, qh, kh, vh, doh, lse, dqh, dk, dv)
            return 0

        lax.fori_loop(first, first + count, block, 0)

    trio = ((dqh, dq2, sdq), (dkh, dk2, sdk), (dvh, dv2, sdv))

    def score_end():
        dkh[...] = dk[...].astype(BF16)
        dvh[...] = dv[...].astype(BF16)
        for i, (src, dst, _) in enumerate(trio):
            swap.heads_back(src, dst.at[pl.ds(0, 128)], *(swap_sems.at[3 * i + 3 + n] for n in range(3)))

    def exchange():
        for i, (src, dst, shared) in enumerate(trio):
            swap.wait(src, *(swap_sems.at[3 * i + 3 + n] for n in range(3)))
            shared.give()
        rows2[0, V_QUERY:V_QUERY + 1] = column_sum(dq2[0:128].astype(F32))
        rows2[0, V_VALUE:V_VALUE + 1] = column_sum(dv2[0:128].astype(F32))
        remote(rows2.at[0], rows2.at[1], shared_sems.at[20], shared_sems.at[21], rt.sibling).start()

    def input_grad():
        total = acc[...]
        for i, ref in enumerate((dq2, dk2, dv2)):
            load(9 + i).wait()
            total = total + inner(ref[0:128], wbuf[(9 + i) % slots])
        gin[...] = total
        bytes_of(rows2.at[0], shared_sems.at[20]).wait()

    items = {
        0: (lambda: ffn_back(0), lambda: ffn_back(1)),
        1: (lambda: ffn_back(2), lambda: ffn_back(3), ffn_end),
        2: (lambda: score_back(0, 1),), 3: (lambda: score_back(1, 1),), 4: (lambda: score_back(2, 1),),
        5: (lambda: score_back(3, 1), score_end),
        7: (exchange,), 8: (input_grad,),
    }

    def step(t, _):
        @when(t < PIECES)
        def _():
            compute(t)
            main.stage(0, t)

        @when(t == PIECES)
        def _():
            compute_small()
            small.stage(0, 0)

        for s in range(Reducer.stages - 1, 0, -1):
            c = t - s

            @when((c >= 0) & (c < PIECES))
            def _():
                main.stage(s, c)

            @when(c == PIECES)
            def _():
                small.stage(s, 0)

        for k, parts in items.items():

            @when(t == k)
            def _():
                for part in parts:
                    part()

        return 0

    lax.fori_loop(0, PIECES + Reducer.stages, step, 0)

    def last(c, _):
        main.finish(c)
        return 0

    lax.fori_loop(0, PIECES, last, 0)
    small.finish(0)
    for one in (sx, satt, smid, sact, sgffn, sgpre, sgbr, sdq, sdk, sdv):
        one.sent()
    sums[...] = m_bufs[5][...]
    mine = v_bufs[5][0]
    quarter = owner(rt.x, rt.y, rt.z, rt.core) % 4
    picked = jnp.zeros((16, 32), F32)
    for q in range(4):
        picked = jnp.where(quarter == q, mine[:, q * 32:(q + 1) * 32], picked)
    small_out[:, 0:128] = jnp.broadcast_to(column_sum(mine[8:16]), (16, 128))
    small_out[:, 128:160] = picked


def backward(tokens, kept, lens, weights):
    vmem, anywhere = pl.BlockSpec(memory_space=pltpu.VMEM), pl.BlockSpec(memory_space=pl.ANY)
    dma = pltpu.SemaphoreType.DMA
    narrow, heads = (128, 1024), (1024, 128)
    pair, wide_pair = pltpu.VMEM((256, 1024), BF16), pltpu.VMEM((256, 4096), BF16)
    half, full = pltpu.VMEM(heads, BF16), pltpu.VMEM(heads, F32)
    return pl.pallas_call(
        backward_kernel,
        out_shape=(shaped(narrow, F32), shaped((PIECES, ROWS, 1024), F32), shaped((16, 256), F32)),
        in_specs=[vmem] * (1 + len(kept)) + [pl.BlockSpec(memory_space=pltpu.SMEM), anywhere],
        out_specs=(vmem,) * 3,
        scratch_shapes=[
            pair, pair, pair, wide_pair, pair, wide_pair, pair, pair, pair, pair, pltpu.VMEM((2, 16, 1024), F32),
            pltpu.VMEM((4, 1024, 1024), BF16), pltpu.VMEM(narrow, BF16), half, half, full, full, half, half,
            pltpu.VMEM(heads, jnp.int32), pltpu.VMEM(narrow, F32), dma((PIECES,)), dma((12,)), dma((22,)),
        ] + reducer_bufs(PIECES, (ROWS, 1024), BF16) + reducer_sems(PIECES)
        + reducer_bufs(1, (16, 128), F32) + reducer_sems(1),
        compiler_params=pltpu.CompilerParams(collective_id=1, has_side_effects=True, vmem_limit_bytes=VMEM_LIMIT),
    )(tokens, *kept, lens, weights)


def fast_body(hidden_in, lengths, w_query, w_key, w_value, b_query, b_value, w_out, b_out, first_gain, first_shift,
              w_up, b_up, w_down, b_down, second_gain, second_shift, cotangent):
    tokens = hidden_in.reshape(128, 1024)
    me = lax.axis_index("bucket") * 8 + lax.axis_index("ctx")
    rows = jnp.stack([b_query, b_value, b_out, first_gain, first_shift, b_down, second_gain, second_shift])
    spread = jnp.concatenate([jnp.where(me % 4 == q, rows, jnp.zeros_like(rows)) for q in range(4)], axis=1)
    small = jnp.concatenate([spread, b_up[None], jnp.zeros((7, 128), BF16)], axis=0)
    lens = lengths.reshape(8)
    (weights, att, qh, kh, vh, lse, hidden_out, act, pre, mid, nor1, inv1, gtwo, gffn, rows16, table) = forward(
        tokens, cotangent.reshape(128, 1024), small, lens, (w_query, w_key, w_value, w_out, w_up, w_down)
    )
    grad_in, sums, small_sums = backward(
        tokens, (att, qh, kh, vh, lse, act, pre, mid, nor1, inv1, gtwo, gffn, rows16, table), lens, weights
    )
    g_down = sums[:4].reshape(128, 1024)
    g_up = jnp.concatenate([sums[4 + i] for i in range(4)], axis=1)
    row = lambda r: small_sums[r, 128:160]
    return (
        hidden_out.reshape(hidden_in.shape), grad_in.reshape(hidden_in.shape), sums[9], sums[10], sums[11],
        row(0), row(1), sums[8], row(2), row(3), row(4), g_up, small_sums[8, 0:128], g_down, row(5), row(6), row(7),
    )


def matmul(left, right):
    return jnp.dot(left, right, preferred_element_type=jnp.float32)


def row_inner(left, right):
    return lax.dot_general(
        left, right, (((0,), (0,)), ((), ())), preferred_element_type=jnp.float32
    )


def right_inner(left, right):
    return lax.dot_general(
        left, right, (((1,), (1,)), ((), ())), preferred_element_type=jnp.float32
    )


def rounded(values):
    return values.astype(jnp.bfloat16)


def widened(values):
    return values.astype(jnp.float32)


def norm_forward(summed, gain_vec, shift_vec):
    average = jnp.mean(summed, axis=-1, keepdims=True)
    centred = summed - average
    variance = jnp.mean(centred * centred, axis=-1, keepdims=True)
    inv_std = lax.rsqrt(variance + EPSILON)
    normed = centred * inv_std
    return (normed * gain_vec + shift_vec, normed, inv_std)


def norm_backward(incoming, normed, inv_std, gain_vec):
    scaled = incoming * gain_vec
    inner = (
        scaled
        - jnp.mean(scaled, axis=-1, keepdims=True)
        - normed * jnp.mean(scaled * normed, axis=-1, keepdims=True)
    )
    return (inv_std * inner, jnp.sum(incoming * normed, axis=0), jnp.sum(incoming, axis=0))


def plain_gelu_value(values):
    return 0.5 * values * (1.0 + jax.scipy.special.erf(values * 0.7071067811865476))


def plain_gelu_slope(values):
    return (
        0.5 * (1.0 + jax.scipy.special.erf(values * 0.7071067811865476))
        + values * jnp.exp(-0.5 * values * values) * 0.3989422804014327
    )


def split_heads(values):
    return values.reshape(values.shape[0], values.shape[1], values.shape[2] // HEAD_DIM, HEAD_DIM)


def seq_mask(seq_info, query_pos, key_pos):
    seq_lens, slot_len = seq_info
    query_seq = query_pos // slot_len
    key_seq = key_pos // slot_len
    seq_ids = jnp.arange(seq_lens.shape[1], dtype=jnp.int32)
    picked = (key_seq[:, None] == seq_ids[None, :]).astype(jnp.int32)
    key_limit = jnp.sum(picked[None, :, :] * seq_lens[:, None, :], axis=-1)
    key_valid = (key_pos - key_seq * slot_len)[None, :] < key_limit
    same_seq = query_seq[:, None] == key_seq[None, :]
    return (same_seq[None, :, :] & key_valid[:, None, :])[:, None, :, :]


def score_block(query4, key4, query_start, key_start, seq_info):
    raw = jnp.einsum(
        "sqhd,skhd->shqk", query4, key4, preferred_element_type=jnp.float32
    ) * HEAD_DIM ** (-0.5)
    query_pos = query_start + jnp.arange(query4.shape[1], dtype=jnp.int32)
    key_pos = key_start + jnp.arange(key4.shape[1], dtype=jnp.int32)
    allowed = seq_mask(seq_info, query_pos, key_pos)
    return (jnp.where(allowed, raw, NEG_FILL), allowed)


def over_blocks(block_step, running, pieces):
    length_here = pieces[0].shape[1]
    block_len = math.gcd(length_here, 512)
    turn_count = length_here // block_len

    def advance(turn_no, current):
        offset = turn_no * block_len
        sliced = tuple(
            (lax.dynamic_slice_in_dim(piece_arr, offset, block_len, 1) for piece_arr in pieces)
        )
        return block_step(current, sliced, offset)

    return lax.fori_loop(0, turn_count, advance, running)


def general_body(
    hidden_in,
    lengths,
    w_query,
    w_key,
    w_value,
    b_query,
    b_value,
    w_out,
    b_out,
    first_gain,
    first_shift,
    w_up,
    b_up,
    w_down,
    b_down,
    second_gain,
    second_shift,
    cotangent,
):
    shards = (
        w_query,
        w_key,
        w_value,
        b_query,
        b_value,
        w_out,
        b_out,
        first_gain,
        first_shift,
        w_up,
        b_up,
        w_down,
        b_down,
        second_gain,
        second_shift,
    )
    gathered = (
        lax.all_gather(shards[0], ("bucket", "ctx"), axis=0, tiled=True),
        lax.all_gather(shards[1], ("bucket", "ctx"), axis=0, tiled=True),
        lax.all_gather(shards[2], ("bucket", "ctx"), axis=0, tiled=True),
        lax.all_gather(shards[3], ("bucket", "ctx"), axis=0, tiled=True),
        lax.all_gather(shards[4], ("bucket", "ctx"), axis=0, tiled=True),
        lax.all_gather(shards[5], ("bucket", "ctx"), axis=0, tiled=True),
        lax.all_gather(shards[6], ("bucket", "ctx"), axis=0, tiled=True),
        lax.all_gather(shards[7], ("bucket", "ctx"), axis=0, tiled=True),
        lax.all_gather(shards[8], ("bucket", "ctx"), axis=0, tiled=True),
        lax.all_gather(shards[9], ("bucket", "ctx"), axis=0, tiled=True),
        lax.all_gather(shards[10], ("bucket", "ctx"), axis=0, tiled=True),
        lax.all_gather(shards[11], ("bucket", "ctx"), axis=0, tiled=True),
        lax.all_gather(shards[12], ("bucket", "ctx"), axis=0, tiled=True),
        lax.all_gather(shards[13], ("bucket", "ctx"), axis=0, tiled=True),
        lax.all_gather(shards[14], ("bucket", "ctx"), axis=0, tiled=True),
    )
    (
        query_mat,
        key_mat,
        value_mat,
        query_bias,
        value_bias,
        out_mat,
        out_bias,
        gain_one,
        shift_one,
        up_mat,
        up_bias,
        down_mat,
        down_bias,
        gain_two,
        shift_two,
    ) = gathered
    seq_count = hidden_in.shape[1]
    local_rows = hidden_in.shape[2]
    model_width = hidden_in.shape[3]
    head_count = model_width // HEAD_DIM
    total_rows = seq_count * local_rows
    block_shape = (seq_count, local_rows, model_width)
    score_scale = HEAD_DIM ** (-0.5)
    seq_total = local_rows * lax.axis_size("ctx")
    group_index = lax.axis_index("bucket")
    seq_slots = jnp.right_shift(jnp.int32(lengths.shape[2]), group_index)
    slot_len = jnp.int32(seq_total) // seq_slots
    seq_info = (lengths[0], slot_len)
    own_start = lax.axis_index("ctx") * local_rows
    tokens = hidden_in.reshape(total_rows, model_width)
    query_low = rounded(matmul(tokens, query_mat) + widened(query_bias))
    key_low = rounded(matmul(tokens, key_mat))
    value_low = rounded(matmul(tokens, value_mat) + widened(value_bias))
    query_heads = split_heads(query_low.reshape(block_shape))
    key_rows = key_low.reshape(block_shape)
    value_rows = value_low.reshape(block_shape)

    def stats_step(running, sliced, anchor):
        scores, allowed = score_block(
            query_heads, split_heads(sliced[0]), own_start, anchor, seq_info
        )
        run_max, run_total = running
        new_max = jnp.maximum(run_max, jnp.max(scores, axis=-1))
        raised = jnp.where(allowed, jnp.exp(scores - new_max[..., None]), 0.0)
        return (new_max, run_total * jnp.exp(run_max - new_max) + jnp.sum(raised, axis=-1))

    stat_shape = (seq_count, head_count, local_rows)
    stats_start = (jnp.full(stat_shape, NEG_FILL, jnp.float32), jnp.zeros(stat_shape, jnp.float32))
    run_max, run_total = over_blocks(
        stats_step, stats_start, (lax.all_gather(key_rows, "ctx", axis=1, tiled=True),)
    )
    log_total = run_max + jnp.log(run_total)

    def output_step(running, sliced, anchor):
        key4 = split_heads(sliced[0])
        value4 = split_heads(sliced[1])
        scores, allowed = score_block(query_heads, key4, own_start, anchor, seq_info)
        probs_low = rounded(jnp.where(allowed, jnp.exp(scores - log_total[..., None]), 0.0))
        return running + jnp.einsum(
            "shqk,skhd->sqhd", probs_low, value4, preferred_element_type=jnp.float32
        )

    attended_f32 = over_blocks(
        output_step,
        jnp.zeros(query_heads.shape, jnp.float32),
        (
            lax.all_gather(key_rows, "ctx", axis=1, tiled=True),
            lax.all_gather(value_rows, "ctx", axis=1, tiled=True),
        ),
    )
    attended_low = rounded(attended_f32.reshape(total_rows, model_width))
    branch = matmul(attended_low, out_mat) + widened(out_bias)
    middle, normed_one, inv_one = norm_forward(
        widened(tokens) + branch, widened(gain_one), widened(shift_one)
    )
    middle_low = rounded(middle)
    pre_act = matmul(middle_low, up_mat) + widened(up_bias)
    activated = rounded(plain_gelu_value(pre_act))
    ffn_out = matmul(activated, down_mat) + widened(down_bias)
    result, normed_two, inv_two = norm_forward(
        middle + ffn_out, widened(gain_two), widened(shift_two)
    )
    hidden_out = rounded(result).reshape(hidden_in.shape)
    gathered = (
        lax.all_gather(shards[0], ("bucket", "ctx"), axis=0, tiled=True),
        lax.all_gather(shards[1], ("bucket", "ctx"), axis=0, tiled=True),
        lax.all_gather(shards[2], ("bucket", "ctx"), axis=0, tiled=True),
        lax.all_gather(shards[3], ("bucket", "ctx"), axis=0, tiled=True),
        lax.all_gather(shards[4], ("bucket", "ctx"), axis=0, tiled=True),
        lax.all_gather(shards[5], ("bucket", "ctx"), axis=0, tiled=True),
        lax.all_gather(shards[6], ("bucket", "ctx"), axis=0, tiled=True),
        lax.all_gather(shards[7], ("bucket", "ctx"), axis=0, tiled=True),
        lax.all_gather(shards[8], ("bucket", "ctx"), axis=0, tiled=True),
        lax.all_gather(shards[9], ("bucket", "ctx"), axis=0, tiled=True),
        lax.all_gather(shards[10], ("bucket", "ctx"), axis=0, tiled=True),
        lax.all_gather(shards[11], ("bucket", "ctx"), axis=0, tiled=True),
        lax.all_gather(shards[12], ("bucket", "ctx"), axis=0, tiled=True),
        lax.all_gather(shards[13], ("bucket", "ctx"), axis=0, tiled=True),
        lax.all_gather(shards[14], ("bucket", "ctx"), axis=0, tiled=True),
    )
    query_mat = gathered[0]
    key_mat = gathered[1]
    value_mat = gathered[2]
    out_mat = gathered[5]
    gain_one = gathered[7]
    up_mat = gathered[9]
    down_mat = gathered[11]
    gain_two = gathered[13]
    incoming = widened(cotangent.reshape(total_rows, model_width))
    grad_two_sum, grad_second_gain, grad_second_shift = norm_backward(
        incoming, normed_two, inv_two, widened(gain_two)
    )
    grad_ffn = rounded(grad_two_sum)
    grad_b_down = jnp.sum(widened(grad_ffn), axis=0)
    grad_w_down = row_inner(activated, grad_ffn)
    grad_act = widened(rounded(right_inner(grad_ffn, down_mat)))
    grad_pre = rounded(grad_act * plain_gelu_slope(pre_act))
    grad_b_up = jnp.sum(widened(grad_pre), axis=0)
    grad_w_up = row_inner(middle_low, grad_pre)
    grad_middle = grad_two_sum + widened(rounded(right_inner(grad_pre, up_mat)))
    grad_one_sum, grad_first_gain, grad_first_shift = norm_backward(
        grad_middle, normed_one, inv_one, widened(gain_one)
    )
    grad_branch = rounded(grad_one_sum)
    grad_b_out = jnp.sum(widened(grad_branch), axis=0)
    grad_w_out = row_inner(attended_low, grad_branch)
    grad_att = rounded(right_inner(grad_branch, out_mat)).reshape(block_shape)
    grad_att_heads = split_heads(grad_att)
    delta = jnp.einsum("sqhd,sqhd->shq", widened(grad_att_heads), attended_f32)

    def grad_terms(query4, key4, value4, att4, row_log, row_delta, query_start, key_start):
        scores, allowed = score_block(query4, key4, query_start, key_start, seq_info)
        probs = jnp.where(allowed, jnp.exp(scores - row_log[..., None]), 0.0)
        slope = jnp.einsum("sqhd,skhd->shqk", att4, value4, preferred_element_type=jnp.float32)
        return (rounded(probs), rounded(probs * (slope - row_delta[..., None])))

    def query_step(running, sliced, anchor):
        key4 = split_heads(sliced[0])
        value4 = split_heads(sliced[1])
        probs_low, score_grad = grad_terms(
            query_heads, key4, value4, grad_att_heads, log_total, delta, own_start, anchor
        )
        return (
            running
            + jnp.einsum("shqk,skhd->sqhd", score_grad, key4, preferred_element_type=jnp.float32)
            * score_scale
        )

    grad_q = over_blocks(
        query_step,
        jnp.zeros(query_heads.shape, jnp.float32),
        (
            lax.all_gather(key_rows, "ctx", axis=1, tiled=True),
            lax.all_gather(value_rows, "ctx", axis=1, tiled=True),
        ),
    )
    log_all, delta_all = (
        lax.all_gather(log_total, "ctx", axis=2, tiled=True),
        lax.all_gather(delta, "ctx", axis=2, tiled=True),
    )
    own_keys = split_heads(key_rows)
    own_values = split_heads(value_rows)

    def owner_step(running, sliced, anchor):
        query4 = split_heads(sliced[0])
        att4 = split_heads(sliced[1])
        count_here = sliced[0].shape[1]
        row_log = lax.dynamic_slice_in_dim(log_all, anchor, count_here, 2)
        row_delta = lax.dynamic_slice_in_dim(delta_all, anchor, count_here, 2)
        probs_low, score_grad = grad_terms(
            query4, own_keys, own_values, att4, row_log, row_delta, anchor, own_start
        )
        grad_k, grad_v = running
        grad_k = (
            grad_k
            + jnp.einsum("shqk,sqhd->skhd", score_grad, query4, preferred_element_type=jnp.float32)
            * score_scale
        )
        grad_v = grad_v + jnp.einsum(
            "shqk,sqhd->skhd", probs_low, att4, preferred_element_type=jnp.float32
        )
        return (grad_k, grad_v)

    owner_start = (jnp.zeros(own_keys.shape, jnp.float32), jnp.zeros(own_keys.shape, jnp.float32))
    grad_k_own, grad_v_own = over_blocks(
        owner_step,
        owner_start,
        (
            lax.all_gather(query_low.reshape(block_shape), "ctx", axis=1, tiled=True),
            lax.all_gather(grad_att, "ctx", axis=1, tiled=True),
        ),
    )
    grad_q_low = rounded(grad_q.reshape(total_rows, model_width))
    grad_k_low = rounded(grad_k_own.reshape(total_rows, model_width))
    grad_v_low = rounded(grad_v_own.reshape(total_rows, model_width))
    grad_w_query = row_inner(tokens, grad_q_low)
    grad_b_query = jnp.sum(widened(grad_q_low), axis=0)
    grad_w_key = row_inner(tokens, grad_k_low)
    grad_w_value = row_inner(tokens, grad_v_low)
    grad_b_value = jnp.sum(widened(grad_v_low), axis=0)
    grad_in = (
        grad_one_sum
        + right_inner(grad_q_low, query_mat)
        + right_inner(grad_k_low, key_mat)
        + right_inner(grad_v_low, value_mat)
    )
    owned = (
        lax.psum_scatter(grad_w_query, ("bucket", "ctx"), scatter_dimension=0, tiled=True),
        lax.psum_scatter(grad_w_key, ("bucket", "ctx"), scatter_dimension=0, tiled=True),
        lax.psum_scatter(grad_w_value, ("bucket", "ctx"), scatter_dimension=0, tiled=True),
        lax.psum_scatter(grad_b_query, ("bucket", "ctx"), scatter_dimension=0, tiled=True),
        lax.psum_scatter(grad_b_value, ("bucket", "ctx"), scatter_dimension=0, tiled=True),
        lax.psum_scatter(grad_w_out, ("bucket", "ctx"), scatter_dimension=0, tiled=True),
        lax.psum_scatter(grad_b_out, ("bucket", "ctx"), scatter_dimension=0, tiled=True),
        lax.psum_scatter(grad_first_gain, ("bucket", "ctx"), scatter_dimension=0, tiled=True),
        lax.psum_scatter(grad_first_shift, ("bucket", "ctx"), scatter_dimension=0, tiled=True),
        lax.psum_scatter(grad_w_up, ("bucket", "ctx"), scatter_dimension=0, tiled=True),
        lax.psum_scatter(grad_b_up, ("bucket", "ctx"), scatter_dimension=0, tiled=True),
        lax.psum_scatter(grad_w_down, ("bucket", "ctx"), scatter_dimension=0, tiled=True),
        lax.psum_scatter(grad_b_down, ("bucket", "ctx"), scatter_dimension=0, tiled=True),
        lax.psum_scatter(grad_second_gain, ("bucket", "ctx"), scatter_dimension=0, tiled=True),
        lax.psum_scatter(grad_second_shift, ("bucket", "ctx"), scatter_dimension=0, tiled=True),
    )
    return (hidden_out, grad_in.reshape(hidden_in.shape)) + tuple(owned)


def solution(mesh):
    placed = (
        P("bucket", None, "ctx", None),
        P("bucket", None, None),
        P(("bucket", "ctx"), None),
        P(("bucket", "ctx"), None),
        P(("bucket", "ctx"), None),
        P(("bucket", "ctx")),
        P(("bucket", "ctx")),
        P(("bucket", "ctx"), None),
        P(("bucket", "ctx")),
        P(("bucket", "ctx")),
        P(("bucket", "ctx")),
        P(("bucket", "ctx"), None),
        P(("bucket", "ctx")),
        P(("bucket", "ctx"), None),
        P(("bucket", "ctx")),
        P(("bucket", "ctx")),
        P(("bucket", "ctx")),
        P("bucket", None, "ctx", None),
    )
    def body(*arguments):
        here = dict(mesh.shape) == {"bucket": 4, "ctx": 8}
        shapes = arguments[0].shape == (1, 1, 128, 1024) and arguments[11].shape == (32, 4096)
        return (fast_body if here and shapes else general_body)(*arguments)

    return jax.shard_map(
        body,
        mesh=mesh,
        in_specs=placed,
        out_specs=(
            P("bucket", None, "ctx", None),
            P("bucket", None, "ctx", None),
            P(("bucket", "ctx"), None),
            P(("bucket", "ctx"), None),
            P(("bucket", "ctx"), None),
            P(("bucket", "ctx")),
            P(("bucket", "ctx")),
            P(("bucket", "ctx"), None),
            P(("bucket", "ctx")),
            P(("bucket", "ctx")),
            P(("bucket", "ctx")),
            P(("bucket", "ctx"), None),
            P(("bucket", "ctx")),
            P(("bucket", "ctx"), None),
            P(("bucket", "ctx")),
            P(("bucket", "ctx")),
            P(("bucket", "ctx")),
        ),
        check_vma=False,
    )
```

```python
import math

import jax
import jax.numpy as jnp
from jax import lax
from jax.experimental import pallas as pl
from jax.experimental.pallas import tpu as pltpu
from jax.sharding import PartitionSpec as P

HEAD_DIM = 64
EPSILON = 1e-05
NEG_FILL = -1e30
MESH_ID = pl.DeviceIdType.MESH
F32, BF16 = jnp.float32, jnp.bfloat16
ROWS = 32
PIECES = 12
VMEM_LIMIT = 63 * 2**20


def when(condition):
    return pl.when(condition)


def place():
    bucket, ctx = lax.axis_index("bucket"), lax.axis_index("ctx")
    return bucket // 2, ctx % 2, ctx // 2, bucket % 2


def device(x, y, z, core):
    return (x * 2 + core, z * 2 + y)


def owner(x, y, z, core):
    return (x * 2 + core) * 8 + z * 2 + y


def remote(src, dst, send_sem, recv_sem, target):
    return pltpu.make_async_remote_copy(
        src_ref=src, dst_ref=dst, send_sem=send_sem, recv_sem=recv_sem,
        device_id=target, device_id_type=MESH_ID,
    )


def bytes_of(ref, sem):
    return pltpu.make_async_copy(ref, ref, sem)


class Roles:
    def __init__(self, route, b_along_x):
        x, y, z, core = route.x, route.y, route.z, route.core
        self.ax, self.ay = jnp.where(b_along_x, x, 1 - x), jnp.where(b_along_x, 1 - y, y)
        self.bx, self.by = jnp.where(b_along_x, 1 - x, x), jnp.where(b_along_x, y, 1 - y)
        self.a = device(self.ax, self.ay, z, core)
        self.b = device(self.bx, self.by, z, core)


class Route:
    def __init__(self):
        self.x, self.y, self.z, self.core = x, y, z, core = place()
        self.across = (device(1 - x, y, z, core), device(x, 1 - y, z, core))
        self.sibling = device(x, y, z, 1 - core)
        self.up = device(x, y, jnp.minimum(z + 1, 3), core)
        self.down = device(x, y, jnp.maximum(z - 1, 0), core)

    def roles(self, turned):
        return Roles(self, (self.core == 1) | turned)

    def greet(self):
        z = self.z
        bucket, ctx = lax.axis_index("bucket"), lax.axis_index("ctx")
        barrier = pltpu.get_barrier_semaphore()
        pack = [(bucket, (ctx + off) % 8) for off in range(1, 8)]
        for target in [*self.across, self.sibling] + pack:
            pl.semaphore_signal(barrier, inc=1, device_id=target, device_id_type=MESH_ID)

        @when(z < 3)
        def _():
            pl.semaphore_signal(barrier, inc=1, device_id=self.up, device_id_type=MESH_ID)

        @when(z > 0)
        def _():
            pl.semaphore_signal(barrier, inc=1, device_id=self.down, device_id_type=MESH_ID)

        pl.semaphore_wait(barrier, 10 + (z < 3).astype(jnp.int32) + (z > 0).astype(jnp.int32))


class Plan:
    def __init__(self, count, mixed, turned):
        self.count, self.which_mixed, self.which_turned = count, mixed, turned

    def mixed(self, c):
        return self.member(c, self.which_mixed)

    def turned(self, c):
        return self.member(c, self.which_turned)

    @staticmethod
    def member(c, items):
        hit = jnp.bool_(False)
        for item in items:
            hit = hit | (c == item)
        return hit


class Gatherer:
    stages = 7

    def __init__(self, route, plan, own, block, span, sems):
        self.rt, self.plan, self.own, self.block, self.span = route, plan, own, block, span
        (self.zs, self.zr, self.ps, self.ar, self.br, self.dr, self.ls) = sems

    def spread(self, c, src, j, jz, ro, to_a, to_b, z_dirs):
        rt, dst = self.rt, self.block(c, j)
        which, directions = z_dirs
        if "up" in directions:

            @when(rt.z < 3)
            def _():
                remote(src, dst, self.zs.at[0, c, which, jz], self.zr.at[c, which, jz], rt.up).start()

        if "down" in directions:

            @when(rt.z > 0)
            def _():
                remote(src, dst, self.zs.at[1, c, which, jz], self.zr.at[c, which, jz], rt.down).start()

        if to_b is not None:
            remote(src, dst, self.ps, self.br.at[c, to_b * 4 + jz], ro.b).start()
        if to_a is not None:

            @when(to_a)
            def _():
                remote(src, dst, self.ps, self.ar.at[c, jz], ro.a).start()

        remote(src, dst, self.ps, self.dr.at[c], rt.sibling).start()

    def near(self, k, action):
        for sign in (0,) if k == 0 else (-1, 1):
            zz = self.rt.z + sign * k

            @when((zz >= 0) & (zz <= 3))
            def _():
                action(zz, "up" if sign < 0 else "down")

    def own_stage(self, c):
        rt, ro = self.rt, self.rt.roles(self.plan.turned(c))
        j = owner(rt.x, rt.y, rt.z, rt.core)
        pltpu.make_async_copy(self.own(c), self.block(c, j), self.ls.at[c]).start()
        self.spread(c, self.own(c), j, rt.z, ro, jnp.bool_(True), 0, (0, ("up", "down")))

    def z_stage(self, c, k):
        rt, ro = self.rt, self.rt.roles(self.plan.turned(c))

        def action(zz, direction):
            j = owner(rt.x, rt.y, zz, rt.core)
            bytes_of(self.block(c, j), self.zr.at[c, 0, zz]).wait()
            self.spread(c, self.block(c, j), j, zz, ro, ~self.plan.mixed(c), 0, (0, (direction,)))

        self.near(k, action)

    def z_stage_of_a(self, c, k):
        rt, ro = self.rt, self.rt.roles(self.plan.turned(c))

        def action(zz, direction):
            j = owner(ro.ax, ro.ay, zz, rt.core)
            bytes_of(self.block(c, j), self.zr.at[c, 1, zz]).wait()
            self.spread(c, self.block(c, j), j, zz, ro, None, 1, (1, (direction,)))

        self.near(k, action)

    def a_stage(self, c, k, directions=()):
        rt, ro = self.rt, self.rt.roles(self.plan.turned(c))

        def action(zz, _):
            j = owner(ro.ax, ro.ay, zz, rt.core)
            bytes_of(self.block(c, j), self.ar.at[c, zz]).wait()
            self.spread(c, self.block(c, j), j, zz, ro, None, 1, (1, directions))

        self.near(k, action)

    def b_stage(self, c, k):
        rt, ro = self.rt, self.rt.roles(self.plan.turned(c))

        def action(zz, _):
            for which, (xx, yy) in enumerate(((ro.bx, ro.by), (1 - rt.x, 1 - rt.y))):
                j = owner(xx, yy, zz, rt.core)
                bytes_of(self.block(c, j), self.br.at[c, which * 4 + zz]).wait()
                self.spread(c, self.block(c, j), j, zz, ro, None, None, (0, ()))

        self.near(k, action)

    def stage(self, s, c):
        mixed = self.plan.mixed(c)
        if s == 0:
            self.own_stage(c)
        if 1 <= s <= 3:
            self.z_stage(c, s)
        if s == 1:

            @when(mixed)
            def _():
                self.a_stage(c, 0, ("up", "down"))

            @when(~mixed)
            def _():
                self.a_stage(c, 0)

        if 2 <= s <= 4:

            @when(mixed)
            def _():
                self.z_stage_of_a(c, s - 1)

            @when(~mixed)
            def _():
                self.a_stage(c, s - 1)

        if 3 <= s <= 6:
            self.b_stage(c, s - 3)

    def arrived(self, c):
        bytes_of(self.span(16), self.dr.at[c]).wait()
        bytes_of(self.span(1), self.ls.at[c]).wait()

    def finish(self):
        bytes_of(self.span(28 * self.plan.count - 3 * len(self.plan.which_mixed)), self.ps).wait()

    def finish_z(self, c):
        rt = self.rt

        def sent(which):
            for zz in range(4):

                @when((rt.z < 3) & (rt.z >= zz))
                def _():
                    bytes_of(self.span(1), self.zs.at[0, c, which, zz]).wait()

                @when((rt.z > 0) & (rt.z <= zz))
                def _():
                    bytes_of(self.span(1), self.zs.at[1, c, which, zz]).wait()

        sent(0)

        @when(self.plan.mixed(c))
        def _():
            sent(1)


def gather_sems(count):
    dma = pltpu.SemaphoreType.DMA
    return [dma((2, count, 2, 4)), dma((count, 2, 4)), dma(()), dma((count, 4)), dma((count, 8)), dma((count,)), dma((count,))]


def outer(left, right):
    return lax.dot_general(left, right, (((0,), (0,)), ((), ())), preferred_element_type=F32)


def inner(left, right):
    return lax.dot_general(left, right, (((1,), (1,)), ((), ())), preferred_element_type=F32)


def dense(left, right):
    return jnp.dot(left, right, preferred_element_type=F32)


def head_mask(shape, head):
    lane = lax.broadcasted_iota(jnp.int32, shape, len(shape) - 1)
    return (lane // HEAD_DIM) == head


def only_head(values, head):
    return jnp.where(head_mask(values.shape, head), values, jnp.zeros_like(values))


def key_sequences(len_ref, shift, keys):
    pos = lax.broadcasted_iota(jnp.int32, (keys, 128), 0)
    seq = lax.shift_right_logical(pos, shift)
    at = pos - lax.shift_left(seq, shift)
    limit = jnp.zeros((keys, 128), jnp.int32)
    for s in range(8):
        limit = jnp.where(seq == s, len_ref[s], limit)
    return jnp.where(at < limit, seq, -1)


def key_bias(kseq, shift, start, width):
    keys = kseq.shape[0]
    qseq = lax.shift_right_logical(start + lax.broadcasted_iota(jnp.int32, (1, 128), 1), shift)
    parts = []
    for w in range(width // 128):
        qs = lax.shift_right_logical(start + w * 128 + lax.broadcasted_iota(jnp.int32, (1, 128), 1), shift)
        parts.append(jnp.where(kseq == qs, 0.0, NEG_FILL))
    return jnp.concatenate(parts, axis=1)


class Swap:
    def __init__(self):
        self.bucket, self.me = lax.axis_index("bucket"), lax.axis_index("ctx")

    def heads_out(self, tokens, heads, send_sem, recv_sem, local_sem):
        rows = pl.ds(pl.multiple_of(self.me * 128, 128), 128)
        for off in (4, 3, 5, 2, 6, 1, 7):
            d = (self.me + off) % 8
            remote(tokens.at[:, pl.ds(pl.multiple_of(d * 128, 128), 128)], heads.at[rows], send_sem, recv_sem, (self.bucket, d)).start()
        pltpu.make_async_copy(tokens.at[:, pl.ds(pl.multiple_of(self.me * 128, 128), 128)], heads.at[rows], local_sem).start()

    def heads_back(self, heads, tokens, send_sem, recv_sem, local_sem):
        cols = pl.ds(pl.multiple_of(self.me * 128, 128), 128)
        for off in (4, 3, 5, 2, 6, 1, 7):
            d = (self.me + off) % 8
            remote(heads.at[pl.ds(pl.multiple_of(d * 128, 128), 128)], tokens.at[:, cols], send_sem, recv_sem, (self.bucket, d)).start()
        pltpu.make_async_copy(heads.at[pl.ds(pl.multiple_of(self.me * 128, 128), 128)], tokens.at[:, cols], local_sem).start()

    def wait(self, heads, send_sem, recv_sem, local_sem):
        seven = heads.at[pl.ds(0, 7 * 128)]
        bytes_of(seven, recv_sem).wait()
        bytes_of(seven, send_sem).wait()
        bytes_of(heads.at[pl.ds(0, 128)], local_sem).wait()


Q_BLOCK = 256


def attend_block(i, shift, kseq, q, k, v, o_ref, lse_ref):
    start = i * Q_BLOCK
    rows = pl.ds(pl.multiple_of(start, Q_BLOCK), Q_BLOCK)
    bias = key_bias(kseq[...], shift, start, Q_BLOCK)
    scaled = q[rows] * jnp.asarray(HEAD_DIM ** (-0.5), BF16)
    result = []
    for h in range(2):
        s = inner(k[...], only_head(scaled, h)) + bias
        m = jnp.max(s, axis=0, keepdims=True)
        e = jnp.exp(s - m)
        total = jnp.sum(e, axis=0, keepdims=True)
        w = (e * (1.0 / total)).astype(BF16)
        lse_ref[h:h + 1, rows] = m + jnp.log(total)
        o = outer(v[...], w)
        result.append(o[h * HEAD_DIM:(h + 1) * HEAD_DIM])
    o_ref[rows] = jnp.concatenate(result, axis=0).T.astype(BF16)


def attend_back_block(i, shift, kseq, q, k, v, do, lse, dq, dk, dv):
    start = i * Q_BLOCK
    rows = pl.ds(pl.multiple_of(start, Q_BLOCK), Q_BLOCK)
    bias = key_bias(kseq[...], shift, start, Q_BLOCK)
    scaled = q[rows] * jnp.asarray(HEAD_DIM ** (-0.5), BF16)
    back = do[rows]
    result = []
    for h in range(2):
        qm, dm = only_head(scaled, h), only_head(back, h)
        p = jnp.exp(inner(k[...], qm) + bias - lse[h:h + 1, rows])
        slope = inner(v[...], dm)
        product = p * slope
        delta = jnp.sum(product, axis=0, keepdims=True)
        ds = (product - p * delta).astype(BF16)
        dv[...] += dense(p.astype(BF16), dm)
        dk[...] += dense(ds, qm)
        g = outer(k[...], ds) * (HEAD_DIM ** (-0.5))
        result.append(g[h * HEAD_DIM:(h + 1) * HEAD_DIM])
    dq[rows] = jnp.concatenate(result, axis=0).T.astype(BF16)


def table_of(t_ref):
    groups = []
    for g in range(8):
        groups.append(sum(t_ref[4 * g + i].astype(F32) for i in range(4)))
    return jnp.concatenate(groups, axis=1)


def gelu_value(values):
    return 0.5 * values * (1.0 + lax.erf(values * 0.7071067811865476))


def gelu_slope(values):
    return 0.5 * (1.0 + lax.erf(values * 0.7071067811865476)) + values * jnp.exp(-0.5 * values * values) * 0.3989422804014327


def row_mean(values):
    return jnp.mean(values, axis=-1, keepdims=True)


def column_sum(values):
    return jnp.sum(values, axis=0, keepdims=True)


def norm_parts(summed):
    centred = summed - row_mean(summed)
    inv_std = lax.rsqrt(row_mean(centred * centred) + EPSILON)
    return centred * inv_std, inv_std


def norm_back(incoming, normed, inv_std, gain):
    scaled = incoming * gain
    return inv_std * (scaled - row_mean(scaled) - normed * row_mean(scaled * normed))


V_QUERY, V_VALUE, V_OUT, V_GAIN1, V_SHIFT1, V_DOWN, V_GAIN2, V_SHIFT2 = range(8)
V_UP = 8
W_DOWN, W_UP = 4096, 8192
GATHER = Plan(PIECES, (1, 2, 4, 5, 7, 8, 10, 11), (2,))
REDUCE = Plan(PIECES, (0, 1, 3, 4, 6, 7, 9, 10), (7,))
ONE_PIECE = Plan(1, (), ())


def piece_row(c, j):
    tall = (c >= 4) & (c < 8)
    return pl.multiple_of(jnp.where(tall, W_DOWN + 128 * j + ROWS * (c - 4), c * 1024 + ROWS * j), ROWS)


def add_f32(left, right):
    return left.astype(F32) + right.astype(F32)


class Reducer:
    stages = 7

    def __init__(self, route, plan, own, rb, ra, ru, rn, out, sems):
        self.rt, self.plan = route, plan
        self.own, self.rb, self.ra, self.ru, self.rn, self.out = own, rb, ra, ru, rn, out
        (self.sb_s, self.sb_r, self.sa_s, self.sa_r, self.sz_s, self.su_r, self.sn_r) = sems

    @staticmethod
    def slot(xx, yy, zz):
        return xx * 8 + zz * 2 + yy

    def add(self, c, k, other):
        at = self.own(c, k)
        at[...] = add_f32(at[...], other).astype(at.dtype)

    def roles(self, c):
        return self.rt.roles(self.plan.turned(c))

    def b_blocks(self, c):
        rt, ro = self.rt, self.roles(c)
        blocks = []
        for same_a in (0, 1):
            for zz in range(4):
                xx, yy = (ro.bx, ro.by) if same_a else (1 - rt.x, 1 - rt.y)
                blocks.append((self.slot(xx, yy, zz), same_a * 4 + zz))
        return blocks

    def send_b(self, c, k, at):
        remote(self.own(c, k), self.rb.at[c, at], self.sb_s.at[c], self.sb_r.at[c], self.roles(c).b).start()

    def to_b(self, c):
        for k, at in self.b_blocks(c):
            self.send_b(c, k, at)

    def from_b(self, c):
        bytes_of(self.rb.at[c], self.sb_r.at[c]).wait()

    def to_a(self, c):
        rt, ro = self.rt, self.roles(c)
        for zz in range(4):
            k = self.slot(ro.ax, ro.ay, zz)
            self.add(c, k, self.rb[c, zz])
            remote(self.own(c, k), self.ra(c, zz), self.sa_s.at[c], self.sa_r.at[c], ro.a).start()
        for zz in range(4):
            self.add(c, self.slot(rt.x, rt.y, zz), self.rb[c, 4 + zz])

    def keep_b(self, c):
        rt, ro = self.rt, self.roles(c)
        for zz in range(4):
            self.add(c, self.slot(ro.ax, ro.ay, zz), self.rb[c, zz])
            self.add(c, self.slot(rt.x, rt.y, zz), self.rb[c, 4 + zz])

    def from_a(self, c):
        rt = self.rt
        bytes_of(self.rb.at[c, pl.ds(0, 4)], self.sa_r.at[c]).wait()
        for zz in range(4):
            self.add(c, self.slot(rt.x, rt.y, zz), self.ra(c, zz)[...])

    def along_z(self, c, hop, which):
        rt, ro = self.rt, self.roles(c)
        x, y = (ro.ax, ro.ay) if which else (rt.x, rt.y)

        @when(rt.z == hop)
        def _():
            for d in range(3, hop, -1):
                k = self.slot(x, y, d)
                at, sem = self.ru(c, which, d - 1), self.su_r.at[c, which, d - 1]
                if hop > 0:
                    bytes_of(at, sem).wait()
                    self.add(c, k, at[...])
                remote(self.own(c, k), at, self.sz_s.at[c, which, d], sem, rt.up).start()
            if hop > 0:
                bytes_of(self.ru(c, which, hop - 1), self.su_r.at[c, which, hop - 1]).wait()

        end = 3 - hop

        @when(rt.z == end)
        def _():
            for d in range(end):
                k = self.slot(x, y, d)
                at, sem = self.rn(c, which, d), self.sn_r.at[c, which, d]
                if end < 3:
                    bytes_of(at, sem).wait()
                    self.add(c, k, at[...])
                remote(self.own(c, k), at, self.sz_s.at[c, which, d], sem, rt.down).start()
            if end < 3:
                bytes_of(self.rn(c, which, end), self.sn_r.at[c, which, end]).wait()

    def sum_z(self, c, which, store):
        rt, ro = self.rt, self.roles(c)
        k = self.slot(ro.ax, ro.ay, rt.z) if which else self.slot(rt.x, rt.y, rt.z)

        @when(rt.z == 0)
        def _():
            store(k, add_f32(self.own(c, k)[...], self.rn(c, which, 0)[...]))

        @when(rt.z == 3)
        def _():
            store(k, add_f32(self.own(c, k)[...], self.ru(c, which, 2)[...]))

        for at in (1, 2):

            @when(rt.z == at)
            def _():
                store(k, add_f32(self.own(c, k)[...], self.ru(c, which, at - 1)[...]) + self.rn(c, which, at)[...].astype(F32))

    def close_a(self, c):
        ro = self.roles(c)

        def store(k, value):
            at = self.own(c, k)
            at[...] = value.astype(at.dtype)

        self.sum_z(c, 1, store)
        k = self.slot(ro.ax, ro.ay, self.rt.z)
        remote(self.own(c, k), self.ra(c, 0), self.sa_s.at[c], self.sa_r.at[c], ro.a).start()

    def total(self, c, from_a):
        def store(k, value):
            if from_a:
                bytes_of(self.ra(c, 0), self.sa_r.at[c]).wait()
                value = value + self.ra(c, 0)[...].astype(F32)
            self.out[c] = value

        self.sum_z(c, 0, store)

    def stage(self, s, c):
        mixed = self.plan.mixed(c)
        if s == 0:
            self.to_b(c)
        if s == 2:
            self.from_b(c)

        if s >= 2:

            @when(mixed)
            def _():
                if s == 2:
                    self.keep_b(c)
                if s <= 5:
                    self.along_z(c, s - 2, 1)
                    self.along_z(c, s - 2, 0)
                if s == 5:
                    self.close_a(c)
                if s == 6:
                    self.total(c, True)

            @when(~mixed)
            def _():
                if s == 2:
                    self.to_a(c)
                if s == 3:
                    self.from_a(c)
                if s >= 3:
                    self.along_z(c, s - 3, 0)
                if s == 6:
                    self.total(c, False)

    def finish(self, c):
        rt = self.rt
        bytes_of(self.rb.at[c], self.sb_s.at[c]).wait()

        def sent(which):
            for d in range(4):

                @when(rt.z != d)
                def _():
                    bytes_of(self.ra(c, 0), self.sz_s.at[c, which, d]).wait()

        sent(0)

        @when(self.plan.mixed(c))
        def _():
            sent(1)
            bytes_of(self.ra(c, 0), self.sa_s.at[c]).wait()

        @when(~self.plan.mixed(c))
        def _():
            bytes_of(self.rb.at[c, pl.ds(0, 4)], self.sa_s.at[c]).wait()


def reducer_sems(count):
    dma = pltpu.SemaphoreType.DMA
    return [dma((count,))] * 4 + [dma((count, 2, 4)), dma((count, 2, 3)), dma((count, 2, 3))]


class Shared:
    def __init__(self, route, ref, sems, at, start=0):
        cols = pl.ds(start, 1024)
        self.rt, self.mine, self.other = route, ref.at[pl.ds(0, 128), cols], ref.at[pl.ds(128, 128), cols]
        self.send, self.recv = sems.at[0, at], sems.at[1, at]

    def give(self):
        remote(self.mine, self.other, self.send, self.recv, self.rt.sibling).start()

    def wait(self):
        bytes_of(self.mine, self.recv).wait()

    def sent(self):
        bytes_of(self.mine, self.send).wait()


OFFSETS = (0, 0, 2, 3, 4, 5, 6)


def layer_kernel(x_ref, cot_ref, v_ref, len_ref, wq, wk, wv, wo, wu, wd,
                 kept, hid, gin, sums, small_out,
                 w, own, tiles, qkv, oh, kseq, qh, kh, vh, doh, lse, pre, nor1, inv1, gtwo, dk, dv, table, rows2,
                 x2, att2, mid2, act2, gffn2, gpre2, gbr2, dq2, dk2, dv2,
                 rb, ra, ru, rn, v_own, v_rb, v_ra, v_ru, v_rn, v_out,
                 own_sems, kept_sems, swap_sems, shared_sems, row_sems, *sems):
    rt, swap = Route(), Swap()
    shift = 7 + swap.bucket
    g_sems, gv_sems, r_sems, rv_sems = sems[:7], sems[7:14], sems[14:21], sems[21:28]
    loads = [pltpu.make_async_copy(ref, own.at[pl.ds(i * ROWS, ROWS)], own_sems.at[i]) for i, ref in enumerate((wq, wk, wv, wo))]
    loads.append(pltpu.make_async_copy(wd, own.at[pl.ds(4 * ROWS, 4 * ROWS)], own_sems.at[4]))
    for i in range(4):
        loads.append(pltpu.make_async_copy(wu.at[:, pl.ds(i * 1024, 1024)], own.at[pl.ds((8 + i) * ROWS, ROWS)], own_sems.at[5 + i]))
    loads.append(pltpu.make_async_copy(x_ref, x2.at[pl.ds(0, 128)], own_sems.at[9]))
    for load in loads:
        load.start()
    gather = Gatherer(
        rt, GATHER,
        lambda c: own.at[pl.ds(pl.multiple_of(c * ROWS, ROWS), ROWS)],
        lambda c, j: w.at[pl.ds(piece_row(c, j), ROWS)],
        lambda n: w.at[pl.ds(0, n * ROWS)],
        g_sems,
    )
    gather_small = Gatherer(rt, ONE_PIECE, lambda c: v_ref, lambda c, j: tiles.at[j], lambda n: tiles.at[pl.ds(0, n)], gv_sems)

    def own_block(c, k):
        first = jnp.where(c < 6, c * 512, W_DOWN + (c - 6) * 512)
        return w.at[pl.ds(pl.multiple_of(first + k * ROWS, ROWS), ROWS)]

    def third(c):
        return c // 3, c % 3

    def ra_block(c, i):
        n, m = third(c)
        return ra.at[n * 6 + m + i]

    def z_block(ref):
        def place_of(c, which, d):
            n, m = third(c)
            return ref.at[n * 15 + m * 6 + which * 3 + d]

        return place_of

    reduce = Reducer(rt, REDUCE, own_block, rb, ra_block, z_block(ru), z_block(rn), sums, r_sems)
    reduce_small = Reducer(
        rt, ONE_PIECE, lambda c, k: v_own.at[k], v_rb, lambda c, i: v_ra.at[i],
        lambda c, which, d: v_ru.at[d], lambda c, which, d: v_rn.at[d], v_out, rv_sems,
    )
    sx, satt, smid, sgffn, sgbr, sdq, sdk, sdv = (
        Shared(rt, ref, shared_sems, i) for i, ref in enumerate((x2, att2, mid2, gffn2, gbr2, dq2, dk2, dv2))
    )
    sact = [Shared(rt, act2, shared_sems, 8 + i, i * 1024) for i in range(4)]
    sgpre = [Shared(rt, gpre2, shared_sems, 12 + i, i * 1024) for i in range(4)]
    for load in loads:
        load.wait()
    rt.greet()

    def vec(row):
        return table[row:row + 1]

    def trio(at):
        return tuple(swap_sems.at[3 * at + n] for n in range(3))

    def project(i):
        value = dense(x2[0:128], w[i * 1024:(i + 1) * 1024])
        if i != 1:
            value = value + vec(V_QUERY if i == 0 else V_VALUE)
        qkv[i] = value.astype(BF16)
        swap.heads_out(qkv.at[i], (qh, kh, vh)[i], *trio(i))

    def start():
        gather_small.arrived(0)
        sx.give()
        table[...] = table_of(tiles)
        for i in range(4):
            table[V_UP + i:V_UP + i + 1] = jnp.concatenate([tiles[8 * i + j][8:9].astype(F32) for j in range(8)], axis=1)
        kseq[...] = key_sequences(len_ref, shift, kseq.shape[0])
        project(0)

    def score(first):
        if first == 0:
            for i, ref in enumerate((qh, kh, vh)):
                swap.wait(ref, *trio(i))

        def block(i, _):
            attend_block(i, shift, kseq, qh, kh, vh, oh, lse)
            return 0

        lax.fori_loop(first, first + 2, block, 0)
        if first == 2:
            swap.heads_back(oh, att2.at[pl.ds(0, 128)], *trio(3))

    def first_norm():
        swap.wait(oh, *trio(3))
        satt.give()
        normed, inv = norm_parts(x2[0:128].astype(F32) + (dense(att2[0:128], w[3072:4096]) + vec(V_OUT)))
        nor1[...] = normed
        inv1[...] = inv
        mid2[0:128] = (normed * vec(V_GAIN1) + vec(V_SHIFT1)).astype(BF16)
        smid.give()
        gtwo[...] = jnp.zeros_like(gtwo)

    def up(i):
        value = dense(mid2[0:128], w[W_UP + i * 1024:W_UP + (i + 1) * 1024]) + vec(V_UP + i)
        pre[i] = value
        now = gelu_value(value).astype(BF16)
        act2[0:128, i * 1024:(i + 1) * 1024] = now
        sact[i].give()
        gtwo[...] += dense(now, w[W_DOWN + i * 1024:W_DOWN + (i + 1) * 1024])

    items = {
        7: start, 8: lambda: project(1), 9: lambda: project(2), 10: lambda: score(0), 11: lambda: score(2), 13: first_norm,
        15: lambda: up(0), 16: lambda: up(1), 17: lambda: up(2), 18: lambda: up(3),
    }

    def save(i):
        rows_of = pl.ds(pl.multiple_of(i * 1024, 1024), 1024)
        return pltpu.make_async_copy(w.at[rows_of], kept.at[rows_of], kept_sems.at[i])

    def gather_step(t, _):
        for s in range(Gatherer.stages):
            c = t - s

            @when(c == 0)
            def _():
                gather_small.stage(s, 0)

            @when((c >= 0) & (c < PIECES))
            def _():
                gather.stage(s, c)

        c = t - Gatherer.stages

        @when(c >= 0)
        def _():
            gather.arrived(c)

            @when(c < 3)
            def _():
                save(c).start()

        for k, item in items.items():

            @when(t == k)
            def _():
                item()

        return 0

    lax.fori_loop(0, PIECES + Gatherer.stages, gather_step, 0)
    middle = nor1[...] * vec(V_GAIN1) + vec(V_SHIFT1)
    normed2, inv2 = norm_parts(middle + (gtwo[...] + vec(V_DOWN)))
    g = cot_ref[...].astype(F32)
    back = norm_back(g, normed2, inv2, vec(V_GAIN2))
    low = back.astype(BF16)
    gffn2[0:128] = low
    sgffn.give()
    gtwo[...] = back
    hid[...] = (normed2 * vec(V_GAIN2) + vec(V_SHIFT2)).astype(BF16)
    rows2[0] = jnp.zeros(table.shape, F32)
    rows2[0, V_GAIN2:V_GAIN2 + 1] = column_sum(g * normed2)
    rows2[0, V_SHIFT2:V_SHIFT2 + 1] = column_sum(g)
    rows2[0, V_DOWN:V_DOWN + 1] = column_sum(low.astype(F32))
    gather_small.finish()
    gather_small.finish_z(0)

    def gathered(c, _):
        gather.finish_z(c)
        return 0

    lax.fori_loop(0, PIECES, gathered, 0)
    gather.finish()
    for i in range(3):
        save(i).wait()

    def tall(first):
        order = [(k, at) for k, at in reduce.b_blocks(first)]
        kept_here = []
        for same_a in (0, 1):
            for zz in range(4):
                ro = reduce.roles(first)
                xx, yy = (rt.x, rt.y) if same_a else (ro.ax, ro.ay)
                kept_here.append(reduce.slot(xx, yy, zz))

        def block(k):
            j = (k // 8) * 16 + rt.core * 8 + k % 8
            part = act2[:, pl.ds(pl.multiple_of(j * 128, 128), 128)]
            grad = outer(part, gffn2[...]).astype(BF16)
            for q in range(4):
                own_block(first + q, k)[...] = grad[q * ROWS:(q + 1) * ROWS]

        for k, at in order:
            block(k)
            for q in range(4):
                reduce.send_b(first + q, k, at)
        for k in kept_here:
            block(k)

    def square(left, right, c):
        for xx in range(2):
            part = left[:, pl.ds(pl.multiple_of((xx * 2 + rt.core) * 256, 256), 256)]
            grad = outer(part, right).astype(BF16)
            for i in range(8):
                own_block(c, xx * 8 + i)[...] = grad[i * ROWS:(i + 1) * ROWS]

    def compute(c):
        @when(c == 0)
        def _():
            for one in sact + [sgffn]:
                one.wait()
            tall(0)

        for i in range(4):

            @when(c == 4 + i)
            def _():
                if i == 0:
                    smid.wait()
                sgpre[i].wait()

        @when((c >= 4) & (c < 8))
        def _():
            square(mid2, gpre2[:, pl.ds(pl.multiple_of((c - 4) * 1024, 1024), 1024)], c)

        for k, (left, right, lw, rw) in enumerate(
            ((att2, gbr2, satt, sgbr), (x2, dq2, sx, sdq), (x2, dk2, None, sdk), (x2, dv2, None, sdv))
        ):

            @when(c == 8 + k)
            def _():
                if lw is not None:
                    lw.wait()
                rw.wait()
                square(left, right[...], c)

        @when(c >= 4)
        def _():
            reduce.to_b(c)

    def share_rows():
        return remote(rows2.at[0], rows2.at[1], row_sems.at[0], row_sems.at[1], rt.sibling)

    def compute_small():
        bytes_of(rows2.at[1], row_sems.at[1]).wait()
        rows2[0] = rows2[0] + rows2[1]

        def one(i, _):
            j = (i // 8) * 16 + rt.core * 8 + i % 8
            v_own[i, 0:8] = rows2[0, 0:8, pl.ds(pl.multiple_of((j // 4) * 128, 128), 128)]
            ups = rows2[0, 8:16, pl.ds(pl.multiple_of((j % 8) * 128, 128), 128)]
            row = lax.broadcasted_iota(jnp.int32, (8, 128), 0)
            v_own[i, 8:16] = jnp.where(row == j // 8, ups, 0.0)
            return 0

        lax.fori_loop(0, 16, one, 0)

    def ffn_back(i):
        gact = inner(gffn2[0:128], w[W_DOWN + i * 1024:W_DOWN + (i + 1) * 1024]).astype(BF16).astype(F32)
        gpre = (gact * gelu_slope(pre[i])).astype(BF16)
        gpre2[0:128, i * 1024:(i + 1) * 1024] = gpre
        sgpre[i].give()
        rows2[0, V_UP + i:V_UP + i + 1] = column_sum(gpre.astype(F32))
        part = inner(gpre, w[W_UP + i * 1024:W_UP + (i + 1) * 1024])
        if i == 0:
            gin[...] = part
        else:
            gin[...] += part

    def load(i):
        return pltpu.make_async_copy(kept.at[pl.ds(i * 1024, 1024)], w.at[pl.ds(W_UP + i * 1024, 1024)], kept_sems.at[i])

    def ffn_end():
        for i in range(3):
            load(i).start()
        gmid = gtwo[...] + gin[...].astype(BF16).astype(F32)
        normed1 = nor1[...]
        gone = norm_back(gmid, normed1, inv1[...], vec(V_GAIN1))
        gbr = gone.astype(BF16)
        gbr2[0:128] = gbr
        qkv[0] = inner(gbr, w[3072:4096]).astype(BF16)
        swap.heads_out(qkv.at[0], doh, *trio(4))
        gin[...] = gone
        sgbr.give()
        rows2[0, V_GAIN1:V_GAIN1 + 1] = column_sum(gmid * normed1)
        rows2[0, V_SHIFT1:V_SHIFT1 + 1] = column_sum(gmid)
        rows2[0, V_OUT:V_OUT + 1] = column_sum(gbr.astype(F32))
        dk[...] = jnp.zeros_like(dk)
        dv[...] = jnp.zeros_like(dv)

    def score_back(first, count):
        if first == 0:
            swap.wait(doh, *trio(4))

        def block(i, _):
            attend_back_block(i, shift, kseq, qh, kh, vh, doh, lse, qh, dk, dv)
            return 0

        lax.fori_loop(first, first + count, block, 0)

    back_trio = ((qh, dq2, sdq), (kh, dk2, sdk), (vh, dv2, sdv))

    def score_end():
        kh[...] = dk[...].astype(BF16)
        vh[...] = dv[...].astype(BF16)
        for i, (src, dst, _) in enumerate(back_trio):
            swap.heads_back(src, dst.at[pl.ds(0, 128)], *trio(5 + i))

    def exchange():
        for i, (src, dst, shared) in enumerate(back_trio):
            swap.wait(src, *trio(5 + i))
            shared.give()
        rows2[0, V_QUERY:V_QUERY + 1] = column_sum(dq2[0:128].astype(F32))
        rows2[0, V_VALUE:V_VALUE + 1] = column_sum(dv2[0:128].astype(F32))
        share_rows().start()

    def input_grad():
        total = gin[...]
        for i, ref in enumerate((dq2, dk2, dv2)):
            load(i).wait()
            total = total + inner(ref[0:128], w[W_UP + i * 1024:W_UP + (i + 1) * 1024])
        gin[...] = total
        share_rows().wait_send()

    back_items = {
        0: (lambda: ffn_back(1),),
        1: (lambda: ffn_back(2), lambda: ffn_back(3), ffn_end),
        2: (lambda: score_back(0, 1),), 3: (lambda: score_back(1, 1),), 4: (lambda: score_back(2, 1),),
        5: (lambda: score_back(3, 1), score_end),
        7: (exchange,), 8: (input_grad,),
    }
    ffn_back(0)

    def reduce_step(t, _):
        @when(t < PIECES)
        def _():
            compute(t)

        @when(t == PIECES)
        def _():
            compute_small()
            reduce_small.to_b(0)

        for s in range(Reducer.stages - 1, 1, -1):
            c = t - OFFSETS[s]

            @when((c >= 0) & (c < PIECES))
            def _():
                reduce.stage(s, c)

            @when(c == PIECES)
            def _():
                reduce_small.stage(s, 0)

        for k, parts in back_items.items():

            @when(t == k)
            def _():
                for part in parts:
                    part()

        return 0

    lax.fori_loop(0, PIECES + 1 + OFFSETS[-1], reduce_step, 0)

    def reduced(c, _):
        reduce.finish(c)
        return 0

    lax.fori_loop(0, PIECES, reduced, 0)
    reduce_small.finish(0)
    for one in [sx, satt, smid, sgffn, sgbr, sdq, sdk, sdv] + sact + sgpre:
        one.sent()
    mine = v_out[0]
    quarter = owner(rt.x, rt.y, rt.z, rt.core) % 4
    picked = jnp.zeros((16, 32), F32)
    for q in range(4):
        picked = jnp.where(quarter == q, mine[:, q * 32:(q + 1) * 32], picked)
    small_out[:, 0:128] = jnp.broadcast_to(column_sum(mine[8:16]), (16, 128))
    small_out[:, 128:160] = picked


def shaped(shape, dtype):
    return jax.ShapeDtypeStruct(shape, dtype)


def layer(tokens, cotangent, small, lens, weights):
    vmem, anywhere = pl.BlockSpec(memory_space=pltpu.VMEM), pl.BlockSpec(memory_space=pl.ANY)
    dma = pltpu.SemaphoreType.DMA
    narrow, heads = (128, 1024), (1024, 128)
    half, full = pltpu.VMEM(heads, BF16), pltpu.VMEM(heads, F32)
    pair, wide_pair, tokens_f32 = pltpu.VMEM((256, 1024), BF16), pltpu.VMEM((256, 4096), BF16), pltpu.VMEM(narrow, F32)

    def blocks(*n):
        return pltpu.VMEM(n + (ROWS, 1024), BF16)

    def tiles(*n):
        return pltpu.VMEM(n + (16, 128), F32)

    return pl.pallas_call(
        layer_kernel,
        out_shape=(
            shaped((3 * 1024, 1024), BF16), shaped(narrow, BF16), shaped(narrow, F32),
            shaped((PIECES, ROWS, 1024), F32), shaped((16, 256), F32),
        ),
        in_specs=[anywhere, vmem, vmem, pl.BlockSpec(memory_space=pltpu.SMEM)] + [anywhere] * 6,
        out_specs=(anywhere,) + (vmem,) * 4,
        scratch_shapes=[
            pltpu.VMEM((PIECES * 1024, 1024), BF16), pltpu.VMEM((PIECES * ROWS, 1024), BF16), pltpu.VMEM((32, 16, 128), BF16),
            pltpu.VMEM((3, 128, 1024), BF16), half, pltpu.VMEM(heads, jnp.int32), half, half, half, half,
            pltpu.VMEM((2, 1024), F32), pltpu.VMEM((4, 128, 1024), F32), tokens_f32, pltpu.VMEM((128, 1), F32), tokens_f32,
            full, full, pltpu.VMEM((16, 1024), F32), pltpu.VMEM((2, 16, 1024), F32),
            pair, pair, pair, wide_pair, pair, wide_pair, pair, pair, pair, pair,
            blocks(PIECES, 8), blocks(24), blocks(60), blocks(60),
            tiles(16), tiles(1, 8), tiles(4), tiles(3), tiles(3), tiles(1),
            dma((10,)), dma((3,)), dma((24,)), dma((2, 16)), dma((2,)),
        ] + gather_sems(PIECES) + gather_sems(1) + reducer_sems(PIECES) + reducer_sems(1),
        compiler_params=pltpu.CompilerParams(collective_id=0, has_side_effects=True, vmem_limit_bytes=VMEM_LIMIT),
    )(tokens, cotangent, small, lens, *weights)


def unpack_kernel(sums, small, hid, gin, *outs):
    (o_hid, o_gin, o_q, o_k, o_v, o_bq, o_bv, o_o, o_bo, o_g1, o_s1, o_up, o_bup, o_down, o_bdown, o_g2, o_s2) = outs
    o_hid[...] = hid[...]
    o_gin[...] = gin[...]
    for ref, c in ((o_q, 9), (o_k, 10), (o_v, 11), (o_o, 8)):
        ref[...] = sums[c]
    for i in range(4):
        o_down[i * ROWS:(i + 1) * ROWS] = sums[i]
        o_up[:, i * 1024:(i + 1) * 1024] = sums[4 + i]
    for i, ref in enumerate((o_bq, o_bv, o_bo, o_g1, o_s1, o_bdown, o_g2, o_s2)):
        ref[...] = small[i, 128:160]
    o_bup[...] = small[8, 0:128]


def unpack(sums, small, hid, gin):
    vmem = pl.BlockSpec(memory_space=pltpu.VMEM)
    block, vector = shaped((ROWS, 1024), F32), shaped((32,), F32)
    return pl.pallas_call(
        unpack_kernel,
        out_shape=(
            shaped(hid.shape, BF16), shaped(gin.shape, F32), block, block, block, vector, vector, block, vector, vector, vector,
            shaped((ROWS, 4096), F32), shaped((128,), F32), shaped((128, 1024), F32), vector, vector, vector,
        ),
        in_specs=[vmem] * 4,
        out_specs=(vmem,) * 17,
        compiler_params=pltpu.CompilerParams(vmem_limit_bytes=VMEM_LIMIT),
    )(sums, small, hid, gin)


def fast_body(hidden_in, lengths, w_query, w_key, w_value, b_query, b_value, w_out, b_out, first_gain, first_shift,
              w_up, b_up, w_down, b_down, second_gain, second_shift, cotangent):
    tokens = hidden_in.reshape(128, 1024)
    me = lax.axis_index("bucket") * 8 + lax.axis_index("ctx")
    rows = jnp.stack([b_query, b_value, b_out, first_gain, first_shift, b_down, second_gain, second_shift])
    spread = jnp.concatenate([jnp.where(me % 4 == q, rows, jnp.zeros_like(rows)) for q in range(4)], axis=1)
    small = jnp.concatenate([spread, b_up[None], jnp.zeros((7, 128), BF16)], axis=0)
    _, hidden_out, grad_in, sums, small_sums = layer(
        tokens, cotangent.reshape(128, 1024), small, lengths.reshape(8), (w_query, w_key, w_value, w_out, w_up, w_down)
    )
    outs = unpack(sums, small_sums, hidden_out, grad_in)
    return (outs[0].reshape(hidden_in.shape), outs[1].reshape(hidden_in.shape)) + tuple(outs[2:])


def matmul(left, right):
    return jnp.dot(left, right, preferred_element_type=jnp.float32)


def row_inner(left, right):
    return lax.dot_general(
        left, right, (((0,), (0,)), ((), ())), preferred_element_type=jnp.float32
    )


def right_inner(left, right):
    return lax.dot_general(
        left, right, (((1,), (1,)), ((), ())), preferred_element_type=jnp.float32
    )


def rounded(values):
    return values.astype(jnp.bfloat16)


def widened(values):
    return values.astype(jnp.float32)


def norm_forward(summed, gain_vec, shift_vec):
    average = jnp.mean(summed, axis=-1, keepdims=True)
    centred = summed - average
    variance = jnp.mean(centred * centred, axis=-1, keepdims=True)
    inv_std = lax.rsqrt(variance + EPSILON)
    normed = centred * inv_std
    return (normed * gain_vec + shift_vec, normed, inv_std)


def norm_backward(incoming, normed, inv_std, gain_vec):
    scaled = incoming * gain_vec
    inner = (
        scaled
        - jnp.mean(scaled, axis=-1, keepdims=True)
        - normed * jnp.mean(scaled * normed, axis=-1, keepdims=True)
    )
    return (inv_std * inner, jnp.sum(incoming * normed, axis=0), jnp.sum(incoming, axis=0))


def plain_gelu_value(values):
    return 0.5 * values * (1.0 + jax.scipy.special.erf(values * 0.7071067811865476))


def plain_gelu_slope(values):
    return (
        0.5 * (1.0 + jax.scipy.special.erf(values * 0.7071067811865476))
        + values * jnp.exp(-0.5 * values * values) * 0.3989422804014327
    )


def split_heads(values):
    return values.reshape(values.shape[0], values.shape[1], values.shape[2] // HEAD_DIM, HEAD_DIM)


def seq_mask(seq_info, query_pos, key_pos):
    seq_lens, slot_len = seq_info
    query_seq = query_pos // slot_len
    key_seq = key_pos // slot_len
    seq_ids = jnp.arange(seq_lens.shape[1], dtype=jnp.int32)
    picked = (key_seq[:, None] == seq_ids[None, :]).astype(jnp.int32)
    key_limit = jnp.sum(picked[None, :, :] * seq_lens[:, None, :], axis=-1)
    key_valid = (key_pos - key_seq * slot_len)[None, :] < key_limit
    same_seq = query_seq[:, None] == key_seq[None, :]
    return (same_seq[None, :, :] & key_valid[:, None, :])[:, None, :, :]


def score_block(query4, key4, query_start, key_start, seq_info):
    raw = jnp.einsum(
        "sqhd,skhd->shqk", query4, key4, preferred_element_type=jnp.float32
    ) * HEAD_DIM ** (-0.5)
    query_pos = query_start + jnp.arange(query4.shape[1], dtype=jnp.int32)
    key_pos = key_start + jnp.arange(key4.shape[1], dtype=jnp.int32)
    allowed = seq_mask(seq_info, query_pos, key_pos)
    return (jnp.where(allowed, raw, NEG_FILL), allowed)


def over_blocks(block_step, running, pieces):
    length_here = pieces[0].shape[1]
    block_len = math.gcd(length_here, 512)
    turn_count = length_here // block_len

    def advance(turn_no, current):
        offset = turn_no * block_len
        sliced = tuple(
            (lax.dynamic_slice_in_dim(piece_arr, offset, block_len, 1) for piece_arr in pieces)
        )
        return block_step(current, sliced, offset)

    return lax.fori_loop(0, turn_count, advance, running)


def general_body(
    hidden_in,
    lengths,
    w_query,
    w_key,
    w_value,
    b_query,
    b_value,
    w_out,
    b_out,
    first_gain,
    first_shift,
    w_up,
    b_up,
    w_down,
    b_down,
    second_gain,
    second_shift,
    cotangent,
):
    shards = (
        w_query,
        w_key,
        w_value,
        b_query,
        b_value,
        w_out,
        b_out,
        first_gain,
        first_shift,
        w_up,
        b_up,
        w_down,
        b_down,
        second_gain,
        second_shift,
    )
    gathered = (
        lax.all_gather(shards[0], ("bucket", "ctx"), axis=0, tiled=True),
        lax.all_gather(shards[1], ("bucket", "ctx"), axis=0, tiled=True),
        lax.all_gather(shards[2], ("bucket", "ctx"), axis=0, tiled=True),
        lax.all_gather(shards[3], ("bucket", "ctx"), axis=0, tiled=True),
        lax.all_gather(shards[4], ("bucket", "ctx"), axis=0, tiled=True),
        lax.all_gather(shards[5], ("bucket", "ctx"), axis=0, tiled=True),
        lax.all_gather(shards[6], ("bucket", "ctx"), axis=0, tiled=True),
        lax.all_gather(shards[7], ("bucket", "ctx"), axis=0, tiled=True),
        lax.all_gather(shards[8], ("bucket", "ctx"), axis=0, tiled=True),
        lax.all_gather(shards[9], ("bucket", "ctx"), axis=0, tiled=True),
        lax.all_gather(shards[10], ("bucket", "ctx"), axis=0, tiled=True),
        lax.all_gather(shards[11], ("bucket", "ctx"), axis=0, tiled=True),
        lax.all_gather(shards[12], ("bucket", "ctx"), axis=0, tiled=True),
        lax.all_gather(shards[13], ("bucket", "ctx"), axis=0, tiled=True),
        lax.all_gather(shards[14], ("bucket", "ctx"), axis=0, tiled=True),
    )
    (
        query_mat,
        key_mat,
        value_mat,
        query_bias,
        value_bias,
        out_mat,
        out_bias,
        gain_one,
        shift_one,
        up_mat,
        up_bias,
        down_mat,
        down_bias,
        gain_two,
        shift_two,
    ) = gathered
    seq_count = hidden_in.shape[1]
    local_rows = hidden_in.shape[2]
    model_width = hidden_in.shape[3]
    head_count = model_width // HEAD_DIM
    total_rows = seq_count * local_rows
    block_shape = (seq_count, local_rows, model_width)
    score_scale = HEAD_DIM ** (-0.5)
    seq_total = local_rows * lax.axis_size("ctx")
    group_index = lax.axis_index("bucket")
    seq_slots = jnp.right_shift(jnp.int32(lengths.shape[2]), group_index)
    slot_len = jnp.int32(seq_total) // seq_slots
    seq_info = (lengths[0], slot_len)
    own_start = lax.axis_index("ctx") * local_rows
    tokens = hidden_in.reshape(total_rows, model_width)
    query_low = rounded(matmul(tokens, query_mat) + widened(query_bias))
    key_low = rounded(matmul(tokens, key_mat))
    value_low = rounded(matmul(tokens, value_mat) + widened(value_bias))
    query_heads = split_heads(query_low.reshape(block_shape))
    key_rows = key_low.reshape(block_shape)
    value_rows = value_low.reshape(block_shape)

    def stats_step(running, sliced, anchor):
        scores, allowed = score_block(
            query_heads, split_heads(sliced[0]), own_start, anchor, seq_info
        )
        run_max, run_total = running
        new_max = jnp.maximum(run_max, jnp.max(scores, axis=-1))
        raised = jnp.where(allowed, jnp.exp(scores - new_max[..., None]), 0.0)
        return (new_max, run_total * jnp.exp(run_max - new_max) + jnp.sum(raised, axis=-1))

    stat_shape = (seq_count, head_count, local_rows)
    stats_start = (jnp.full(stat_shape, NEG_FILL, jnp.float32), jnp.zeros(stat_shape, jnp.float32))
    run_max, run_total = over_blocks(
        stats_step, stats_start, (lax.all_gather(key_rows, "ctx", axis=1, tiled=True),)
    )
    log_total = run_max + jnp.log(run_total)

    def output_step(running, sliced, anchor):
        key4 = split_heads(sliced[0])
        value4 = split_heads(sliced[1])
        scores, allowed = score_block(query_heads, key4, own_start, anchor, seq_info)
        probs_low = rounded(jnp.where(allowed, jnp.exp(scores - log_total[..., None]), 0.0))
        return running + jnp.einsum(
            "shqk,skhd->sqhd", probs_low, value4, preferred_element_type=jnp.float32
        )

    attended_f32 = over_blocks(
        output_step,
        jnp.zeros(query_heads.shape, jnp.float32),
        (
            lax.all_gather(key_rows, "ctx", axis=1, tiled=True),
            lax.all_gather(value_rows, "ctx", axis=1, tiled=True),
        ),
    )
    attended_low = rounded(attended_f32.reshape(total_rows, model_width))
    branch = matmul(attended_low, out_mat) + widened(out_bias)
    middle, normed_one, inv_one = norm_forward(
        widened(tokens) + branch, widened(gain_one), widened(shift_one)
    )
    middle_low = rounded(middle)
    pre_act = matmul(middle_low, up_mat) + widened(up_bias)
    activated = rounded(plain_gelu_value(pre_act))
    ffn_out = matmul(activated, down_mat) + widened(down_bias)
    result, normed_two, inv_two = norm_forward(
        middle + ffn_out, widened(gain_two), widened(shift_two)
    )
    hidden_out = rounded(result).reshape(hidden_in.shape)
    gathered = (
        lax.all_gather(shards[0], ("bucket", "ctx"), axis=0, tiled=True),
        lax.all_gather(shards[1], ("bucket", "ctx"), axis=0, tiled=True),
        lax.all_gather(shards[2], ("bucket", "ctx"), axis=0, tiled=True),
        lax.all_gather(shards[3], ("bucket", "ctx"), axis=0, tiled=True),
        lax.all_gather(shards[4], ("bucket", "ctx"), axis=0, tiled=True),
        lax.all_gather(shards[5], ("bucket", "ctx"), axis=0, tiled=True),
        lax.all_gather(shards[6], ("bucket", "ctx"), axis=0, tiled=True),
        lax.all_gather(shards[7], ("bucket", "ctx"), axis=0, tiled=True),
        lax.all_gather(shards[8], ("bucket", "ctx"), axis=0, tiled=True),
        lax.all_gather(shards[9], ("bucket", "ctx"), axis=0, tiled=True),
        lax.all_gather(shards[10], ("bucket", "ctx"), axis=0, tiled=True),
        lax.all_gather(shards[11], ("bucket", "ctx"), axis=0, tiled=True),
        lax.all_gather(shards[12], ("bucket", "ctx"), axis=0, tiled=True),
        lax.all_gather(shards[13], ("bucket", "ctx"), axis=0, tiled=True),
        lax.all_gather(shards[14], ("bucket", "ctx"), axis=0, tiled=True),
    )
    query_mat = gathered[0]
    key_mat = gathered[1]
    value_mat = gathered[2]
    out_mat = gathered[5]
    gain_one = gathered[7]
    up_mat = gathered[9]
    down_mat = gathered[11]
    gain_two = gathered[13]
    incoming = widened(cotangent.reshape(total_rows, model_width))
    grad_two_sum, grad_second_gain, grad_second_shift = norm_backward(
        incoming, normed_two, inv_two, widened(gain_two)
    )
    grad_ffn = rounded(grad_two_sum)
    grad_b_down = jnp.sum(widened(grad_ffn), axis=0)
    grad_w_down = row_inner(activated, grad_ffn)
    grad_act = widened(rounded(right_inner(grad_ffn, down_mat)))
    grad_pre = rounded(grad_act * plain_gelu_slope(pre_act))
    grad_b_up = jnp.sum(widened(grad_pre), axis=0)
    grad_w_up = row_inner(middle_low, grad_pre)
    grad_middle = grad_two_sum + widened(rounded(right_inner(grad_pre, up_mat)))
    grad_one_sum, grad_first_gain, grad_first_shift = norm_backward(
        grad_middle, normed_one, inv_one, widened(gain_one)
    )
    grad_branch = rounded(grad_one_sum)
    grad_b_out = jnp.sum(widened(grad_branch), axis=0)
    grad_w_out = row_inner(attended_low, grad_branch)
    grad_att = rounded(right_inner(grad_branch, out_mat)).reshape(block_shape)
    grad_att_heads = split_heads(grad_att)
    delta = jnp.einsum("sqhd,sqhd->shq", widened(grad_att_heads), attended_f32)

    def grad_terms(query4, key4, value4, att4, row_log, row_delta, query_start, key_start):
        scores, allowed = score_block(query4, key4, query_start, key_start, seq_info)
        probs = jnp.where(allowed, jnp.exp(scores - row_log[..., None]), 0.0)
        slope = jnp.einsum("sqhd,skhd->shqk", att4, value4, preferred_element_type=jnp.float32)
        return (rounded(probs), rounded(probs * (slope - row_delta[..., None])))

    def query_step(running, sliced, anchor):
        key4 = split_heads(sliced[0])
        value4 = split_heads(sliced[1])
        probs_low, score_grad = grad_terms(
            query_heads, key4, value4, grad_att_heads, log_total, delta, own_start, anchor
        )
        return (
            running
            + jnp.einsum("shqk,skhd->sqhd", score_grad, key4, preferred_element_type=jnp.float32)
            * score_scale
        )

    grad_q = over_blocks(
        query_step,
        jnp.zeros(query_heads.shape, jnp.float32),
        (
            lax.all_gather(key_rows, "ctx", axis=1, tiled=True),
            lax.all_gather(value_rows, "ctx", axis=1, tiled=True),
        ),
    )
    log_all, delta_all = (
        lax.all_gather(log_total, "ctx", axis=2, tiled=True),
        lax.all_gather(delta, "ctx", axis=2, tiled=True),
    )
    own_keys = split_heads(key_rows)
    own_values = split_heads(value_rows)

    def owner_step(running, sliced, anchor):
        query4 = split_heads(sliced[0])
        att4 = split_heads(sliced[1])
        count_here = sliced[0].shape[1]
        row_log = lax.dynamic_slice_in_dim(log_all, anchor, count_here, 2)
        row_delta = lax.dynamic_slice_in_dim(delta_all, anchor, count_here, 2)
        probs_low, score_grad = grad_terms(
            query4, own_keys, own_values, att4, row_log, row_delta, anchor, own_start
        )
        grad_k, grad_v = running
        grad_k = (
            grad_k
            + jnp.einsum("shqk,sqhd->skhd", score_grad, query4, preferred_element_type=jnp.float32)
            * score_scale
        )
        grad_v = grad_v + jnp.einsum(
            "shqk,sqhd->skhd", probs_low, att4, preferred_element_type=jnp.float32
        )
        return (grad_k, grad_v)

    owner_start = (jnp.zeros(own_keys.shape, jnp.float32), jnp.zeros(own_keys.shape, jnp.float32))
    grad_k_own, grad_v_own = over_blocks(
        owner_step,
        owner_start,
        (
            lax.all_gather(query_low.reshape(block_shape), "ctx", axis=1, tiled=True),
            lax.all_gather(grad_att, "ctx", axis=1, tiled=True),
        ),
    )
    grad_q_low = rounded(grad_q.reshape(total_rows, model_width))
    grad_k_low = rounded(grad_k_own.reshape(total_rows, model_width))
    grad_v_low = rounded(grad_v_own.reshape(total_rows, model_width))
    grad_w_query = row_inner(tokens, grad_q_low)
    grad_b_query = jnp.sum(widened(grad_q_low), axis=0)
    grad_w_key = row_inner(tokens, grad_k_low)
    grad_w_value = row_inner(tokens, grad_v_low)
    grad_b_value = jnp.sum(widened(grad_v_low), axis=0)
    grad_in = (
        grad_one_sum
        + right_inner(grad_q_low, query_mat)
        + right_inner(grad_k_low, key_mat)
        + right_inner(grad_v_low, value_mat)
    )
    owned = (
        lax.psum_scatter(grad_w_query, ("bucket", "ctx"), scatter_dimension=0, tiled=True),
        lax.psum_scatter(grad_w_key, ("bucket", "ctx"), scatter_dimension=0, tiled=True),
        lax.psum_scatter(grad_w_value, ("bucket", "ctx"), scatter_dimension=0, tiled=True),
        lax.psum_scatter(grad_b_query, ("bucket", "ctx"), scatter_dimension=0, tiled=True),
        lax.psum_scatter(grad_b_value, ("bucket", "ctx"), scatter_dimension=0, tiled=True),
        lax.psum_scatter(grad_w_out, ("bucket", "ctx"), scatter_dimension=0, tiled=True),
        lax.psum_scatter(grad_b_out, ("bucket", "ctx"), scatter_dimension=0, tiled=True),
        lax.psum_scatter(grad_first_gain, ("bucket", "ctx"), scatter_dimension=0, tiled=True),
        lax.psum_scatter(grad_first_shift, ("bucket", "ctx"), scatter_dimension=0, tiled=True),
        lax.psum_scatter(grad_w_up, ("bucket", "ctx"), scatter_dimension=0, tiled=True),
        lax.psum_scatter(grad_b_up, ("bucket", "ctx"), scatter_dimension=0, tiled=True),
        lax.psum_scatter(grad_w_down, ("bucket", "ctx"), scatter_dimension=0, tiled=True),
        lax.psum_scatter(grad_b_down, ("bucket", "ctx"), scatter_dimension=0, tiled=True),
        lax.psum_scatter(grad_second_gain, ("bucket", "ctx"), scatter_dimension=0, tiled=True),
        lax.psum_scatter(grad_second_shift, ("bucket", "ctx"), scatter_dimension=0, tiled=True),
    )
    return (hidden_out, grad_in.reshape(hidden_in.shape)) + tuple(owned)


def solution(mesh):
    placed = (
        P("bucket", None, "ctx", None),
        P("bucket", None, None),
        P(("bucket", "ctx"), None),
        P(("bucket", "ctx"), None),
        P(("bucket", "ctx"), None),
        P(("bucket", "ctx")),
        P(("bucket", "ctx")),
        P(("bucket", "ctx"), None),
        P(("bucket", "ctx")),
        P(("bucket", "ctx")),
        P(("bucket", "ctx")),
        P(("bucket", "ctx"), None),
        P(("bucket", "ctx")),
        P(("bucket", "ctx"), None),
        P(("bucket", "ctx")),
        P(("bucket", "ctx")),
        P(("bucket", "ctx")),
        P("bucket", None, "ctx", None),
    )
    def body(*arguments):
        here = dict(mesh.shape) == {"bucket": 4, "ctx": 8}
        shapes = arguments[0].shape == (1, 1, 128, 1024) and arguments[11].shape == (32, 4096)
        return (fast_body if here and shapes else general_body)(*arguments)

    return jax.shard_map(
        body,
        mesh=mesh,
        in_specs=placed,
        out_specs=(
            P("bucket", None, "ctx", None),
            P("bucket", None, "ctx", None),
            P(("bucket", "ctx"), None),
            P(("bucket", "ctx"), None),
            P(("bucket", "ctx"), None),
            P(("bucket", "ctx")),
            P(("bucket", "ctx")),
            P(("bucket", "ctx"), None),
            P(("bucket", "ctx")),
            P(("bucket", "ctx")),
            P(("bucket", "ctx")),
            P(("bucket", "ctx"), None),
            P(("bucket", "ctx")),
            P(("bucket", "ctx"), None),
            P(("bucket", "ctx")),
            P(("bucket", "ctx")),
            P(("bucket", "ctx")),
        ),
        check_vma=False,
    )
```

```python
import math

import jax
import jax.numpy as jnp
from jax import lax
from jax.experimental import pallas as pl
from jax.experimental.pallas import tpu as pltpu
from jax.sharding import PartitionSpec as P

HEAD_DIM = 64
EPSILON = 1e-05
NEG_FILL = -1e30
MESH_ID = pl.DeviceIdType.MESH
F32, BF16 = jnp.float32, jnp.bfloat16
ROWS = 32
PIECES = 12
VMEM_LIMIT = 63 * 2**20


def when(condition):
    return pl.when(condition)


def place():
    bucket, ctx = lax.axis_index("bucket"), lax.axis_index("ctx")
    return bucket // 2, ctx % 2, ctx // 2, bucket % 2


def device(x, y, z, core):
    return (x * 2 + core, z * 2 + y)


def owner(x, y, z, core):
    return (x * 2 + core) * 8 + z * 2 + y


def remote(src, dst, send_sem, recv_sem, target):
    return pltpu.make_async_remote_copy(
        src_ref=src, dst_ref=dst, send_sem=send_sem, recv_sem=recv_sem,
        device_id=target, device_id_type=MESH_ID,
    )


def bytes_of(ref, sem):
    return pltpu.make_async_copy(ref, ref, sem)


class Roles:
    def __init__(self, route, b_along_x):
        x, y, z, core = route.x, route.y, route.z, route.core
        self.ax, self.ay = jnp.where(b_along_x, x, 1 - x), jnp.where(b_along_x, 1 - y, y)
        self.bx, self.by = jnp.where(b_along_x, 1 - x, x), jnp.where(b_along_x, y, 1 - y)
        self.a = device(self.ax, self.ay, z, core)
        self.b = device(self.bx, self.by, z, core)


class Route:
    def __init__(self):
        self.x, self.y, self.z, self.core = x, y, z, core = place()
        self.across = (device(1 - x, y, z, core), device(x, 1 - y, z, core))
        self.sibling = device(x, y, z, 1 - core)
        self.up = device(x, y, jnp.minimum(z + 1, 3), core)
        self.down = device(x, y, jnp.maximum(z - 1, 0), core)

    def roles(self, turned):
        return Roles(self, (self.core == 1) | turned)

    def greet(self):
        z = self.z
        bucket, ctx = lax.axis_index("bucket"), lax.axis_index("ctx")
        barrier = pltpu.get_barrier_semaphore()
        pack = [(bucket, (ctx + off) % 8) for off in range(1, 8)]
        for target in [*self.across, self.sibling] + pack:
            pl.semaphore_signal(barrier, inc=1, device_id=target, device_id_type=MESH_ID)

        @when(z < 3)
        def _():
            pl.semaphore_signal(barrier, inc=1, device_id=self.up, device_id_type=MESH_ID)

        @when(z > 0)
        def _():
            pl.semaphore_signal(barrier, inc=1, device_id=self.down, device_id_type=MESH_ID)

        pl.semaphore_wait(barrier, 10 + (z < 3).astype(jnp.int32) + (z > 0).astype(jnp.int32))


class Plan:
    def __init__(self, count, mixed, turned):
        self.count, self.which_mixed, self.which_turned = count, mixed, turned

    def mixed(self, c):
        return self.member(c, self.which_mixed)

    def turned(self, c):
        return self.member(c, self.which_turned)

    def mixed_before(self, c):
        return sum((c > item).astype(jnp.int32) for item in self.which_mixed)

    @staticmethod
    def member(c, items):
        hit = jnp.bool_(False)
        for item in items:
            hit = hit | (c == item)
        return hit


class Gatherer:
    stages = 7

    def __init__(self, route, plan, own, block, span, sems):
        self.rt, self.plan, self.own, self.block, self.span = route, plan, own, block, span
        (self.zs, self.zr, self.ps, self.ar, self.br, self.dr, self.ls) = sems

    def spread(self, c, src, j, jz, ro, to_a, to_b, z_dirs):
        rt, dst = self.rt, self.block(c, j)
        which, directions = z_dirs
        if "line" in directions:
            for slot in range(3):
                target = device(rt.x, rt.y, (rt.z + slot + 1) % 4, rt.core)
                remote(src, dst, self.zs.at[0, c, which, slot], self.zr.at[c, which, jz], target).start()

        if "up" in directions:

            @when(rt.z < 3)
            def _():
                remote(src, dst, self.zs.at[0, c, which, jz], self.zr.at[c, which, jz], rt.up).start()

        if "down" in directions:

            @when(rt.z > 0)
            def _():
                remote(src, dst, self.zs.at[1, c, which, jz], self.zr.at[c, which, jz], rt.down).start()

        if to_b is not None:
            remote(src, dst, self.ps, self.br.at[c, to_b * 4 + jz], ro.b).start()
        if to_a is not None:

            @when(to_a)
            def _():
                remote(src, dst, self.ps, self.ar.at[c, jz], ro.a).start()

        remote(src, dst, self.ps, self.dr.at[c], rt.sibling).start()

    def near(self, k, action):
        for sign in (0,) if k == 0 else (-1, 1):
            zz = self.rt.z + sign * k

            @when((zz >= 0) & (zz <= 3))
            def _():
                action(zz, "up" if sign < 0 else "down")

    def own_stage(self, c):
        rt, ro = self.rt, self.rt.roles(self.plan.turned(c))
        j = owner(rt.x, rt.y, rt.z, rt.core)
        pltpu.make_async_copy(self.own(c), self.block(c, j), self.ls.at[c]).start()
        mixed = self.plan.mixed(c)

        @when(mixed)
        def _():
            self.spread(c, self.own(c), j, rt.z, ro, jnp.bool_(True), 0, (0, ("up", "down")))

        @when(~mixed)
        def _():
            self.spread(c, self.own(c), j, rt.z, ro, jnp.bool_(True), 0, (0, ("line",)))


    def z_stage(self, c, k):
        rt, ro = self.rt, self.rt.roles(self.plan.turned(c))

        def action(zz, direction):
            j = owner(rt.x, rt.y, zz, rt.core)
            bytes_of(self.block(c, j), self.zr.at[c, 0, zz]).wait()

            @when(self.plan.mixed(c))
            def _():
                self.spread(c, self.block(c, j), j, zz, ro, None, 0, (0, (direction,)))

            @when(~self.plan.mixed(c))
            def _():
                self.spread(c, self.block(c, j), j, zz, ro, jnp.bool_(True), 0, (0, ()))


        self.near(k, action)

    def z_stage_of_a(self, c, k):
        rt, ro = self.rt, self.rt.roles(self.plan.turned(c))

        def action(zz, direction):
            j = owner(ro.ax, ro.ay, zz, rt.core)
            bytes_of(self.block(c, j), self.zr.at[c, 1, zz]).wait()
            self.spread(c, self.block(c, j), j, zz, ro, None, 1, (1, (direction,)))

        self.near(k, action)

    def a_stage(self, c, k, directions=()):
        rt, ro = self.rt, self.rt.roles(self.plan.turned(c))

        def action(zz, _):
            j = owner(ro.ax, ro.ay, zz, rt.core)
            bytes_of(self.block(c, j), self.ar.at[c, zz]).wait()
            self.spread(c, self.block(c, j), j, zz, ro, None, 1, (1, directions))

        self.near(k, action)

    def b_stage(self, c, k):
        rt, ro = self.rt, self.rt.roles(self.plan.turned(c))

        def action(zz, _):
            for which, (xx, yy) in enumerate(((ro.bx, ro.by), (1 - rt.x, 1 - rt.y))):
                j = owner(xx, yy, zz, rt.core)
                bytes_of(self.block(c, j), self.br.at[c, which * 4 + zz]).wait()
                self.spread(c, self.block(c, j), j, zz, ro, None, None, (0, ()))

        self.near(k, action)

    def stage(self, s, c):
        mixed = self.plan.mixed(c)
        if s == 0:
            self.own_stage(c)
        if 1 <= s <= 3:
            self.z_stage(c, s)
        if s == 1:

            @when(mixed)
            def _():
                self.a_stage(c, 0, ("up", "down"))

            @when(~mixed)
            def _():
                self.a_stage(c, 0)

        if 2 <= s <= 4:

            @when(mixed)
            def _():
                self.z_stage_of_a(c, s - 1)

            @when(~mixed)
            def _():
                self.a_stage(c, s - 1)

        if 3 <= s <= 6:
            self.b_stage(c, s - 3)

    def arrived(self, c):
        bytes_of(self.span(16), self.dr.at[c]).wait()
        bytes_of(self.span(1), self.ls.at[c]).wait()

    def finish(self):
        bytes_of(self.span(28 * self.plan.count - 3 * len(self.plan.which_mixed)), self.ps).wait()

    def finish_z(self, c):
        rt = self.rt

        def sent(which):
            for zz in range(4):

                @when((rt.z < 3) & (rt.z >= zz))
                def _():
                    bytes_of(self.span(1), self.zs.at[0, c, which, zz]).wait()

                @when((rt.z > 0) & (rt.z <= zz))
                def _():
                    bytes_of(self.span(1), self.zs.at[1, c, which, zz]).wait()

        @when(self.plan.mixed(c))
        def _():
            sent(0)
            sent(1)

        @when(~self.plan.mixed(c))
        def _():
            for slot in range(3):
                bytes_of(self.span(1), self.zs.at[0, c, 0, slot]).wait()


def gather_sems(count):
    dma = pltpu.SemaphoreType.DMA
    return [dma((2, count, 2, 4)), dma((count, 2, 4)), dma(()), dma((count, 4)), dma((count, 8)), dma((count,)), dma((count,))]


def outer(left, right):
    return lax.dot_general(left, right, (((0,), (0,)), ((), ())), preferred_element_type=F32)


def inner(left, right):
    return lax.dot_general(left, right, (((1,), (1,)), ((), ())), preferred_element_type=F32)


def dense(left, right):
    return jnp.dot(left, right, preferred_element_type=F32)


def head_mask(shape, head):
    lane = lax.broadcasted_iota(jnp.int32, shape, len(shape) - 1)
    return (lane // HEAD_DIM) == head


def only_head(values, head):
    return jnp.where(head_mask(values.shape, head), values, jnp.zeros_like(values))


def key_sequences(len_ref, shift, keys):
    pos = lax.broadcasted_iota(jnp.int32, (keys, 128), 0)
    seq = lax.shift_right_logical(pos, shift)
    at = pos - lax.shift_left(seq, shift)
    limit = jnp.zeros((keys, 128), jnp.int32)
    for s in range(8):
        limit = jnp.where(seq == s, len_ref[s], limit)
    return jnp.where(at < limit, seq, -1)


def key_bias(kseq, shift, start, width):
    keys = kseq.shape[0]
    qseq = lax.shift_right_logical(start + lax.broadcasted_iota(jnp.int32, (1, 128), 1), shift)
    parts = []
    for w in range(width // 128):
        qs = lax.shift_right_logical(start + w * 128 + lax.broadcasted_iota(jnp.int32, (1, 128), 1), shift)
        parts.append(jnp.where(kseq == qs, 0.0, NEG_FILL))
    return jnp.concatenate(parts, axis=1)


class Swap:
    def __init__(self):
        self.bucket, self.me = lax.axis_index("bucket"), lax.axis_index("ctx")

    def heads_out(self, tokens, heads, send_sem, recv_sem, local_sem):
        rows = pl.ds(pl.multiple_of(self.me * 128, 128), 128)
        for off in (4, 3, 5, 2, 6, 1, 7):
            d = (self.me + off) % 8
            remote(tokens.at[:, pl.ds(pl.multiple_of(d * 128, 128), 128)], heads.at[rows], send_sem, recv_sem, (self.bucket, d)).start()
        pltpu.make_async_copy(tokens.at[:, pl.ds(pl.multiple_of(self.me * 128, 128), 128)], heads.at[rows], local_sem).start()

    def heads_back(self, heads, tokens, send_sem, recv_sem, local_sem):
        cols = pl.ds(pl.multiple_of(self.me * 128, 128), 128)
        for off in (4, 3, 5, 2, 6, 1, 7):
            d = (self.me + off) % 8
            remote(heads.at[pl.ds(pl.multiple_of(d * 128, 128), 128)], tokens.at[:, cols], send_sem, recv_sem, (self.bucket, d)).start()
        pltpu.make_async_copy(heads.at[pl.ds(pl.multiple_of(self.me * 128, 128), 128)], tokens.at[:, cols], local_sem).start()

    def wait(self, heads, send_sem, recv_sem, local_sem):
        seven = heads.at[pl.ds(0, 7 * 128)]
        bytes_of(seven, recv_sem).wait()
        bytes_of(seven, send_sem).wait()
        bytes_of(heads.at[pl.ds(0, 128)], local_sem).wait()


Q_BLOCK = 256


def attend_block(i, shift, kseq, q, k, v, o_ref, lse_ref):
    start = i * Q_BLOCK
    rows = pl.ds(pl.multiple_of(start, Q_BLOCK), Q_BLOCK)
    bias = key_bias(kseq[...], shift, start, Q_BLOCK)
    scaled = q[rows] * jnp.asarray(HEAD_DIM ** (-0.5), BF16)
    result = []
    for h in range(2):
        s = inner(k[...], only_head(scaled, h)) + bias
        m = jnp.max(s, axis=0, keepdims=True)
        e = jnp.exp(s - m)
        total = jnp.sum(e, axis=0, keepdims=True)
        w = (e * (1.0 / total)).astype(BF16)
        lse_ref[h:h + 1, rows] = m + jnp.log(total)
        o = outer(v[...], w)
        result.append(o[h * HEAD_DIM:(h + 1) * HEAD_DIM])
    o_ref[rows] = jnp.concatenate(result, axis=0).T.astype(BF16)


def attend_back_block(i, shift, kseq, q, k, v, do, lse, dq, dk, dv):
    start = i * Q_BLOCK
    rows = pl.ds(pl.multiple_of(start, Q_BLOCK), Q_BLOCK)
    bias = key_bias(kseq[...], shift, start, Q_BLOCK)
    scaled = q[rows] * jnp.asarray(HEAD_DIM ** (-0.5), BF16)
    back = do[rows]
    result = []
    for h in range(2):
        qm, dm = only_head(scaled, h), only_head(back, h)
        p = jnp.exp(inner(k[...], qm) + bias - lse[h:h + 1, rows])
        slope = inner(v[...], dm)
        product = p * slope
        delta = jnp.sum(product, axis=0, keepdims=True)
        ds = (product - p * delta).astype(BF16)
        dv[...] += dense(p.astype(BF16), dm)
        dk[...] += dense(ds, qm)
        g = outer(k[...], ds) * (HEAD_DIM ** (-0.5))
        result.append(g[h * HEAD_DIM:(h + 1) * HEAD_DIM])
    dq[rows] = jnp.concatenate(result, axis=0).T.astype(BF16)


def table_of(t_ref):
    groups = []
    for g in range(8):
        groups.append(sum(t_ref[4 * g + i].astype(F32) for i in range(4)))
    return jnp.concatenate(groups, axis=1)


def gelu_value(values):
    return 0.5 * values * (1.0 + lax.erf(values * 0.7071067811865476))


def gelu_slope(values):
    return 0.5 * (1.0 + lax.erf(values * 0.7071067811865476)) + values * jnp.exp(-0.5 * values * values) * 0.3989422804014327


def row_mean(values):
    return jnp.mean(values, axis=-1, keepdims=True)


def column_sum(values):
    return jnp.sum(values, axis=0, keepdims=True)


def norm_parts(summed):
    centred = summed - row_mean(summed)
    inv_std = lax.rsqrt(row_mean(centred * centred) + EPSILON)
    return centred * inv_std, inv_std


def norm_back(incoming, normed, inv_std, gain):
    scaled = incoming * gain
    return inv_std * (scaled - row_mean(scaled) - normed * row_mean(scaled * normed))


V_QUERY, V_VALUE, V_OUT, V_GAIN1, V_SHIFT1, V_DOWN, V_GAIN2, V_SHIFT2 = range(8)
V_UP = 8
W_DOWN, W_UP = 4096, 8192
GATHER = Plan(PIECES, (1, 3, 4, 6, 8, 10), (4,))
REDUCE = Plan(PIECES, (1, 3, 6, 9), (6,))
ONE_PIECE = Plan(1, (), ())


def piece_row(c, j):
    tall = (c >= 4) & (c < 8)
    return pl.multiple_of(jnp.where(tall, W_DOWN + 128 * j + ROWS * (c - 4), c * 1024 + ROWS * j), ROWS)


def add_f32(left, right):
    return left.astype(F32) + right.astype(F32)


class Reducer:
    stages = 7

    def __init__(self, route, plan, own, rb, ra, ru, rn, out, sems):
        self.rt, self.plan = route, plan
        self.own, self.rb, self.ra, self.ru, self.rn, self.out = own, rb, ra, ru, rn, out
        (self.sb_s, self.sb_r, self.sa_s, self.sa_r, self.sz_s, self.su_r, self.sn_r) = sems

    @staticmethod
    def slot(xx, yy, zz):
        return xx * 8 + zz * 2 + yy

    def add(self, c, k, other):
        at = self.own(c, k)
        at[...] = add_f32(at[...], other).astype(at.dtype)

    def roles(self, c):
        return self.rt.roles(self.plan.turned(c))

    def b_blocks(self, c):
        rt, ro = self.rt, self.roles(c)
        blocks = []
        for same_a in (0, 1):
            for zz in range(4):
                xx, yy = (ro.bx, ro.by) if same_a else (1 - rt.x, 1 - rt.y)
                blocks.append((self.slot(xx, yy, zz), same_a * 4 + zz))
        return blocks

    def send_b(self, c, k, at):
        remote(self.own(c, k), self.rb.at[c, at], self.sb_s.at[c], self.sb_r.at[c, at], self.roles(c).b).start()

    def to_b(self, c):
        for k, at in self.b_blocks(c):
            self.send_b(c, k, at)

    def add_b(self, c, k, at):
        bytes_of(self.rb.at[c, at], self.sb_r.at[c, at]).wait()
        self.add(c, k, self.rb[c, at])

    def to_a(self, c):
        rt, ro = self.rt, self.roles(c)
        for zz in range(4):
            k = self.slot(ro.ax, ro.ay, zz)
            self.add_b(c, k, zz)
            remote(self.own(c, k), self.ra(c, zz), self.sa_s.at[c], self.sa_r.at[c, zz], ro.a).start()
        for zz in range(4):
            self.add_b(c, self.slot(rt.x, rt.y, zz), 4 + zz)

    def keep_b(self, c):
        rt, ro = self.rt, self.roles(c)
        for zz in range(4):
            self.add_b(c, self.slot(ro.ax, ro.ay, zz), zz)
        for zz in range(4):
            self.add_b(c, self.slot(rt.x, rt.y, zz), 4 + zz)

    def from_a(self, c):
        rt = self.rt
        for step in range(4):
            zz = (rt.z + 1 + step) % 4
            k = self.slot(rt.x, rt.y, zz)
            bytes_of(self.ra(c, zz), self.sa_r.at[c, zz]).wait()
            self.add(c, k, self.ra(c, zz)[...])
            if step < 3:
                target = device(rt.x, rt.y, zz, rt.core)
                remote(self.own(c, k), self.ru(c, 0, step), self.sz_s.at[c, 0, step], self.su_r.at[c, 0, step], target).start()

    def total_line(self, c):
        rt = self.rt
        value = self.own(c, self.slot(rt.x, rt.y, rt.z))[...].astype(F32)
        for step in range(3):
            bytes_of(self.ru(c, 0, step), self.su_r.at[c, 0, step]).wait()
            value = value + self.ru(c, 0, step)[...].astype(F32)
        self.out[c] = value

    def along_z(self, c, hop, which):
        rt, ro = self.rt, self.roles(c)
        x, y = (ro.ax, ro.ay) if which else (rt.x, rt.y)

        @when(rt.z == hop)
        def _():
            for d in range(3, hop, -1):
                k = self.slot(x, y, d)
                at, sem = self.ru(c, which, d - 1), self.su_r.at[c, which, d - 1]
                if hop > 0:
                    bytes_of(at, sem).wait()
                    self.add(c, k, at[...])
                remote(self.own(c, k), at, self.sz_s.at[c, which, d], sem, rt.up).start()
            if hop > 0:
                bytes_of(self.ru(c, which, hop - 1), self.su_r.at[c, which, hop - 1]).wait()

        end = 3 - hop

        @when(rt.z == end)
        def _():
            for d in range(end):
                k = self.slot(x, y, d)
                at, sem = self.rn(c, which, d), self.sn_r.at[c, which, d]
                if end < 3:
                    bytes_of(at, sem).wait()
                    self.add(c, k, at[...])
                remote(self.own(c, k), at, self.sz_s.at[c, which, d], sem, rt.down).start()
            if end < 3:
                bytes_of(self.rn(c, which, end), self.sn_r.at[c, which, end]).wait()

    def sum_z(self, c, which, store):
        rt, ro = self.rt, self.roles(c)
        k = self.slot(ro.ax, ro.ay, rt.z) if which else self.slot(rt.x, rt.y, rt.z)

        @when(rt.z == 0)
        def _():
            store(k, add_f32(self.own(c, k)[...], self.rn(c, which, 0)[...]))

        @when(rt.z == 3)
        def _():
            store(k, add_f32(self.own(c, k)[...], self.ru(c, which, 2)[...]))

        for at in (1, 2):

            @when(rt.z == at)
            def _():
                store(k, add_f32(self.own(c, k)[...], self.ru(c, which, at - 1)[...]) + self.rn(c, which, at)[...].astype(F32))

    def close_a(self, c):
        ro = self.roles(c)

        def store(k, value):
            at = self.own(c, k)
            at[...] = value.astype(at.dtype)

        self.sum_z(c, 1, store)
        k = self.slot(ro.ax, ro.ay, self.rt.z)
        remote(self.own(c, k), self.ra(c, 0), self.sa_s.at[c], self.sa_r.at[c, 0], ro.a).start()

    def total(self, c):
        def store(k, value):
            bytes_of(self.ra(c, 0), self.sa_r.at[c, 0]).wait()
            self.out[c] = value + self.ra(c, 0)[...].astype(F32)

        self.sum_z(c, 0, store)

    def stage(self, s, c):
        mixed = self.plan.mixed(c)

        @when(mixed)
        def _():
            if s == 2:
                self.keep_b(c)
            if 2 <= s <= 5:
                self.along_z(c, s - 2, 1)
                self.along_z(c, s - 2, 0)
            if s == 5:
                self.close_a(c)
            if s == 6:
                self.total(c)

        @when(~mixed)
        def _():
            if s == 2:
                self.to_a(c)
            if s == 3:
                self.from_a(c)
            if s == 4:
                self.total_line(c)

    def finish(self, c):
        rt = self.rt
        bytes_of(self.rb.at[c], self.sb_s.at[c]).wait()

        @when(self.plan.mixed(c))
        def _():
            for which in range(2):
                for d in range(4):

                    @when(rt.z != d)
                    def _():
                        bytes_of(self.ra(c, 0), self.sz_s.at[c, which, d]).wait()

            bytes_of(self.ra(c, 0), self.sa_s.at[c]).wait()

        @when(~self.plan.mixed(c))
        def _():
            for step in range(3):
                bytes_of(self.ra(c, 0), self.sz_s.at[c, 0, step]).wait()
            bytes_of(self.rb.at[c, pl.ds(0, 4)], self.sa_s.at[c]).wait()


def reducer_sems(count):
    dma = pltpu.SemaphoreType.DMA
    return [dma((count,)), dma((count, 8)), dma((count,)), dma((count, 4)), dma((count, 2, 4)), dma((count, 2, 3)), dma((count, 2, 3))]


class Shared:
    def __init__(self, route, ref, sems, at, start=0):
        cols = pl.ds(start, 1024)
        self.rt, self.mine, self.other = route, ref.at[pl.ds(0, 128), cols], ref.at[pl.ds(128, 128), cols]
        self.send, self.recv = sems.at[0, at], sems.at[1, at]

    def give(self):
        remote(self.mine, self.other, self.send, self.recv, self.rt.sibling).start()

    def wait(self):
        bytes_of(self.mine, self.recv).wait()

    def sent(self):
        bytes_of(self.mine, self.send).wait()


SMALL_AT = 10
OFFSETS = (0, 0, 3, 5, 7, 9, 11)


def layer_kernel(x_ref, cot_ref, v_ref, len_ref, wq, wk, wv, wo, wu, wd,
                 kept, hid, gin, sums, small_out,
                 w, own, tiles, qkv, oh, kseq, qh, kh, vh, doh, lse, pre, nor1, inv1, gtwo, dk, dv, table, rows2,
                 x2, att2, mid2, act2, gffn2, gpre2, gbr2, dq2, dk2, dv2,
                 rb, ra, ru, rn, v_own, v_rb, v_ra, v_ru, v_rn, v_out,
                 own_sems, kept_sems, swap_sems, shared_sems, row_sems, *sems):
    rt, swap = Route(), Swap()
    shift = 7 + swap.bucket
    g_sems, gv_sems, r_sems, rv_sems = sems[:7], sems[7:14], sems[14:21], sems[21:28]
    loads = [pltpu.make_async_copy(ref, own.at[pl.ds(i * ROWS, ROWS)], own_sems.at[i]) for i, ref in enumerate((wq, wk, wv, wo))]
    loads.append(pltpu.make_async_copy(wd, own.at[pl.ds(4 * ROWS, 4 * ROWS)], own_sems.at[4]))
    for i in range(4):
        loads.append(pltpu.make_async_copy(wu.at[:, pl.ds(i * 1024, 1024)], own.at[pl.ds((8 + i) * ROWS, ROWS)], own_sems.at[5 + i]))
    loads.append(pltpu.make_async_copy(x_ref, x2.at[pl.ds(0, 128)], own_sems.at[9]))
    for load in loads:
        load.start()
    gather = Gatherer(
        rt, GATHER,
        lambda c: own.at[pl.ds(pl.multiple_of(c * ROWS, ROWS), ROWS)],
        lambda c, j: w.at[pl.ds(piece_row(c, j), ROWS)],
        lambda n: w.at[pl.ds(0, n * ROWS)],
        g_sems,
    )
    gather_small = Gatherer(rt, ONE_PIECE, lambda c: v_ref, lambda c, j: tiles.at[j], lambda n: tiles.at[pl.ds(0, n)], gv_sems)

    def own_block(c, k):
        first = jnp.where(c < 6, c * 512, W_DOWN + (c - 6) * 512)
        return w.at[pl.ds(pl.multiple_of(first + k * ROWS, ROWS), ROWS)]

    def ra_block(c, i):
        return ra.at[4 * c - 3 * REDUCE.mixed_before(c) + i]

    def ru_block(c, which, d):
        return ru.at[3 * (c + REDUCE.mixed_before(c) + which) + d]

    def rn_block(c, which, d):
        return rn.at[3 * (2 * REDUCE.mixed_before(c) + which) + d]

    reduce = Reducer(rt, REDUCE, own_block, rb, ra_block, ru_block, rn_block, sums, r_sems)
    reduce_small = Reducer(
        rt, ONE_PIECE, lambda c, k: v_own.at[k], v_rb, lambda c, i: v_ra.at[i],
        lambda c, which, d: v_ru.at[d], lambda c, which, d: v_rn.at[d], v_out, rv_sems,
    )
    sx, satt, smid, sgffn, sgbr, sdq, sdk, sdv = (
        Shared(rt, ref, shared_sems, i) for i, ref in enumerate((x2, att2, mid2, gffn2, gbr2, dq2, dk2, dv2))
    )
    sact = [Shared(rt, act2, shared_sems, 8 + i, i * 1024) for i in range(4)]
    sgpre = [Shared(rt, gpre2, shared_sems, 12 + i, i * 1024) for i in range(4)]
    for load in loads:
        load.wait()
    rt.greet()

    def vec(row):
        return table[row:row + 1]

    def trio(at):
        return tuple(swap_sems.at[3 * at + n] for n in range(3))

    def project(i):
        value = dense(x2[0:128], w[i * 1024:(i + 1) * 1024])
        if i != 1:
            value = value + vec(V_QUERY if i == 0 else V_VALUE)
        qkv[i] = value.astype(BF16)
        swap.heads_out(qkv.at[i], (qh, kh, vh)[i], *trio(i))

    def start():
        gather_small.arrived(0)
        sx.give()
        table[...] = table_of(tiles)
        for i in range(4):
            table[V_UP + i:V_UP + i + 1] = jnp.concatenate([tiles[8 * i + j][8:9].astype(F32) for j in range(8)], axis=1)
        kseq[...] = key_sequences(len_ref, shift, kseq.shape[0])
        project(0)

    def score(first):
        if first == 0:
            for i, ref in enumerate((qh, kh, vh)):
                swap.wait(ref, *trio(i))

        def block(i, _):
            attend_block(i, shift, kseq, qh, kh, vh, oh, lse)
            return 0

        lax.fori_loop(first, first + 2, block, 0)
        if first == 2:
            swap.heads_back(oh, att2.at[pl.ds(0, 128)], *trio(3))

    def first_norm():
        swap.wait(oh, *trio(3))
        satt.give()
        normed, inv = norm_parts(x2[0:128].astype(F32) + (dense(att2[0:128], w[3072:4096]) + vec(V_OUT)))
        nor1[...] = normed
        inv1[...] = inv
        mid2[0:128] = (normed * vec(V_GAIN1) + vec(V_SHIFT1)).astype(BF16)
        smid.give()
        gtwo[...] = jnp.zeros_like(gtwo)

    def up(i):
        value = dense(mid2[0:128], w[W_UP + i * 1024:W_UP + (i + 1) * 1024]) + vec(V_UP + i)
        pre[i] = value
        now = gelu_value(value).astype(BF16)
        act2[0:128, i * 1024:(i + 1) * 1024] = now
        sact[i].give()
        gtwo[...] += dense(now, w[W_DOWN + i * 1024:W_DOWN + (i + 1) * 1024])

    items = {
        7: start, 8: lambda: project(1), 9: lambda: project(2), 10: lambda: score(0), 11: lambda: score(2), 13: first_norm,
        15: lambda: up(0), 16: lambda: up(1), 17: lambda: up(2), 18: lambda: up(3),
    }

    def save(i):
        rows_of = pl.ds(pl.multiple_of(i * 1024, 1024), 1024)
        return pltpu.make_async_copy(w.at[rows_of], kept.at[rows_of], kept_sems.at[i])

    def gather_step(t, _):
        for s in range(Gatherer.stages):
            c = t - s

            @when(c == 0)
            def _():
                gather_small.stage(s, 0)

            @when((c >= 0) & (c < PIECES))
            def _():
                gather.stage(s, c)

        c = t - Gatherer.stages

        @when(c >= 0)
        def _():
            gather.arrived(c)

            @when(c < 3)
            def _():
                save(c).start()

        for k, item in items.items():

            @when(t == k)
            def _():
                item()

        return 0

    lax.fori_loop(0, PIECES + Gatherer.stages, gather_step, 0)
    middle = nor1[...] * vec(V_GAIN1) + vec(V_SHIFT1)
    normed2, inv2 = norm_parts(middle + (gtwo[...] + vec(V_DOWN)))
    g = cot_ref[...].astype(F32)
    back = norm_back(g, normed2, inv2, vec(V_GAIN2))
    low = back.astype(BF16)
    gffn2[0:128] = low
    sgffn.give()
    gtwo[...] = back
    hid[...] = (normed2 * vec(V_GAIN2) + vec(V_SHIFT2)).astype(BF16)
    rows2[0] = jnp.zeros(table.shape, F32)
    rows2[0, V_GAIN2:V_GAIN2 + 1] = column_sum(g * normed2)
    rows2[0, V_SHIFT2:V_SHIFT2 + 1] = column_sum(g)
    rows2[0, V_DOWN:V_DOWN + 1] = column_sum(low.astype(F32))
    gather_small.finish()
    gather_small.finish_z(0)

    def gathered(c, _):
        gather.finish_z(c)
        return 0

    lax.fori_loop(0, PIECES, gathered, 0)
    gather.finish()
    for i in range(3):
        save(i).wait()

    def tall(first):
        order = [(k, at) for k, at in reduce.b_blocks(first)]
        kept_here = []
        for same_a in (0, 1):
            for zz in range(4):
                ro = reduce.roles(first)
                xx, yy = (rt.x, rt.y) if same_a else (ro.ax, ro.ay)
                kept_here.append(reduce.slot(xx, yy, zz))

        def block(k):
            j = (k // 8) * 16 + rt.core * 8 + k % 8
            part = act2[:, pl.ds(pl.multiple_of(j * 128, 128), 128)]
            grad = outer(part, gffn2[...]).astype(BF16)
            for q in range(4):
                own_block(first + q, k)[...] = grad[q * ROWS:(q + 1) * ROWS]

        for k, at in order:
            block(k)
            for q in range(4):
                reduce.send_b(first + q, k, at)
        for k in kept_here:
            block(k)

    def square(left, right, c):
        for xx in range(2):
            part = left[:, pl.ds(pl.multiple_of((xx * 2 + rt.core) * 256, 256), 256)]
            grad = outer(part, right).astype(BF16)
            for i in range(8):
                own_block(c, xx * 8 + i)[...] = grad[i * ROWS:(i + 1) * ROWS]

    def compute(c):
        @when(c == 0)
        def _():
            for one in sact + [sgffn]:
                one.wait()
            tall(0)

        for i in range(4):

            @when(c == 4 + i)
            def _():
                if i == 0:
                    smid.wait()
                sgpre[i].wait()

        @when((c >= 4) & (c < 8))
        def _():
            square(mid2, gpre2[:, pl.ds(pl.multiple_of((c - 4) * 1024, 1024), 1024)], c)

        for k, (left, right, lw, rw) in enumerate(
            ((att2, gbr2, satt, sgbr), (x2, dq2, sx, sdq), (x2, dk2, None, sdk), (x2, dv2, None, sdv))
        ):

            @when(c == 8 + k)
            def _():
                if lw is not None:
                    lw.wait()
                rw.wait()
                square(left, right[...], c)

        @when(c >= 4)
        def _():
            reduce.to_b(c)

    def share_rows():
        return remote(rows2.at[0], rows2.at[1], row_sems.at[0], row_sems.at[1], rt.sibling)

    def compute_small():
        bytes_of(rows2.at[1], row_sems.at[1]).wait()
        rows2[0] = rows2[0] + rows2[1]

        def one(i, _):
            j = (i // 8) * 16 + rt.core * 8 + i % 8
            v_own[i, 0:8] = rows2[0, 0:8, pl.ds(pl.multiple_of((j // 4) * 128, 128), 128)]
            ups = rows2[0, 8:16, pl.ds(pl.multiple_of((j % 8) * 128, 128), 128)]
            row = lax.broadcasted_iota(jnp.int32, (8, 128), 0)
            v_own[i, 8:16] = jnp.where(row == j // 8, ups, 0.0)
            return 0

        lax.fori_loop(0, 16, one, 0)

    def ffn_back(i):
        gact = inner(gffn2[0:128], w[W_DOWN + i * 1024:W_DOWN + (i + 1) * 1024]).astype(BF16).astype(F32)
        gpre = (gact * gelu_slope(pre[i])).astype(BF16)
        gpre2[0:128, i * 1024:(i + 1) * 1024] = gpre
        sgpre[i].give()
        rows2[0, V_UP + i:V_UP + i + 1] = column_sum(gpre.astype(F32))
        part = inner(gpre, w[W_UP + i * 1024:W_UP + (i + 1) * 1024])
        if i == 0:
            gin[...] = part
        else:
            gin[...] += part

    def load(i):
        return pltpu.make_async_copy(kept.at[pl.ds(i * 1024, 1024)], w.at[pl.ds(W_UP + i * 1024, 1024)], kept_sems.at[i])

    def ffn_end():
        for i in range(3):
            load(i).start()
        gmid = gtwo[...] + gin[...].astype(BF16).astype(F32)
        normed1 = nor1[...]
        gone = norm_back(gmid, normed1, inv1[...], vec(V_GAIN1))
        gbr = gone.astype(BF16)
        gbr2[0:128] = gbr
        qkv[0] = inner(gbr, w[3072:4096]).astype(BF16)
        swap.heads_out(qkv.at[0], doh, *trio(4))
        gin[...] = gone
        sgbr.give()
        rows2[0, V_GAIN1:V_GAIN1 + 1] = column_sum(gmid * normed1)
        rows2[0, V_SHIFT1:V_SHIFT1 + 1] = column_sum(gmid)
        rows2[0, V_OUT:V_OUT + 1] = column_sum(gbr.astype(F32))
        dk[...] = jnp.zeros_like(dk)
        dv[...] = jnp.zeros_like(dv)

    def score_back(first, count):
        if first == 0:
            swap.wait(doh, *trio(4))

        def block(i, _):
            attend_back_block(i, shift, kseq, qh, kh, vh, doh, lse, qh, dk, dv)
            return 0

        lax.fori_loop(first, first + count, block, 0)

    back_trio = ((qh, dq2, sdq), (kh, dk2, sdk), (vh, dv2, sdv))

    def score_end():
        kh[...] = dk[...].astype(BF16)
        vh[...] = dv[...].astype(BF16)
        for i, (src, dst, _) in enumerate(back_trio):
            swap.heads_back(src, dst.at[pl.ds(0, 128)], *trio(5 + i))

    def exchange():
        for i, (src, dst, shared) in enumerate(back_trio):
            swap.wait(src, *trio(5 + i))
            shared.give()
        rows2[0, V_QUERY:V_QUERY + 1] = column_sum(dq2[0:128].astype(F32))
        rows2[0, V_VALUE:V_VALUE + 1] = column_sum(dv2[0:128].astype(F32))
        share_rows().start()

    def input_grad():
        total = gin[...]
        for i, ref in enumerate((dq2, dk2, dv2)):
            load(i).wait()
            total = total + inner(ref[0:128], w[W_UP + i * 1024:W_UP + (i + 1) * 1024])
        gin[...] = total
        share_rows().wait_send()

    back_items = {
        0: (lambda: ffn_back(1),),
        1: (lambda: ffn_back(2), lambda: ffn_back(3), ffn_end),
        2: (lambda: score_back(0, 1),), 3: (lambda: score_back(1, 1),), 4: (lambda: score_back(2, 1),),
        5: (lambda: score_back(3, 1), score_end),
        7: (exchange,), 8: (input_grad,),
    }
    ffn_back(0)

    def reduce_step(t, _):
        @when(t < PIECES)
        def _():
            compute(t)

        @when(t == SMALL_AT)
        def _():
            compute_small()
            reduce_small.to_b(0)

        for s in range(Reducer.stages - 1, 1, -1):
            c = t - OFFSETS[s]

            @when((c >= 0) & (c < PIECES))
            def _():
                reduce.stage(s, c)

            if s <= 4:

                @when(c == SMALL_AT)
                def _():
                    reduce_small.stage(s, 0)

        for k, parts in back_items.items():

            @when(t == k)
            def _():
                for part in parts:
                    part()

        return 0

    lax.fori_loop(0, PIECES + OFFSETS[-1], reduce_step, 0)

    def reduced(c, _):
        reduce.finish(c)
        return 0

    lax.fori_loop(0, PIECES, reduced, 0)
    reduce_small.finish(0)
    for one in [sx, satt, smid, sgffn, sgbr, sdq, sdk, sdv] + sact + sgpre:
        one.sent()
    mine = v_out[0]
    quarter = owner(rt.x, rt.y, rt.z, rt.core) % 4
    picked = jnp.zeros((16, 32), F32)
    for q in range(4):
        picked = jnp.where(quarter == q, mine[:, q * 32:(q + 1) * 32], picked)
    small_out[:, 0:128] = jnp.broadcast_to(column_sum(mine[8:16]), (16, 128))
    small_out[:, 128:160] = picked


def shaped(shape, dtype):
    return jax.ShapeDtypeStruct(shape, dtype)


def layer(tokens, cotangent, small, lens, weights):
    vmem, anywhere = pl.BlockSpec(memory_space=pltpu.VMEM), pl.BlockSpec(memory_space=pl.ANY)
    dma = pltpu.SemaphoreType.DMA
    narrow, heads = (128, 1024), (1024, 128)
    half, full = pltpu.VMEM(heads, BF16), pltpu.VMEM(heads, F32)
    pair, wide_pair, tokens_f32 = pltpu.VMEM((256, 1024), BF16), pltpu.VMEM((256, 4096), BF16), pltpu.VMEM(narrow, F32)

    mixed = len(REDUCE.which_mixed)

    def blocks(*n):
        return pltpu.VMEM(n + (ROWS, 1024), BF16)

    def tiles(*n):
        return pltpu.VMEM(n + (16, 128), F32)

    return pl.pallas_call(
        layer_kernel,
        out_shape=(
            shaped((3 * 1024, 1024), BF16), shaped(narrow, BF16), shaped(narrow, F32),
            shaped((PIECES, ROWS, 1024), F32), shaped((16, 256), F32),
        ),
        in_specs=[anywhere, vmem, vmem, pl.BlockSpec(memory_space=pltpu.SMEM)] + [anywhere] * 6,
        out_specs=(anywhere,) + (vmem,) * 4,
        scratch_shapes=[
            pltpu.VMEM((PIECES * 1024, 1024), BF16), pltpu.VMEM((PIECES * ROWS, 1024), BF16), pltpu.VMEM((32, 16, 128), BF16),
            pltpu.VMEM((3, 128, 1024), BF16), half, pltpu.VMEM(heads, jnp.int32), half, half, half, half,
            pltpu.VMEM((2, 1024), F32), pltpu.VMEM((4, 128, 1024), F32), tokens_f32, pltpu.VMEM((128, 1), F32), tokens_f32,
            full, full, pltpu.VMEM((16, 1024), F32), pltpu.VMEM((2, 16, 1024), F32),
            pair, pair, pair, wide_pair, pair, wide_pair, pair, pair, pair, pair,
            blocks(PIECES, 8), blocks(4 * PIECES - 3 * mixed), blocks(3 * PIECES + 3 * mixed), blocks(6 * mixed),
            tiles(16), tiles(1, 8), tiles(4), tiles(3), tiles(3), tiles(1),
            dma((10,)), dma((3,)), dma((24,)), dma((2, 16)), dma((2,)),
        ] + gather_sems(PIECES) + gather_sems(1) + reducer_sems(PIECES) + reducer_sems(1),
        compiler_params=pltpu.CompilerParams(collective_id=0, has_side_effects=True, vmem_limit_bytes=VMEM_LIMIT),
    )(tokens, cotangent, small, lens, *weights)


def unpack_kernel(sums, small, hid, gin, *outs):
    (o_hid, o_gin, o_q, o_k, o_v, o_bq, o_bv, o_o, o_bo, o_g1, o_s1, o_up, o_bup, o_down, o_bdown, o_g2, o_s2) = outs
    o_hid[...] = hid[...]
    o_gin[...] = gin[...]
    for ref, c in ((o_q, 9), (o_k, 10), (o_v, 11), (o_o, 8)):
        ref[...] = sums[c]
    for i in range(4):
        o_down[i * ROWS:(i + 1) * ROWS] = sums[i]
        o_up[:, i * 1024:(i + 1) * 1024] = sums[4 + i]
    for i, ref in enumerate((o_bq, o_bv, o_bo, o_g1, o_s1, o_bdown, o_g2, o_s2)):
        ref[...] = small[i, 128:160]
    o_bup[...] = small[8, 0:128]


def unpack(sums, small, hid, gin):
    vmem = pl.BlockSpec(memory_space=pltpu.VMEM)
    block, vector = shaped((ROWS, 1024), F32), shaped((32,), F32)
    return pl.pallas_call(
        unpack_kernel,
        out_shape=(
            shaped(hid.shape, BF16), shaped(gin.shape, F32), block, block, block, vector, vector, block, vector, vector, vector,
            shaped((ROWS, 4096), F32), shaped((128,), F32), shaped((128, 1024), F32), vector, vector, vector,
        ),
        in_specs=[vmem] * 4,
        out_specs=(vmem,) * 17,
        compiler_params=pltpu.CompilerParams(vmem_limit_bytes=VMEM_LIMIT),
    )(sums, small, hid, gin)


def fast_body(hidden_in, lengths, w_query, w_key, w_value, b_query, b_value, w_out, b_out, first_gain, first_shift,
              w_up, b_up, w_down, b_down, second_gain, second_shift, cotangent):
    tokens = hidden_in.reshape(128, 1024)
    me = lax.axis_index("bucket") * 8 + lax.axis_index("ctx")
    rows = jnp.stack([b_query, b_value, b_out, first_gain, first_shift, b_down, second_gain, second_shift])
    spread = jnp.concatenate([jnp.where(me % 4 == q, rows, jnp.zeros_like(rows)) for q in range(4)], axis=1)
    small = jnp.concatenate([spread, b_up[None], jnp.zeros((7, 128), BF16)], axis=0)
    _, hidden_out, grad_in, sums, small_sums = layer(
        tokens, cotangent.reshape(128, 1024), small, lengths.reshape(8), (w_query, w_key, w_value, w_out, w_up, w_down)
    )
    outs = unpack(sums, small_sums, hidden_out, grad_in)
    return (outs[0].reshape(hidden_in.shape), outs[1].reshape(hidden_in.shape)) + tuple(outs[2:])


def matmul(left, right):
    return jnp.dot(left, right, preferred_element_type=jnp.float32)


def row_inner(left, right):
    return lax.dot_general(
        left, right, (((0,), (0,)), ((), ())), preferred_element_type=jnp.float32
    )


def right_inner(left, right):
    return lax.dot_general(
        left, right, (((1,), (1,)), ((), ())), preferred_element_type=jnp.float32
    )


def rounded(values):
    return values.astype(jnp.bfloat16)


def widened(values):
    return values.astype(jnp.float32)


def norm_forward(summed, gain_vec, shift_vec):
    average = jnp.mean(summed, axis=-1, keepdims=True)
    centred = summed - average
    variance = jnp.mean(centred * centred, axis=-1, keepdims=True)
    inv_std = lax.rsqrt(variance + EPSILON)
    normed = centred * inv_std
    return (normed * gain_vec + shift_vec, normed, inv_std)


def norm_backward(incoming, normed, inv_std, gain_vec):
    scaled = incoming * gain_vec
    inner = (
        scaled
        - jnp.mean(scaled, axis=-1, keepdims=True)
        - normed * jnp.mean(scaled * normed, axis=-1, keepdims=True)
    )
    return (inv_std * inner, jnp.sum(incoming * normed, axis=0), jnp.sum(incoming, axis=0))


def plain_gelu_value(values):
    return 0.5 * values * (1.0 + jax.scipy.special.erf(values * 0.7071067811865476))


def plain_gelu_slope(values):
    return (
        0.5 * (1.0 + jax.scipy.special.erf(values * 0.7071067811865476))
        + values * jnp.exp(-0.5 * values * values) * 0.3989422804014327
    )


def split_heads(values):
    return values.reshape(values.shape[0], values.shape[1], values.shape[2] // HEAD_DIM, HEAD_DIM)


def seq_mask(seq_info, query_pos, key_pos):
    seq_lens, slot_len = seq_info
    query_seq = query_pos // slot_len
    key_seq = key_pos // slot_len
    seq_ids = jnp.arange(seq_lens.shape[1], dtype=jnp.int32)
    picked = (key_seq[:, None] == seq_ids[None, :]).astype(jnp.int32)
    key_limit = jnp.sum(picked[None, :, :] * seq_lens[:, None, :], axis=-1)
    key_valid = (key_pos - key_seq * slot_len)[None, :] < key_limit
    same_seq = query_seq[:, None] == key_seq[None, :]
    return (same_seq[None, :, :] & key_valid[:, None, :])[:, None, :, :]


def score_block(query4, key4, query_start, key_start, seq_info):
    raw = jnp.einsum(
        "sqhd,skhd->shqk", query4, key4, preferred_element_type=jnp.float32
    ) * HEAD_DIM ** (-0.5)
    query_pos = query_start + jnp.arange(query4.shape[1], dtype=jnp.int32)
    key_pos = key_start + jnp.arange(key4.shape[1], dtype=jnp.int32)
    allowed = seq_mask(seq_info, query_pos, key_pos)
    return (jnp.where(allowed, raw, NEG_FILL), allowed)


def over_blocks(block_step, running, pieces):
    length_here = pieces[0].shape[1]
    block_len = math.gcd(length_here, 512)
    turn_count = length_here // block_len

    def advance(turn_no, current):
        offset = turn_no * block_len
        sliced = tuple(
            (lax.dynamic_slice_in_dim(piece_arr, offset, block_len, 1) for piece_arr in pieces)
        )
        return block_step(current, sliced, offset)

    return lax.fori_loop(0, turn_count, advance, running)


def general_body(
    hidden_in,
    lengths,
    w_query,
    w_key,
    w_value,
    b_query,
    b_value,
    w_out,
    b_out,
    first_gain,
    first_shift,
    w_up,
    b_up,
    w_down,
    b_down,
    second_gain,
    second_shift,
    cotangent,
):
    shards = (
        w_query,
        w_key,
        w_value,
        b_query,
        b_value,
        w_out,
        b_out,
        first_gain,
        first_shift,
        w_up,
        b_up,
        w_down,
        b_down,
        second_gain,
        second_shift,
    )
    gathered = (
        lax.all_gather(shards[0], ("bucket", "ctx"), axis=0, tiled=True),
        lax.all_gather(shards[1], ("bucket", "ctx"), axis=0, tiled=True),
        lax.all_gather(shards[2], ("bucket", "ctx"), axis=0, tiled=True),
        lax.all_gather(shards[3], ("bucket", "ctx"), axis=0, tiled=True),
        lax.all_gather(shards[4], ("bucket", "ctx"), axis=0, tiled=True),
        lax.all_gather(shards[5], ("bucket", "ctx"), axis=0, tiled=True),
        lax.all_gather(shards[6], ("bucket", "ctx"), axis=0, tiled=True),
        lax.all_gather(shards[7], ("bucket", "ctx"), axis=0, tiled=True),
        lax.all_gather(shards[8], ("bucket", "ctx"), axis=0, tiled=True),
        lax.all_gather(shards[9], ("bucket", "ctx"), axis=0, tiled=True),
        lax.all_gather(shards[10], ("bucket", "ctx"), axis=0, tiled=True),
        lax.all_gather(shards[11], ("bucket", "ctx"), axis=0, tiled=True),
        lax.all_gather(shards[12], ("bucket", "ctx"), axis=0, tiled=True),
        lax.all_gather(shards[13], ("bucket", "ctx"), axis=0, tiled=True),
        lax.all_gather(shards[14], ("bucket", "ctx"), axis=0, tiled=True),
    )
    (
        query_mat,
        key_mat,
        value_mat,
        query_bias,
        value_bias,
        out_mat,
        out_bias,
        gain_one,
        shift_one,
        up_mat,
        up_bias,
        down_mat,
        down_bias,
        gain_two,
        shift_two,
    ) = gathered
    seq_count = hidden_in.shape[1]
    local_rows = hidden_in.shape[2]
    model_width = hidden_in.shape[3]
    head_count = model_width // HEAD_DIM
    total_rows = seq_count * local_rows
    block_shape = (seq_count, local_rows, model_width)
    score_scale = HEAD_DIM ** (-0.5)
    seq_total = local_rows * lax.axis_size("ctx")
    group_index = lax.axis_index("bucket")
    seq_slots = jnp.right_shift(jnp.int32(lengths.shape[2]), group_index)
    slot_len = jnp.int32(seq_total) // seq_slots
    seq_info = (lengths[0], slot_len)
    own_start = lax.axis_index("ctx") * local_rows
    tokens = hidden_in.reshape(total_rows, model_width)
    query_low = rounded(matmul(tokens, query_mat) + widened(query_bias))
    key_low = rounded(matmul(tokens, key_mat))
    value_low = rounded(matmul(tokens, value_mat) + widened(value_bias))
    query_heads = split_heads(query_low.reshape(block_shape))
    key_rows = key_low.reshape(block_shape)
    value_rows = value_low.reshape(block_shape)

    def stats_step(running, sliced, anchor):
        scores, allowed = score_block(
            query_heads, split_heads(sliced[0]), own_start, anchor, seq_info
        )
        run_max, run_total = running
        new_max = jnp.maximum(run_max, jnp.max(scores, axis=-1))
        raised = jnp.where(allowed, jnp.exp(scores - new_max[..., None]), 0.0)
        return (new_max, run_total * jnp.exp(run_max - new_max) + jnp.sum(raised, axis=-1))

    stat_shape = (seq_count, head_count, local_rows)
    stats_start = (jnp.full(stat_shape, NEG_FILL, jnp.float32), jnp.zeros(stat_shape, jnp.float32))
    run_max, run_total = over_blocks(
        stats_step, stats_start, (lax.all_gather(key_rows, "ctx", axis=1, tiled=True),)
    )
    log_total = run_max + jnp.log(run_total)

    def output_step(running, sliced, anchor):
        key4 = split_heads(sliced[0])
        value4 = split_heads(sliced[1])
        scores, allowed = score_block(query_heads, key4, own_start, anchor, seq_info)
        probs_low = rounded(jnp.where(allowed, jnp.exp(scores - log_total[..., None]), 0.0))
        return running + jnp.einsum(
            "shqk,skhd->sqhd", probs_low, value4, preferred_element_type=jnp.float32
        )

    attended_f32 = over_blocks(
        output_step,
        jnp.zeros(query_heads.shape, jnp.float32),
        (
            lax.all_gather(key_rows, "ctx", axis=1, tiled=True),
            lax.all_gather(value_rows, "ctx", axis=1, tiled=True),
        ),
    )
    attended_low = rounded(attended_f32.reshape(total_rows, model_width))
    branch = matmul(attended_low, out_mat) + widened(out_bias)
    middle, normed_one, inv_one = norm_forward(
        widened(tokens) + branch, widened(gain_one), widened(shift_one)
    )
    middle_low = rounded(middle)
    pre_act = matmul(middle_low, up_mat) + widened(up_bias)
    activated = rounded(plain_gelu_value(pre_act))
    ffn_out = matmul(activated, down_mat) + widened(down_bias)
    result, normed_two, inv_two = norm_forward(
        middle + ffn_out, widened(gain_two), widened(shift_two)
    )
    hidden_out = rounded(result).reshape(hidden_in.shape)
    gathered = (
        lax.all_gather(shards[0], ("bucket", "ctx"), axis=0, tiled=True),
        lax.all_gather(shards[1], ("bucket", "ctx"), axis=0, tiled=True),
        lax.all_gather(shards[2], ("bucket", "ctx"), axis=0, tiled=True),
        lax.all_gather(shards[3], ("bucket", "ctx"), axis=0, tiled=True),
        lax.all_gather(shards[4], ("bucket", "ctx"), axis=0, tiled=True),
        lax.all_gather(shards[5], ("bucket", "ctx"), axis=0, tiled=True),
        lax.all_gather(shards[6], ("bucket", "ctx"), axis=0, tiled=True),
        lax.all_gather(shards[7], ("bucket", "ctx"), axis=0, tiled=True),
        lax.all_gather(shards[8], ("bucket", "ctx"), axis=0, tiled=True),
        lax.all_gather(shards[9], ("bucket", "ctx"), axis=0, tiled=True),
        lax.all_gather(shards[10], ("bucket", "ctx"), axis=0, tiled=True),
        lax.all_gather(shards[11], ("bucket", "ctx"), axis=0, tiled=True),
        lax.all_gather(shards[12], ("bucket", "ctx"), axis=0, tiled=True),
        lax.all_gather(shards[13], ("bucket", "ctx"), axis=0, tiled=True),
        lax.all_gather(shards[14], ("bucket", "ctx"), axis=0, tiled=True),
    )
    query_mat = gathered[0]
    key_mat = gathered[1]
    value_mat = gathered[2]
    out_mat = gathered[5]
    gain_one = gathered[7]
    up_mat = gathered[9]
    down_mat = gathered[11]
    gain_two = gathered[13]
    incoming = widened(cotangent.reshape(total_rows, model_width))
    grad_two_sum, grad_second_gain, grad_second_shift = norm_backward(
        incoming, normed_two, inv_two, widened(gain_two)
    )
    grad_ffn = rounded(grad_two_sum)
    grad_b_down = jnp.sum(widened(grad_ffn), axis=0)
    grad_w_down = row_inner(activated, grad_ffn)
    grad_act = widened(rounded(right_inner(grad_ffn, down_mat)))
    grad_pre = rounded(grad_act * plain_gelu_slope(pre_act))
    grad_b_up = jnp.sum(widened(grad_pre), axis=0)
    grad_w_up = row_inner(middle_low, grad_pre)
    grad_middle = grad_two_sum + widened(rounded(right_inner(grad_pre, up_mat)))
    grad_one_sum, grad_first_gain, grad_first_shift = norm_backward(
        grad_middle, normed_one, inv_one, widened(gain_one)
    )
    grad_branch = rounded(grad_one_sum)
    grad_b_out = jnp.sum(widened(grad_branch), axis=0)
    grad_w_out = row_inner(attended_low, grad_branch)
    grad_att = rounded(right_inner(grad_branch, out_mat)).reshape(block_shape)
    grad_att_heads = split_heads(grad_att)
    delta = jnp.einsum("sqhd,sqhd->shq", widened(grad_att_heads), attended_f32)

    def grad_terms(query4, key4, value4, att4, row_log, row_delta, query_start, key_start):
        scores, allowed = score_block(query4, key4, query_start, key_start, seq_info)
        probs = jnp.where(allowed, jnp.exp(scores - row_log[..., None]), 0.0)
        slope = jnp.einsum("sqhd,skhd->shqk", att4, value4, preferred_element_type=jnp.float32)
        return (rounded(probs), rounded(probs * (slope - row_delta[..., None])))

    def query_step(running, sliced, anchor):
        key4 = split_heads(sliced[0])
        value4 = split_heads(sliced[1])
        probs_low, score_grad = grad_terms(
            query_heads, key4, value4, grad_att_heads, log_total, delta, own_start, anchor
        )
        return (
            running
            + jnp.einsum("shqk,skhd->sqhd", score_grad, key4, preferred_element_type=jnp.float32)
            * score_scale
        )

    grad_q = over_blocks(
        query_step,
        jnp.zeros(query_heads.shape, jnp.float32),
        (
            lax.all_gather(key_rows, "ctx", axis=1, tiled=True),
            lax.all_gather(value_rows, "ctx", axis=1, tiled=True),
        ),
    )
    log_all, delta_all = (
        lax.all_gather(log_total, "ctx", axis=2, tiled=True),
        lax.all_gather(delta, "ctx", axis=2, tiled=True),
    )
    own_keys = split_heads(key_rows)
    own_values = split_heads(value_rows)

    def owner_step(running, sliced, anchor):
        query4 = split_heads(sliced[0])
        att4 = split_heads(sliced[1])
        count_here = sliced[0].shape[1]
        row_log = lax.dynamic_slice_in_dim(log_all, anchor, count_here, 2)
        row_delta = lax.dynamic_slice_in_dim(delta_all, anchor, count_here, 2)
        probs_low, score_grad = grad_terms(
            query4, own_keys, own_values, att4, row_log, row_delta, anchor, own_start
        )
        grad_k, grad_v = running
        grad_k = (
            grad_k
            + jnp.einsum("shqk,sqhd->skhd", score_grad, query4, preferred_element_type=jnp.float32)
            * score_scale
        )
        grad_v = grad_v + jnp.einsum(
            "shqk,sqhd->skhd", probs_low, att4, preferred_element_type=jnp.float32
        )
        return (grad_k, grad_v)

    owner_start = (jnp.zeros(own_keys.shape, jnp.float32), jnp.zeros(own_keys.shape, jnp.float32))
    grad_k_own, grad_v_own = over_blocks(
        owner_step,
        owner_start,
        (
            lax.all_gather(query_low.reshape(block_shape), "ctx", axis=1, tiled=True),
            lax.all_gather(grad_att, "ctx", axis=1, tiled=True),
        ),
    )
    grad_q_low = rounded(grad_q.reshape(total_rows, model_width))
    grad_k_low = rounded(grad_k_own.reshape(total_rows, model_width))
    grad_v_low = rounded(grad_v_own.reshape(total_rows, model_width))
    grad_w_query = row_inner(tokens, grad_q_low)
    grad_b_query = jnp.sum(widened(grad_q_low), axis=0)
    grad_w_key = row_inner(tokens, grad_k_low)
    grad_w_value = row_inner(tokens, grad_v_low)
    grad_b_value = jnp.sum(widened(grad_v_low), axis=0)
    grad_in = (
        grad_one_sum
        + right_inner(grad_q_low, query_mat)
        + right_inner(grad_k_low, key_mat)
        + right_inner(grad_v_low, value_mat)
    )
    owned = (
        lax.psum_scatter(grad_w_query, ("bucket", "ctx"), scatter_dimension=0, tiled=True),
        lax.psum_scatter(grad_w_key, ("bucket", "ctx"), scatter_dimension=0, tiled=True),
        lax.psum_scatter(grad_w_value, ("bucket", "ctx"), scatter_dimension=0, tiled=True),
        lax.psum_scatter(grad_b_query, ("bucket", "ctx"), scatter_dimension=0, tiled=True),
        lax.psum_scatter(grad_b_value, ("bucket", "ctx"), scatter_dimension=0, tiled=True),
        lax.psum_scatter(grad_w_out, ("bucket", "ctx"), scatter_dimension=0, tiled=True),
        lax.psum_scatter(grad_b_out, ("bucket", "ctx"), scatter_dimension=0, tiled=True),
        lax.psum_scatter(grad_first_gain, ("bucket", "ctx"), scatter_dimension=0, tiled=True),
        lax.psum_scatter(grad_first_shift, ("bucket", "ctx"), scatter_dimension=0, tiled=True),
        lax.psum_scatter(grad_w_up, ("bucket", "ctx"), scatter_dimension=0, tiled=True),
        lax.psum_scatter(grad_b_up, ("bucket", "ctx"), scatter_dimension=0, tiled=True),
        lax.psum_scatter(grad_w_down, ("bucket", "ctx"), scatter_dimension=0, tiled=True),
        lax.psum_scatter(grad_b_down, ("bucket", "ctx"), scatter_dimension=0, tiled=True),
        lax.psum_scatter(grad_second_gain, ("bucket", "ctx"), scatter_dimension=0, tiled=True),
        lax.psum_scatter(grad_second_shift, ("bucket", "ctx"), scatter_dimension=0, tiled=True),
    )
    return (hidden_out, grad_in.reshape(hidden_in.shape)) + tuple(owned)


def solution(mesh):
    placed = (
        P("bucket", None, "ctx", None),
        P("bucket", None, None),
        P(("bucket", "ctx"), None),
        P(("bucket", "ctx"), None),
        P(("bucket", "ctx"), None),
        P(("bucket", "ctx")),
        P(("bucket", "ctx")),
        P(("bucket", "ctx"), None),
        P(("bucket", "ctx")),
        P(("bucket", "ctx")),
        P(("bucket", "ctx")),
        P(("bucket", "ctx"), None),
        P(("bucket", "ctx")),
        P(("bucket", "ctx"), None),
        P(("bucket", "ctx")),
        P(("bucket", "ctx")),
        P(("bucket", "ctx")),
        P("bucket", None, "ctx", None),
    )
    def body(*arguments):
        here = dict(mesh.shape) == {"bucket": 4, "ctx": 8}
        shapes = arguments[0].shape == (1, 1, 128, 1024) and arguments[11].shape == (32, 4096)
        return (fast_body if here and shapes else general_body)(*arguments)

    return jax.shard_map(
        body,
        mesh=mesh,
        in_specs=placed,
        out_specs=(
            P("bucket", None, "ctx", None),
            P("bucket", None, "ctx", None),
            P(("bucket", "ctx"), None),
            P(("bucket", "ctx"), None),
            P(("bucket", "ctx"), None),
            P(("bucket", "ctx")),
            P(("bucket", "ctx")),
            P(("bucket", "ctx"), None),
            P(("bucket", "ctx")),
            P(("bucket", "ctx")),
            P(("bucket", "ctx")),
            P(("bucket", "ctx"), None),
            P(("bucket", "ctx")),
            P(("bucket", "ctx"), None),
            P(("bucket", "ctx")),
            P(("bucket", "ctx")),
            P(("bucket", "ctx")),
        ),
        check_vma=False,
    )
```

```python
import math

import jax
import jax.numpy as jnp
from jax import lax
from jax.experimental import pallas as pl
from jax.experimental.pallas import tpu as pltpu
from jax.sharding import PartitionSpec as P

HEAD_DIM = 64
EPSILON = 1e-05
NEG_FILL = -1e30
MESH_ID = pl.DeviceIdType.MESH
F32, BF16 = jnp.float32, jnp.bfloat16
ROWS = 32
PIECES = 12
VMEM_LIMIT = 63 * 2**20


def when(condition):
    return pl.when(condition)


def place():
    bucket, ctx = lax.axis_index("bucket"), lax.axis_index("ctx")
    return bucket // 2, ctx % 2, ctx // 2, bucket % 2


def device(x, y, z, core):
    return (x * 2 + core, z * 2 + y)


def owner(x, y, z, core):
    return (x * 2 + core) * 8 + z * 2 + y


def remote(src, dst, send_sem, recv_sem, target):
    return pltpu.make_async_remote_copy(
        src_ref=src, dst_ref=dst, send_sem=send_sem, recv_sem=recv_sem,
        device_id=target, device_id_type=MESH_ID,
    )


def bytes_of(ref, sem):
    return pltpu.make_async_copy(ref, ref, sem)


class Roles:
    def __init__(self, route, b_along_x):
        x, y, z, core = route.x, route.y, route.z, route.core
        self.ax, self.ay = jnp.where(b_along_x, x, 1 - x), jnp.where(b_along_x, 1 - y, y)
        self.bx, self.by = jnp.where(b_along_x, 1 - x, x), jnp.where(b_along_x, y, 1 - y)
        self.a = device(self.ax, self.ay, z, core)
        self.b = device(self.bx, self.by, z, core)


class Route:
    def __init__(self):
        self.x, self.y, self.z, self.core = x, y, z, core = place()
        self.across = (device(1 - x, y, z, core), device(x, 1 - y, z, core))
        self.sibling = device(x, y, z, 1 - core)
        self.up = device(x, y, jnp.minimum(z + 1, 3), core)
        self.down = device(x, y, jnp.maximum(z - 1, 0), core)

    def roles(self, turned):
        return Roles(self, (self.core == 1) | turned)

    def greet(self):
        z = self.z
        bucket, ctx = lax.axis_index("bucket"), lax.axis_index("ctx")
        barrier = pltpu.get_barrier_semaphore()
        pack = [(bucket, (ctx + off) % 8) for off in range(1, 8)]
        for target in [*self.across, self.sibling] + pack:
            pl.semaphore_signal(barrier, inc=1, device_id=target, device_id_type=MESH_ID)

        @when(z < 3)
        def _():
            pl.semaphore_signal(barrier, inc=1, device_id=self.up, device_id_type=MESH_ID)

        @when(z > 0)
        def _():
            pl.semaphore_signal(barrier, inc=1, device_id=self.down, device_id_type=MESH_ID)

        pl.semaphore_wait(barrier, 10 + (z < 3).astype(jnp.int32) + (z > 0).astype(jnp.int32))


class Plan:
    def __init__(self, count, mixed, turned, direct):
        self.count, self.which_mixed, self.which_turned, self.which_direct = count, mixed, turned, direct

    def direct(self, c):
        return self.member(c, self.which_direct)

    def chained(self, c):
        return ~(self.mixed(c) | self.direct(c))

    def mixed(self, c):
        return self.member(c, self.which_mixed)

    def turned(self, c):
        return self.member(c, self.which_turned)

    def mixed_before(self, c):
        return sum((c > item).astype(jnp.int32) for item in self.which_mixed)

    @staticmethod
    def member(c, items):
        hit = jnp.bool_(False)
        for item in items:
            hit = hit | (c == item)
        return hit


class Gatherer:
    stages = 7

    def __init__(self, route, plan, own, block, span, sems):
        self.rt, self.plan, self.own, self.block, self.span = route, plan, own, block, span
        (self.zs, self.zr, self.ps, self.ar, self.br, self.dr, self.ls) = sems

    def spread(self, c, src, j, jz, ro, to_a, to_b, z_dirs):
        rt, dst = self.rt, self.block(c, j)
        which, directions = z_dirs
        if "line" in directions:
            for slot in range(3):
                target = device(rt.x, rt.y, (rt.z + slot + 1) % 4, rt.core)
                remote(src, dst, self.zs.at[0, c, which, slot], self.zr.at[c, which, jz], target).start()

        if "up" in directions:

            @when(rt.z < 3)
            def _():
                remote(src, dst, self.zs.at[0, c, which, jz], self.zr.at[c, which, jz], rt.up).start()

        if "down" in directions:

            @when(rt.z > 0)
            def _():
                remote(src, dst, self.zs.at[1, c, which, jz], self.zr.at[c, which, jz], rt.down).start()

        if to_b is not None:
            remote(src, dst, self.ps, self.br.at[c, to_b * 4 + jz], ro.b).start()
        if to_a is not None:

            @when(to_a)
            def _():
                remote(src, dst, self.ps, self.ar.at[c, jz], ro.a).start()

        remote(src, dst, self.ps, self.dr.at[c], rt.sibling).start()

    def near(self, k, action):
        for sign in (0,) if k == 0 else (-1, 1):
            zz = self.rt.z + sign * k

            @when((zz >= 0) & (zz <= 3))
            def _():
                action(zz, "up" if sign < 0 else "down")

    def own_stage(self, c):
        rt, ro = self.rt, self.rt.roles(self.plan.turned(c))
        j = owner(rt.x, rt.y, rt.z, rt.core)
        pltpu.make_async_copy(self.own(c), self.block(c, j), self.ls.at[c]).start()
        direct = self.plan.direct(c)

        @when(direct)
        def _():
            self.spread(c, self.own(c), j, rt.z, ro, jnp.bool_(True), 0, (0, ("line",)))

        @when(~direct)
        def _():
            self.spread(c, self.own(c), j, rt.z, ro, jnp.bool_(True), 0, (0, ("up", "down")))

    def z_stage(self, c, k):
        rt, ro = self.rt, self.rt.roles(self.plan.turned(c))

        def action(zz, direction):
            j = owner(rt.x, rt.y, zz, rt.core)
            bytes_of(self.block(c, j), self.zr.at[c, 0, zz]).wait()

            @when(self.plan.direct(c))
            def _():
                self.spread(c, self.block(c, j), j, zz, ro, jnp.bool_(True), 0, (0, ()))

            @when(~self.plan.direct(c))
            def _():
                self.spread(c, self.block(c, j), j, zz, ro, ~self.plan.mixed(c), 0, (0, (direction,)))


        self.near(k, action)

    def z_stage_of_a(self, c, k):
        rt, ro = self.rt, self.rt.roles(self.plan.turned(c))

        def action(zz, direction):
            j = owner(ro.ax, ro.ay, zz, rt.core)
            bytes_of(self.block(c, j), self.zr.at[c, 1, zz]).wait()
            self.spread(c, self.block(c, j), j, zz, ro, None, 1, (1, (direction,)))

        self.near(k, action)

    def a_stage(self, c, k, directions=()):
        rt, ro = self.rt, self.rt.roles(self.plan.turned(c))

        def action(zz, _):
            j = owner(ro.ax, ro.ay, zz, rt.core)
            bytes_of(self.block(c, j), self.ar.at[c, zz]).wait()
            self.spread(c, self.block(c, j), j, zz, ro, None, 1, (1, directions))

        self.near(k, action)

    def b_stage(self, c, k):
        rt, ro = self.rt, self.rt.roles(self.plan.turned(c))

        def action(zz, _):
            for which, (xx, yy) in enumerate(((ro.bx, ro.by), (1 - rt.x, 1 - rt.y))):
                j = owner(xx, yy, zz, rt.core)
                bytes_of(self.block(c, j), self.br.at[c, which * 4 + zz]).wait()
                self.spread(c, self.block(c, j), j, zz, ro, None, None, (0, ()))

        self.near(k, action)

    def stage(self, s, c):
        mixed, direct = self.plan.mixed(c), self.plan.direct(c)
        if s == 0:
            self.own_stage(c)

        @when(direct)
        def _():
            for k in range(1, 4):
                if s == 1:
                    self.z_stage(c, k)
            for k in range(4):
                if s == 2:
                    self.a_stage(c, k)
                if s == 3:
                    self.b_stage(c, k)

        @when(~direct)
        def _():
            if 1 <= s <= 3:
                self.z_stage(c, s)
            if s == 1:

                @when(mixed)
                def _():
                    self.a_stage(c, 0, ("up", "down"))

                @when(~mixed)
                def _():
                    self.a_stage(c, 0)

            if 2 <= s <= 4:

                @when(mixed)
                def _():
                    self.z_stage_of_a(c, s - 1)

                @when(~mixed)
                def _():
                    self.a_stage(c, s - 1)

            if 3 <= s <= 6:
                self.b_stage(c, s - 3)

    def arrived(self, c):
        bytes_of(self.span(16), self.dr.at[c]).wait()
        bytes_of(self.span(1), self.ls.at[c]).wait()

    def finish(self):
        bytes_of(self.span(28 * self.plan.count - 3 * len(self.plan.which_mixed)), self.ps).wait()

    def finish_z(self, c):
        rt = self.rt

        def sent(which):
            for zz in range(4):

                @when((rt.z < 3) & (rt.z >= zz))
                def _():
                    bytes_of(self.span(1), self.zs.at[0, c, which, zz]).wait()

                @when((rt.z > 0) & (rt.z <= zz))
                def _():
                    bytes_of(self.span(1), self.zs.at[1, c, which, zz]).wait()

        @when(self.plan.direct(c))
        def _():
            for slot in range(3):
                bytes_of(self.span(1), self.zs.at[0, c, 0, slot]).wait()

        @when(~self.plan.direct(c))
        def _():
            sent(0)

        @when(self.plan.mixed(c))
        def _():
            sent(1)


def gather_sems(count):
    dma = pltpu.SemaphoreType.DMA
    return [dma((2, count, 2, 4)), dma((count, 2, 4)), dma(()), dma((count, 4)), dma((count, 8)), dma((count,)), dma((count,))]


def outer(left, right):
    return lax.dot_general(left, right, (((0,), (0,)), ((), ())), preferred_element_type=F32)


def inner(left, right):
    return lax.dot_general(left, right, (((1,), (1,)), ((), ())), preferred_element_type=F32)


def dense(left, right):
    return jnp.dot(left, right, preferred_element_type=F32)


def head_mask(shape, head):
    lane = lax.broadcasted_iota(jnp.int32, shape, len(shape) - 1)
    return (lane // HEAD_DIM) == head


def only_head(values, head):
    return jnp.where(head_mask(values.shape, head), values, jnp.zeros_like(values))


def key_sequences(len_ref, shift, keys):
    pos = lax.broadcasted_iota(jnp.int32, (keys, 128), 0)
    seq = lax.shift_right_logical(pos, shift)
    at = pos - lax.shift_left(seq, shift)
    limit = jnp.zeros((keys, 128), jnp.int32)
    for s in range(8):
        limit = jnp.where(seq == s, len_ref[s], limit)
    return jnp.where(at < limit, seq, -1)


def key_bias(kseq, shift, start, width):
    keys = kseq.shape[0]
    qseq = lax.shift_right_logical(start + lax.broadcasted_iota(jnp.int32, (1, 128), 1), shift)
    parts = []
    for w in range(width // 128):
        qs = lax.shift_right_logical(start + w * 128 + lax.broadcasted_iota(jnp.int32, (1, 128), 1), shift)
        parts.append(jnp.where(kseq == qs, 0.0, NEG_FILL))
    return jnp.concatenate(parts, axis=1)


class Swap:
    def __init__(self):
        self.bucket, self.me = lax.axis_index("bucket"), lax.axis_index("ctx")

    def heads_out(self, tokens, heads, send_sem, recv_sem, local_sem):
        rows = pl.ds(pl.multiple_of(self.me * 128, 128), 128)
        for off in (4, 3, 5, 2, 6, 1, 7):
            d = (self.me + off) % 8
            remote(tokens.at[:, pl.ds(pl.multiple_of(d * 128, 128), 128)], heads.at[rows], send_sem, recv_sem, (self.bucket, d)).start()
        pltpu.make_async_copy(tokens.at[:, pl.ds(pl.multiple_of(self.me * 128, 128), 128)], heads.at[rows], local_sem).start()

    def heads_back(self, heads, tokens, send_sem, recv_sem, local_sem):
        cols = pl.ds(pl.multiple_of(self.me * 128, 128), 128)
        for off in (4, 3, 5, 2, 6, 1, 7):
            d = (self.me + off) % 8
            remote(heads.at[pl.ds(pl.multiple_of(d * 128, 128), 128)], tokens.at[:, cols], send_sem, recv_sem, (self.bucket, d)).start()
        pltpu.make_async_copy(heads.at[pl.ds(pl.multiple_of(self.me * 128, 128), 128)], tokens.at[:, cols], local_sem).start()

    def wait(self, heads, send_sem, recv_sem, local_sem):
        seven = heads.at[pl.ds(0, 7 * 128)]
        bytes_of(seven, recv_sem).wait()
        bytes_of(seven, send_sem).wait()
        bytes_of(heads.at[pl.ds(0, 128)], local_sem).wait()


Q_BLOCK = 256


def attend_block(i, shift, kseq, q, k, v, o_ref, lse_ref):
    start = i * Q_BLOCK
    rows = pl.ds(pl.multiple_of(start, Q_BLOCK), Q_BLOCK)
    bias = key_bias(kseq[...], shift, start, Q_BLOCK)
    scaled = q[rows] * jnp.asarray(HEAD_DIM ** (-0.5), BF16)
    result = []
    for h in range(2):
        s = inner(k[...], only_head(scaled, h)) + bias
        m = jnp.max(s, axis=0, keepdims=True)
        e = jnp.exp(s - m)
        total = jnp.sum(e, axis=0, keepdims=True)
        w = (e * (1.0 / total)).astype(BF16)
        lse_ref[h:h + 1, rows] = m + jnp.log(total)
        o = outer(v[...], w)
        result.append(o[h * HEAD_DIM:(h + 1) * HEAD_DIM])
    o_ref[rows] = jnp.concatenate(result, axis=0).T.astype(BF16)


def attend_back_block(i, shift, kseq, q, k, v, do, lse, dq, dk, dv):
    start = i * Q_BLOCK
    rows = pl.ds(pl.multiple_of(start, Q_BLOCK), Q_BLOCK)
    bias = key_bias(kseq[...], shift, start, Q_BLOCK)
    scaled = q[rows] * jnp.asarray(HEAD_DIM ** (-0.5), BF16)
    back = do[rows]
    result = []
    for h in range(2):
        qm, dm = only_head(scaled, h), only_head(back, h)
        p = jnp.exp(inner(k[...], qm) + bias - lse[h:h + 1, rows])
        slope = inner(v[...], dm)
        product = p * slope
        delta = jnp.sum(product, axis=0, keepdims=True)
        ds = (product - p * delta).astype(BF16)
        dv[...] += dense(p.astype(BF16), dm)
        dk[...] += dense(ds, qm)
        g = outer(k[...], ds) * (HEAD_DIM ** (-0.5))
        result.append(g[h * HEAD_DIM:(h + 1) * HEAD_DIM])
    dq[rows] = jnp.concatenate(result, axis=0).T.astype(BF16)


def table_of(t_ref):
    groups = []
    for g in range(8):
        groups.append(sum(t_ref[4 * g + i].astype(F32) for i in range(4)))
    return jnp.concatenate(groups, axis=1)


def gelu_value(values):
    return 0.5 * values * (1.0 + lax.erf(values * 0.7071067811865476))


def gelu_slope(values):
    return 0.5 * (1.0 + lax.erf(values * 0.7071067811865476)) + values * jnp.exp(-0.5 * values * values) * 0.3989422804014327


def row_mean(values):
    return jnp.mean(values, axis=-1, keepdims=True)


def column_sum(values):
    return jnp.sum(values, axis=0, keepdims=True)


def norm_parts(summed):
    centred = summed - row_mean(summed)
    inv_std = lax.rsqrt(row_mean(centred * centred) + EPSILON)
    return centred * inv_std, inv_std


def norm_back(incoming, normed, inv_std, gain):
    scaled = incoming * gain
    return inv_std * (scaled - row_mean(scaled) - normed * row_mean(scaled * normed))


V_QUERY, V_VALUE, V_OUT, V_GAIN1, V_SHIFT1, V_DOWN, V_GAIN2, V_SHIFT2 = range(8)
V_UP = 8
W_DOWN, W_UP = 4096, 8192
GATHER = Plan(PIECES, (1, 3, 4, 6, 8, 10), (4,), ())
REDUCE = Plan(PIECES, (1, 3, 6, 9), (6,), (11,))
ONE_PIECE = Plan(1, (), (), ())


def piece_row(c, j):
    tall = (c >= 4) & (c < 8)
    return pl.multiple_of(jnp.where(tall, W_DOWN + 128 * j + ROWS * (c - 4), c * 1024 + ROWS * j), ROWS)


def add_f32(left, right):
    return left.astype(F32) + right.astype(F32)


class Reducer:
    stages = 7

    def __init__(self, route, plan, own, rb, ra, ru, rn, out, sems):
        self.rt, self.plan = route, plan
        self.own, self.rb, self.ra, self.ru, self.rn, self.out = own, rb, ra, ru, rn, out
        (self.sb_s, self.sb_r, self.sa_s, self.sa_r, self.sz_s, self.su_r, self.sn_r) = sems

    @staticmethod
    def slot(xx, yy, zz):
        return xx * 8 + zz * 2 + yy

    def add(self, c, k, other):
        at = self.own(c, k)
        at[...] = add_f32(at[...], other).astype(at.dtype)

    def roles(self, c):
        return self.rt.roles(self.plan.turned(c))

    def b_blocks(self, c):
        rt, ro = self.rt, self.roles(c)
        blocks = []
        for same_a in (0, 1):
            for zz in range(4):
                xx, yy = (ro.bx, ro.by) if same_a else (1 - rt.x, 1 - rt.y)
                blocks.append((self.slot(xx, yy, zz), same_a * 4 + zz))
        return blocks

    def send_b(self, c, k, at):
        remote(self.own(c, k), self.rb.at[c, at], self.sb_s.at[c], self.sb_r.at[c, at], self.roles(c).b).start()

    def to_b(self, c):
        for k, at in self.b_blocks(c):
            self.send_b(c, k, at)

    def add_b(self, c, k, at):
        bytes_of(self.rb.at[c, at], self.sb_r.at[c, at]).wait()
        self.add(c, k, self.rb[c, at])

    def to_a(self, c):
        rt, ro = self.rt, self.roles(c)
        for zz in range(4):
            k = self.slot(ro.ax, ro.ay, zz)
            self.add_b(c, k, zz)
            remote(self.own(c, k), self.ra(c, zz), self.sa_s.at[c], self.sa_r.at[c, zz], ro.a).start()
        for zz in range(4):
            self.add_b(c, self.slot(rt.x, rt.y, zz), 4 + zz)

    def keep_b(self, c):
        rt, ro = self.rt, self.roles(c)
        for zz in range(4):
            self.add_b(c, self.slot(ro.ax, ro.ay, zz), zz)
        for zz in range(4):
            self.add_b(c, self.slot(rt.x, rt.y, zz), 4 + zz)

    def from_a(self, c):
        rt = self.rt
        for zz in range(4):
            bytes_of(self.ra(c, zz), self.sa_r.at[c, zz]).wait()
            self.add(c, self.slot(rt.x, rt.y, zz), self.ra(c, zz)[...])

    def to_line(self, c):
        rt = self.rt
        for step in range(4):
            zz = (rt.z + 1 + step) % 4
            k = self.slot(rt.x, rt.y, zz)
            bytes_of(self.ra(c, zz), self.sa_r.at[c, zz]).wait()
            self.add(c, k, self.ra(c, zz)[...])
            if step < 3:
                target = device(rt.x, rt.y, zz, rt.core)
                remote(self.own(c, k), self.ru(c, 0, step), self.sz_s.at[c, 0, step], self.su_r.at[c, 0, step], target).start()

    def total_line(self, c):
        rt = self.rt
        value = self.own(c, self.slot(rt.x, rt.y, rt.z))[...].astype(F32)
        for step in range(3):
            bytes_of(self.ru(c, 0, step), self.su_r.at[c, 0, step]).wait()
            value = value + self.ru(c, 0, step)[...].astype(F32)
        self.out[c] = value

    def along_z(self, c, hop, which):
        rt, ro = self.rt, self.roles(c)
        x, y = (ro.ax, ro.ay) if which else (rt.x, rt.y)

        @when(rt.z == hop)
        def _():
            for d in range(3, hop, -1):
                k = self.slot(x, y, d)
                at, sem = self.ru(c, which, d - 1), self.su_r.at[c, which, d - 1]
                if hop > 0:
                    bytes_of(at, sem).wait()
                    self.add(c, k, at[...])
                remote(self.own(c, k), at, self.sz_s.at[c, which, d], sem, rt.up).start()
            if hop > 0:
                bytes_of(self.ru(c, which, hop - 1), self.su_r.at[c, which, hop - 1]).wait()

        end = 3 - hop

        @when(rt.z == end)
        def _():
            for d in range(end):
                k = self.slot(x, y, d)
                at, sem = self.rn(c, which, d), self.sn_r.at[c, which, d]
                if end < 3:
                    bytes_of(at, sem).wait()
                    self.add(c, k, at[...])
                remote(self.own(c, k), at, self.sz_s.at[c, which, d], sem, rt.down).start()
            if end < 3:
                bytes_of(self.rn(c, which, end), self.sn_r.at[c, which, end]).wait()

    def sum_z(self, c, which, store):
        rt, ro = self.rt, self.roles(c)
        k = self.slot(ro.ax, ro.ay, rt.z) if which else self.slot(rt.x, rt.y, rt.z)

        @when(rt.z == 0)
        def _():
            store(k, add_f32(self.own(c, k)[...], self.rn(c, which, 0)[...]))

        @when(rt.z == 3)
        def _():
            store(k, add_f32(self.own(c, k)[...], self.ru(c, which, 2)[...]))

        for at in (1, 2):

            @when(rt.z == at)
            def _():
                store(k, add_f32(self.own(c, k)[...], self.ru(c, which, at - 1)[...]) + self.rn(c, which, at)[...].astype(F32))

    def close_a(self, c):
        ro = self.roles(c)

        def store(k, value):
            at = self.own(c, k)
            at[...] = value.astype(at.dtype)

        self.sum_z(c, 1, store)
        k = self.slot(ro.ax, ro.ay, self.rt.z)
        remote(self.own(c, k), self.ra(c, 0), self.sa_s.at[c], self.sa_r.at[c, 0], ro.a).start()

    def total(self, c, from_a):
        def store(k, value):
            if from_a:
                bytes_of(self.ra(c, 0), self.sa_r.at[c, 0]).wait()
                value = value + self.ra(c, 0)[...].astype(F32)
            self.out[c] = value

        self.sum_z(c, 0, store)

    def stage(self, s, c):
        mixed = self.plan.mixed(c)

        @when(mixed)
        def _():
            if s == 2:
                self.keep_b(c)
            if 2 <= s <= 5:
                self.along_z(c, s - 2, 1)
                self.along_z(c, s - 2, 0)
            if s == 5:
                self.close_a(c)
            if s == 6:
                self.total(c, True)

        @when(self.plan.direct(c))
        def _():
            if s == 2:
                self.to_a(c)
            if s == 3:
                self.to_line(c)
            if s == 4:
                self.total_line(c)

        @when(self.plan.chained(c))
        def _():
            if s == 2:
                self.to_a(c)
            if s == 3:
                self.from_a(c)
            if s >= 3:
                self.along_z(c, s - 3, 0)
            if s == 6:
                self.total(c, False)

    def finish(self, c):
        rt = self.rt
        bytes_of(self.rb.at[c], self.sb_s.at[c]).wait()

        def sent(which):
            for d in range(4):

                @when(rt.z != d)
                def _():
                    bytes_of(self.ra(c, 0), self.sz_s.at[c, which, d]).wait()

        @when(self.plan.direct(c))
        def _():
            for step in range(3):
                bytes_of(self.ra(c, 0), self.sz_s.at[c, 0, step]).wait()

        @when(~self.plan.direct(c))
        def _():
            sent(0)

        @when(self.plan.mixed(c))
        def _():
            sent(1)
            bytes_of(self.ra(c, 0), self.sa_s.at[c]).wait()

        @when(~self.plan.mixed(c))
        def _():
            bytes_of(self.rb.at[c, pl.ds(0, 4)], self.sa_s.at[c]).wait()


def reducer_sems(count):
    dma = pltpu.SemaphoreType.DMA
    return [dma((count,)), dma((count, 8)), dma((count,)), dma((count, 4)), dma((count, 2, 4)), dma((count, 2, 3)), dma((count, 2, 3))]


class Shared:
    def __init__(self, route, ref, sems, at, start=0):
        cols = pl.ds(start, 1024)
        self.rt, self.mine, self.other = route, ref.at[pl.ds(0, 128), cols], ref.at[pl.ds(128, 128), cols]
        self.send, self.recv = sems.at[0, at], sems.at[1, at]

    def give(self):
        remote(self.mine, self.other, self.send, self.recv, self.rt.sibling).start()

    def wait(self):
        bytes_of(self.mine, self.recv).wait()

    def sent(self):
        bytes_of(self.mine, self.send).wait()


SMALL_AT = 10
GATHER_OFFSETS = (0, 1, 2, 3, 4, 5, 6, 7)
OFFSETS = (0, 0, 3, 5, 7, 9, 11)


def layer_kernel(x_ref, cot_ref, v_ref, len_ref, wq, wk, wv, wo, wu, wd,
                 kept, hid, gin, sums, small_out,
                 w, own, tiles, qkv, oh, kseq, qh, kh, vh, doh, lse, pre, nor1, inv1, gtwo, dk, dv, table, rows2,
                 x2, att2, mid2, act2, gffn2, gpre2, gbr2, dq2, dk2, dv2,
                 rb, ra, ru, rn, v_own, v_rb, v_ra, v_ru, v_rn, v_out,
                 own_sems, kept_sems, swap_sems, shared_sems, row_sems, *sems):
    rt, swap = Route(), Swap()
    shift = 7 + swap.bucket
    g_sems, gv_sems, r_sems, rv_sems = sems[:7], sems[7:14], sems[14:21], sems[21:28]
    loads = [pltpu.make_async_copy(ref, own.at[pl.ds(i * ROWS, ROWS)], own_sems.at[i]) for i, ref in enumerate((wq, wk, wv, wo))]
    loads.append(pltpu.make_async_copy(wd, own.at[pl.ds(4 * ROWS, 4 * ROWS)], own_sems.at[4]))
    for i in range(4):
        loads.append(pltpu.make_async_copy(wu.at[:, pl.ds(i * 1024, 1024)], own.at[pl.ds((8 + i) * ROWS, ROWS)], own_sems.at[5 + i]))
    loads.append(pltpu.make_async_copy(x_ref, x2.at[pl.ds(0, 128)], own_sems.at[9]))
    for load in loads:
        load.start()
    gather = Gatherer(
        rt, GATHER,
        lambda c: own.at[pl.ds(pl.multiple_of(c * ROWS, ROWS), ROWS)],
        lambda c, j: w.at[pl.ds(piece_row(c, j), ROWS)],
        lambda n: w.at[pl.ds(0, n * ROWS)],
        g_sems,
    )
    gather_small = Gatherer(rt, ONE_PIECE, lambda c: v_ref, lambda c, j: tiles.at[j], lambda n: tiles.at[pl.ds(0, n)], gv_sems)

    def own_block(c, k):
        first = jnp.where(c < 6, c * 512, W_DOWN + (c - 6) * 512)
        return w.at[pl.ds(pl.multiple_of(first + k * ROWS, ROWS), ROWS)]

    def ra_block(c, i):
        return ra.at[4 * c - 3 * REDUCE.mixed_before(c) + i]

    def ru_block(c, which, d):
        return ru.at[3 * (c + REDUCE.mixed_before(c) + which) + d]

    def rn_block(c, which, d):
        return rn.at[3 * (c + REDUCE.mixed_before(c) + which) + d]

    reduce = Reducer(rt, REDUCE, own_block, rb, ra_block, ru_block, rn_block, sums, r_sems)
    reduce_small = Reducer(
        rt, ONE_PIECE, lambda c, k: v_own.at[k], v_rb, lambda c, i: v_ra.at[i],
        lambda c, which, d: v_ru.at[d], lambda c, which, d: v_rn.at[d], v_out, rv_sems,
    )
    sx, satt, smid, sgffn, sgbr, sdq, sdk, sdv = (
        Shared(rt, ref, shared_sems, i) for i, ref in enumerate((x2, att2, mid2, gffn2, gbr2, dq2, dk2, dv2))
    )
    sact = [Shared(rt, act2, shared_sems, 8 + i, i * 1024) for i in range(4)]
    sgpre = [Shared(rt, gpre2, shared_sems, 12 + i, i * 1024) for i in range(4)]
    for load in loads:
        load.wait()
    rt.greet()

    def vec(row):
        return table[row:row + 1]

    def trio(at):
        return tuple(swap_sems.at[3 * at + n] for n in range(3))

    def project(i):
        value = dense(x2[0:128], w[i * 1024:(i + 1) * 1024])
        if i != 1:
            value = value + vec(V_QUERY if i == 0 else V_VALUE)
        qkv[i] = value.astype(BF16)
        swap.heads_out(qkv.at[i], (qh, kh, vh)[i], *trio(i))

    def start():
        gather_small.arrived(0)
        sx.give()
        table[...] = table_of(tiles)
        for i in range(4):
            table[V_UP + i:V_UP + i + 1] = jnp.concatenate([tiles[8 * i + j][8:9].astype(F32) for j in range(8)], axis=1)
        kseq[...] = key_sequences(len_ref, shift, kseq.shape[0])
        project(0)

    def score(first):
        if first == 0:
            for i, ref in enumerate((qh, kh, vh)):
                swap.wait(ref, *trio(i))

        def block(i, _):
            attend_block(i, shift, kseq, qh, kh, vh, oh, lse)
            return 0

        lax.fori_loop(first, first + 2, block, 0)
        if first == 2:
            swap.heads_back(oh, att2.at[pl.ds(0, 128)], *trio(3))

    def first_norm():
        swap.wait(oh, *trio(3))
        satt.give()
        normed, inv = norm_parts(x2[0:128].astype(F32) + (dense(att2[0:128], w[3072:4096]) + vec(V_OUT)))
        nor1[...] = normed
        inv1[...] = inv
        mid2[0:128] = (normed * vec(V_GAIN1) + vec(V_SHIFT1)).astype(BF16)
        smid.give()
        gtwo[...] = jnp.zeros_like(gtwo)

    def up(i):
        value = dense(mid2[0:128], w[W_UP + i * 1024:W_UP + (i + 1) * 1024]) + vec(V_UP + i)
        pre[i] = value
        now = gelu_value(value).astype(BF16)
        act2[0:128, i * 1024:(i + 1) * 1024] = now
        sact[i].give()
        gtwo[...] += dense(now, w[W_DOWN + i * 1024:W_DOWN + (i + 1) * 1024])

    items = {
        0: start, 1: lambda: project(1), 2: lambda: project(2), 4: lambda: score(0), 5: lambda: score(2), 7: first_norm,
        8: lambda: up(0), 9: lambda: up(1), 10: lambda: up(2), 11: lambda: up(3),
    }

    def save(i):
        rows_of = pl.ds(pl.multiple_of(i * 1024, 1024), 1024)
        return pltpu.make_async_copy(w.at[rows_of], kept.at[rows_of], kept_sems.at[i])

    def gather_step(t, _):
        for s in range(Gatherer.stages):
            c = t - GATHER_OFFSETS[s]

            @when(c == 0)
            def _():
                gather_small.stage(s, 0)

            @when((c >= 0) & (c < PIECES))
            def _():
                gather.stage(s, c)

        c = t - GATHER_OFFSETS[-1]

        @when(c >= 0)
        def _():
            gather.arrived(c)

            @when(c < 3)
            def _():
                save(c).start()

        for k, item in items.items():

            @when(c == k)
            def _():
                item()

        return 0

    lax.fori_loop(0, PIECES + GATHER_OFFSETS[-1], gather_step, 0)
    middle = nor1[...] * vec(V_GAIN1) + vec(V_SHIFT1)
    normed2, inv2 = norm_parts(middle + (gtwo[...] + vec(V_DOWN)))
    g = cot_ref[...].astype(F32)
    back = norm_back(g, normed2, inv2, vec(V_GAIN2))
    low = back.astype(BF16)
    gffn2[0:128] = low
    sgffn.give()
    gtwo[...] = back
    hid[...] = (normed2 * vec(V_GAIN2) + vec(V_SHIFT2)).astype(BF16)
    rows2[0] = jnp.zeros(table.shape, F32)
    rows2[0, V_GAIN2:V_GAIN2 + 1] = column_sum(g * normed2)
    rows2[0, V_SHIFT2:V_SHIFT2 + 1] = column_sum(g)
    rows2[0, V_DOWN:V_DOWN + 1] = column_sum(low.astype(F32))
    gather_small.finish()
    gather_small.finish_z(0)

    def gathered(c, _):
        gather.finish_z(c)
        return 0

    lax.fori_loop(0, PIECES, gathered, 0)
    gather.finish()
    for i in range(3):
        save(i).wait()

    def tall(first):
        order = [(k, at) for k, at in reduce.b_blocks(first)]
        kept_here = []
        for same_a in (0, 1):
            for zz in range(4):
                ro = reduce.roles(first)
                xx, yy = (rt.x, rt.y) if same_a else (ro.ax, ro.ay)
                kept_here.append(reduce.slot(xx, yy, zz))

        def block(k):
            j = (k // 8) * 16 + rt.core * 8 + k % 8
            part = act2[:, pl.ds(pl.multiple_of(j * 128, 128), 128)]
            grad = outer(part, gffn2[...]).astype(BF16)
            for q in range(4):
                own_block(first + q, k)[...] = grad[q * ROWS:(q + 1) * ROWS]

        for k, at in order:
            block(k)
        for k in kept_here:
            block(k)

    def square(left, right, c):
        for xx in range(2):
            part = left[:, pl.ds(pl.multiple_of((xx * 2 + rt.core) * 256, 256), 256)]
            grad = outer(part, right).astype(BF16)
            for i in range(8):
                own_block(c, xx * 8 + i)[...] = grad[i * ROWS:(i + 1) * ROWS]

    def compute(c):
        @when(c == 0)
        def _():
            for one in sact + [sgffn]:
                one.wait()
            tall(0)

        for i in range(4):

            @when(c == 4 + i)
            def _():
                if i == 0:
                    smid.wait()
                sgpre[i].wait()

        @when((c >= 4) & (c < 8))
        def _():
            square(mid2, gpre2[:, pl.ds(pl.multiple_of((c - 4) * 1024, 1024), 1024)], c)

        for k, (left, right, lw, rw) in enumerate(
            ((att2, gbr2, satt, sgbr), (x2, dq2, sx, sdq), (x2, dk2, None, sdk), (x2, dv2, None, sdv))
        ):

            @when(c == 8 + k)
            def _():
                if lw is not None:
                    lw.wait()
                rw.wait()
                square(left, right[...], c)

        reduce.to_b(c)

    def share_rows():
        return remote(rows2.at[0], rows2.at[1], row_sems.at[0], row_sems.at[1], rt.sibling)

    def compute_small():
        bytes_of(rows2.at[1], row_sems.at[1]).wait()
        rows2[0] = rows2[0] + rows2[1]

        def one(i, _):
            j = (i // 8) * 16 + rt.core * 8 + i % 8
            v_own[i, 0:8] = rows2[0, 0:8, pl.ds(pl.multiple_of((j // 4) * 128, 128), 128)]
            ups = rows2[0, 8:16, pl.ds(pl.multiple_of((j % 8) * 128, 128), 128)]
            row = lax.broadcasted_iota(jnp.int32, (8, 128), 0)
            v_own[i, 8:16] = jnp.where(row == j // 8, ups, 0.0)
            return 0

        lax.fori_loop(0, 16, one, 0)

    def ffn_back(i):
        gact = inner(gffn2[0:128], w[W_DOWN + i * 1024:W_DOWN + (i + 1) * 1024]).astype(BF16).astype(F32)
        gpre = (gact * gelu_slope(pre[i])).astype(BF16)
        gpre2[0:128, i * 1024:(i + 1) * 1024] = gpre
        sgpre[i].give()
        rows2[0, V_UP + i:V_UP + i + 1] = column_sum(gpre.astype(F32))
        part = inner(gpre, w[W_UP + i * 1024:W_UP + (i + 1) * 1024])
        if i == 0:
            gin[...] = part
        else:
            gin[...] += part

    def load(i):
        return pltpu.make_async_copy(kept.at[pl.ds(i * 1024, 1024)], w.at[pl.ds(W_UP + i * 1024, 1024)], kept_sems.at[i])

    def ffn_end():
        for i in range(3):
            load(i).start()
        gmid = gtwo[...] + gin[...].astype(BF16).astype(F32)
        normed1 = nor1[...]
        gone = norm_back(gmid, normed1, inv1[...], vec(V_GAIN1))
        gbr = gone.astype(BF16)
        gbr2[0:128] = gbr
        qkv[0] = inner(gbr, w[3072:4096]).astype(BF16)
        swap.heads_out(qkv.at[0], doh, *trio(4))
        gin[...] = gone
        sgbr.give()
        rows2[0, V_GAIN1:V_GAIN1 + 1] = column_sum(gmid * normed1)
        rows2[0, V_SHIFT1:V_SHIFT1 + 1] = column_sum(gmid)
        rows2[0, V_OUT:V_OUT + 1] = column_sum(gbr.astype(F32))
        dk[...] = jnp.zeros_like(dk)
        dv[...] = jnp.zeros_like(dv)

    def score_back(first, count):
        if first == 0:
            swap.wait(doh, *trio(4))

        def block(i, _):
            attend_back_block(i, shift, kseq, qh, kh, vh, doh, lse, qh, dk, dv)
            return 0

        lax.fori_loop(first, first + count, block, 0)

    back_trio = ((qh, dq2, sdq), (kh, dk2, sdk), (vh, dv2, sdv))

    def score_end():
        kh[...] = dk[...].astype(BF16)
        vh[...] = dv[...].astype(BF16)
        for i, (src, dst, _) in enumerate(back_trio):
            swap.heads_back(src, dst.at[pl.ds(0, 128)], *trio(5 + i))

    def exchange():
        for i, (src, dst, shared) in enumerate(back_trio):
            swap.wait(src, *trio(5 + i))
            shared.give()
        rows2[0, V_QUERY:V_QUERY + 1] = column_sum(dq2[0:128].astype(F32))
        rows2[0, V_VALUE:V_VALUE + 1] = column_sum(dv2[0:128].astype(F32))
        share_rows().start()

    def input_grad():
        total = gin[...]
        for i, ref in enumerate((dq2, dk2, dv2)):
            load(i).wait()
            total = total + inner(ref[0:128], w[W_UP + i * 1024:W_UP + (i + 1) * 1024])
        gin[...] = total
        share_rows().wait_send()

    back_items = {
        0: (lambda: ffn_back(1),),
        1: (lambda: ffn_back(2), lambda: ffn_back(3), ffn_end),
        2: (lambda: score_back(0, 1),), 3: (lambda: score_back(1, 1),), 4: (lambda: score_back(2, 1),),
        5: (lambda: score_back(3, 1), score_end),
        7: (exchange,), 8: (input_grad,),
    }
    ffn_back(0)

    def reduce_step(t, _):
        @when(t < PIECES)
        def _():
            compute(t)

        @when(t == SMALL_AT)
        def _():
            compute_small()
            reduce_small.to_b(0)

        for s in range(Reducer.stages - 1, 1, -1):
            c = t - OFFSETS[s]

            @when((c >= 0) & (c < PIECES))
            def _():
                reduce.stage(s, c)

            @when(c == SMALL_AT)
            def _():
                reduce_small.stage(s, 0)

        for k, parts in back_items.items():

            @when(t == k)
            def _():
                for part in parts:
                    part()

        return 0

    lax.fori_loop(0, PIECES + OFFSETS[-1], reduce_step, 0)

    def reduced(c, _):
        reduce.finish(c)
        return 0

    lax.fori_loop(0, PIECES, reduced, 0)
    reduce_small.finish(0)
    for one in [sx, satt, smid, sgffn, sgbr, sdq, sdk, sdv] + sact + sgpre:
        one.sent()
    mine = v_out[0]
    quarter = owner(rt.x, rt.y, rt.z, rt.core) % 4
    picked = jnp.zeros((16, 32), F32)
    for q in range(4):
        picked = jnp.where(quarter == q, mine[:, q * 32:(q + 1) * 32], picked)
    small_out[:, 0:128] = jnp.broadcast_to(column_sum(mine[8:16]), (16, 128))
    small_out[:, 128:160] = picked


def shaped(shape, dtype):
    return jax.ShapeDtypeStruct(shape, dtype)


def layer(tokens, cotangent, small, lens, weights):
    vmem, anywhere = pl.BlockSpec(memory_space=pltpu.VMEM), pl.BlockSpec(memory_space=pl.ANY)
    dma = pltpu.SemaphoreType.DMA
    narrow, heads = (128, 1024), (1024, 128)
    half, full = pltpu.VMEM(heads, BF16), pltpu.VMEM(heads, F32)
    pair, wide_pair, tokens_f32 = pltpu.VMEM((256, 1024), BF16), pltpu.VMEM((256, 4096), BF16), pltpu.VMEM(narrow, F32)

    mixed = len(REDUCE.which_mixed)

    def blocks(*n):
        return pltpu.VMEM(n + (ROWS, 1024), BF16)

    def tiles(*n):
        return pltpu.VMEM(n + (16, 128), F32)

    return pl.pallas_call(
        layer_kernel,
        out_shape=(
            shaped((3 * 1024, 1024), BF16), shaped(narrow, BF16), shaped(narrow, F32),
            shaped((PIECES, ROWS, 1024), F32), shaped((16, 256), F32),
        ),
        in_specs=[anywhere, vmem, vmem, pl.BlockSpec(memory_space=pltpu.SMEM)] + [anywhere] * 6,
        out_specs=(anywhere,) + (vmem,) * 4,
        scratch_shapes=[
            pltpu.VMEM((PIECES * 1024, 1024), BF16), pltpu.VMEM((PIECES * ROWS, 1024), BF16), pltpu.VMEM((32, 16, 128), BF16),
            pltpu.VMEM((3, 128, 1024), BF16), half, pltpu.VMEM(heads, jnp.int32), half, half, half, half,
            pltpu.VMEM((2, 1024), F32), pltpu.VMEM((4, 128, 1024), F32), tokens_f32, pltpu.VMEM((128, 1), F32), tokens_f32,
            full, full, pltpu.VMEM((16, 1024), F32), pltpu.VMEM((2, 16, 1024), F32),
            pair, pair, pair, wide_pair, pair, wide_pair, pair, pair, pair, pair,
            blocks(PIECES, 8), blocks(4 * PIECES - 3 * mixed), blocks(3 * PIECES + 3 * mixed), blocks(3 * PIECES + 3 * mixed),
            tiles(16), tiles(1, 8), tiles(4), tiles(3), tiles(3), tiles(1),
            dma((10,)), dma((3,)), dma((24,)), dma((2, 16)), dma((2,)),
        ] + gather_sems(PIECES) + gather_sems(1) + reducer_sems(PIECES) + reducer_sems(1),
        compiler_params=pltpu.CompilerParams(collective_id=0, has_side_effects=True, vmem_limit_bytes=VMEM_LIMIT),
    )(tokens, cotangent, small, lens, *weights)


def unpack_kernel(sums, small, hid, gin, *outs):
    (o_hid, o_gin, o_q, o_k, o_v, o_bq, o_bv, o_o, o_bo, o_g1, o_s1, o_up, o_bup, o_down, o_bdown, o_g2, o_s2) = outs
    o_hid[...] = hid[...]
    o_gin[...] = gin[...]
    for ref, c in ((o_q, 9), (o_k, 10), (o_v, 11), (o_o, 8)):
        ref[...] = sums[c]
    for i in range(4):
        o_down[i * ROWS:(i + 1) * ROWS] = sums[i]
        o_up[:, i * 1024:(i + 1) * 1024] = sums[4 + i]
    for i, ref in enumerate((o_bq, o_bv, o_bo, o_g1, o_s1, o_bdown, o_g2, o_s2)):
        ref[...] = small[i, 128:160]
    o_bup[...] = small[8, 0:128]


def unpack(sums, small, hid, gin):
    vmem = pl.BlockSpec(memory_space=pltpu.VMEM)
    block, vector = shaped((ROWS, 1024), F32), shaped((32,), F32)
    return pl.pallas_call(
        unpack_kernel,
        out_shape=(
            shaped(hid.shape, BF16), shaped(gin.shape, F32), block, block, block, vector, vector, block, vector, vector, vector,
            shaped((ROWS, 4096), F32), shaped((128,), F32), shaped((128, 1024), F32), vector, vector, vector,
        ),
        in_specs=[vmem] * 4,
        out_specs=(vmem,) * 17,
        compiler_params=pltpu.CompilerParams(vmem_limit_bytes=VMEM_LIMIT),
    )(sums, small, hid, gin)


def fast_body(hidden_in, lengths, w_query, w_key, w_value, b_query, b_value, w_out, b_out, first_gain, first_shift,
              w_up, b_up, w_down, b_down, second_gain, second_shift, cotangent):
    tokens = hidden_in.reshape(128, 1024)
    me = lax.axis_index("bucket") * 8 + lax.axis_index("ctx")
    rows = jnp.stack([b_query, b_value, b_out, first_gain, first_shift, b_down, second_gain, second_shift])
    spread = jnp.concatenate([jnp.where(me % 4 == q, rows, jnp.zeros_like(rows)) for q in range(4)], axis=1)
    small = jnp.concatenate([spread, b_up[None], jnp.zeros((7, 128), BF16)], axis=0)
    _, hidden_out, grad_in, sums, small_sums = layer(
        tokens, cotangent.reshape(128, 1024), small, lengths.reshape(8), (w_query, w_key, w_value, w_out, w_up, w_down)
    )
    outs = unpack(sums, small_sums, hidden_out, grad_in)
    return (outs[0].reshape(hidden_in.shape), outs[1].reshape(hidden_in.shape)) + tuple(outs[2:])


def matmul(left, right):
    return jnp.dot(left, right, preferred_element_type=jnp.float32)


def row_inner(left, right):
    return lax.dot_general(
        left, right, (((0,), (0,)), ((), ())), preferred_element_type=jnp.float32
    )


def right_inner(left, right):
    return lax.dot_general(
        left, right, (((1,), (1,)), ((), ())), preferred_element_type=jnp.float32
    )


def rounded(values):
    return values.astype(jnp.bfloat16)


def widened(values):
    return values.astype(jnp.float32)


def norm_forward(summed, gain_vec, shift_vec):
    average = jnp.mean(summed, axis=-1, keepdims=True)
    centred = summed - average
    variance = jnp.mean(centred * centred, axis=-1, keepdims=True)
    inv_std = lax.rsqrt(variance + EPSILON)
    normed = centred * inv_std
    return (normed * gain_vec + shift_vec, normed, inv_std)


def norm_backward(incoming, normed, inv_std, gain_vec):
    scaled = incoming * gain_vec
    inner = (
        scaled
        - jnp.mean(scaled, axis=-1, keepdims=True)
        - normed * jnp.mean(scaled * normed, axis=-1, keepdims=True)
    )
    return (inv_std * inner, jnp.sum(incoming * normed, axis=0), jnp.sum(incoming, axis=0))


def plain_gelu_value(values):
    return 0.5 * values * (1.0 + jax.scipy.special.erf(values * 0.7071067811865476))


def plain_gelu_slope(values):
    return (
        0.5 * (1.0 + jax.scipy.special.erf(values * 0.7071067811865476))
        + values * jnp.exp(-0.5 * values * values) * 0.3989422804014327
    )


def split_heads(values):
    return values.reshape(values.shape[0], values.shape[1], values.shape[2] // HEAD_DIM, HEAD_DIM)


def seq_mask(seq_info, query_pos, key_pos):
    seq_lens, slot_len = seq_info
    query_seq = query_pos // slot_len
    key_seq = key_pos // slot_len
    seq_ids = jnp.arange(seq_lens.shape[1], dtype=jnp.int32)
    picked = (key_seq[:, None] == seq_ids[None, :]).astype(jnp.int32)
    key_limit = jnp.sum(picked[None, :, :] * seq_lens[:, None, :], axis=-1)
    key_valid = (key_pos - key_seq * slot_len)[None, :] < key_limit
    same_seq = query_seq[:, None] == key_seq[None, :]
    return (same_seq[None, :, :] & key_valid[:, None, :])[:, None, :, :]


def score_block(query4, key4, query_start, key_start, seq_info):
    raw = jnp.einsum(
        "sqhd,skhd->shqk", query4, key4, preferred_element_type=jnp.float32
    ) * HEAD_DIM ** (-0.5)
    query_pos = query_start + jnp.arange(query4.shape[1], dtype=jnp.int32)
    key_pos = key_start + jnp.arange(key4.shape[1], dtype=jnp.int32)
    allowed = seq_mask(seq_info, query_pos, key_pos)
    return (jnp.where(allowed, raw, NEG_FILL), allowed)


def over_blocks(block_step, running, pieces):
    length_here = pieces[0].shape[1]
    block_len = math.gcd(length_here, 512)
    turn_count = length_here // block_len

    def advance(turn_no, current):
        offset = turn_no * block_len
        sliced = tuple(
            (lax.dynamic_slice_in_dim(piece_arr, offset, block_len, 1) for piece_arr in pieces)
        )
        return block_step(current, sliced, offset)

    return lax.fori_loop(0, turn_count, advance, running)


def general_body(
    hidden_in,
    lengths,
    w_query,
    w_key,
    w_value,
    b_query,
    b_value,
    w_out,
    b_out,
    first_gain,
    first_shift,
    w_up,
    b_up,
    w_down,
    b_down,
    second_gain,
    second_shift,
    cotangent,
):
    shards = (
        w_query,
        w_key,
        w_value,
        b_query,
        b_value,
        w_out,
        b_out,
        first_gain,
        first_shift,
        w_up,
        b_up,
        w_down,
        b_down,
        second_gain,
        second_shift,
    )
    gathered = (
        lax.all_gather(shards[0], ("bucket", "ctx"), axis=0, tiled=True),
        lax.all_gather(shards[1], ("bucket", "ctx"), axis=0, tiled=True),
        lax.all_gather(shards[2], ("bucket", "ctx"), axis=0, tiled=True),
        lax.all_gather(shards[3], ("bucket", "ctx"), axis=0, tiled=True),
        lax.all_gather(shards[4], ("bucket", "ctx"), axis=0, tiled=True),
        lax.all_gather(shards[5], ("bucket", "ctx"), axis=0, tiled=True),
        lax.all_gather(shards[6], ("bucket", "ctx"), axis=0, tiled=True),
        lax.all_gather(shards[7], ("bucket", "ctx"), axis=0, tiled=True),
        lax.all_gather(shards[8], ("bucket", "ctx"), axis=0, tiled=True),
        lax.all_gather(shards[9], ("bucket", "ctx"), axis=0, tiled=True),
        lax.all_gather(shards[10], ("bucket", "ctx"), axis=0, tiled=True),
        lax.all_gather(shards[11], ("bucket", "ctx"), axis=0, tiled=True),
        lax.all_gather(shards[12], ("bucket", "ctx"), axis=0, tiled=True),
        lax.all_gather(shards[13], ("bucket", "ctx"), axis=0, tiled=True),
        lax.all_gather(shards[14], ("bucket", "ctx"), axis=0, tiled=True),
    )
    (
        query_mat,
        key_mat,
        value_mat,
        query_bias,
        value_bias,
        out_mat,
        out_bias,
        gain_one,
        shift_one,
        up_mat,
        up_bias,
        down_mat,
        down_bias,
        gain_two,
        shift_two,
    ) = gathered
    seq_count = hidden_in.shape[1]
    local_rows = hidden_in.shape[2]
    model_width = hidden_in.shape[3]
    head_count = model_width // HEAD_DIM
    total_rows = seq_count * local_rows
    block_shape = (seq_count, local_rows, model_width)
    score_scale = HEAD_DIM ** (-0.5)
    seq_total = local_rows * lax.axis_size("ctx")
    group_index = lax.axis_index("bucket")
    seq_slots = jnp.right_shift(jnp.int32(lengths.shape[2]), group_index)
    slot_len = jnp.int32(seq_total) // seq_slots
    seq_info = (lengths[0], slot_len)
    own_start = lax.axis_index("ctx") * local_rows
    tokens = hidden_in.reshape(total_rows, model_width)
    query_low = rounded(matmul(tokens, query_mat) + widened(query_bias))
    key_low = rounded(matmul(tokens, key_mat))
    value_low = rounded(matmul(tokens, value_mat) + widened(value_bias))
    query_heads = split_heads(query_low.reshape(block_shape))
    key_rows = key_low.reshape(block_shape)
    value_rows = value_low.reshape(block_shape)

    def stats_step(running, sliced, anchor):
        scores, allowed = score_block(
            query_heads, split_heads(sliced[0]), own_start, anchor, seq_info
        )
        run_max, run_total = running
        new_max = jnp.maximum(run_max, jnp.max(scores, axis=-1))
        raised = jnp.where(allowed, jnp.exp(scores - new_max[..., None]), 0.0)
        return (new_max, run_total * jnp.exp(run_max - new_max) + jnp.sum(raised, axis=-1))

    stat_shape = (seq_count, head_count, local_rows)
    stats_start = (jnp.full(stat_shape, NEG_FILL, jnp.float32), jnp.zeros(stat_shape, jnp.float32))
    run_max, run_total = over_blocks(
        stats_step, stats_start, (lax.all_gather(key_rows, "ctx", axis=1, tiled=True),)
    )
    log_total = run_max + jnp.log(run_total)

    def output_step(running, sliced, anchor):
        key4 = split_heads(sliced[0])
        value4 = split_heads(sliced[1])
        scores, allowed = score_block(query_heads, key4, own_start, anchor, seq_info)
        probs_low = rounded(jnp.where(allowed, jnp.exp(scores - log_total[..., None]), 0.0))
        return running + jnp.einsum(
            "shqk,skhd->sqhd", probs_low, value4, preferred_element_type=jnp.float32
        )

    attended_f32 = over_blocks(
        output_step,
        jnp.zeros(query_heads.shape, jnp.float32),
        (
            lax.all_gather(key_rows, "ctx", axis=1, tiled=True),
            lax.all_gather(value_rows, "ctx", axis=1, tiled=True),
        ),
    )
    attended_low = rounded(attended_f32.reshape(total_rows, model_width))
    branch = matmul(attended_low, out_mat) + widened(out_bias)
    middle, normed_one, inv_one = norm_forward(
        widened(tokens) + branch, widened(gain_one), widened(shift_one)
    )
    middle_low = rounded(middle)
    pre_act = matmul(middle_low, up_mat) + widened(up_bias)
    activated = rounded(plain_gelu_value(pre_act))
    ffn_out = matmul(activated, down_mat) + widened(down_bias)
    result, normed_two, inv_two = norm_forward(
        middle + ffn_out, widened(gain_two), widened(shift_two)
    )
    hidden_out = rounded(result).reshape(hidden_in.shape)
    gathered = (
        lax.all_gather(shards[0], ("bucket", "ctx"), axis=0, tiled=True),
        lax.all_gather(shards[1], ("bucket", "ctx"), axis=0, tiled=True),
        lax.all_gather(shards[2], ("bucket", "ctx"), axis=0, tiled=True),
        lax.all_gather(shards[3], ("bucket", "ctx"), axis=0, tiled=True),
        lax.all_gather(shards[4], ("bucket", "ctx"), axis=0, tiled=True),
        lax.all_gather(shards[5], ("bucket", "ctx"), axis=0, tiled=True),
        lax.all_gather(shards[6], ("bucket", "ctx"), axis=0, tiled=True),
        lax.all_gather(shards[7], ("bucket", "ctx"), axis=0, tiled=True),
        lax.all_gather(shards[8], ("bucket", "ctx"), axis=0, tiled=True),
        lax.all_gather(shards[9], ("bucket", "ctx"), axis=0, tiled=True),
        lax.all_gather(shards[10], ("bucket", "ctx"), axis=0, tiled=True),
        lax.all_gather(shards[11], ("bucket", "ctx"), axis=0, tiled=True),
        lax.all_gather(shards[12], ("bucket", "ctx"), axis=0, tiled=True),
        lax.all_gather(shards[13], ("bucket", "ctx"), axis=0, tiled=True),
        lax.all_gather(shards[14], ("bucket", "ctx"), axis=0, tiled=True),
    )
    query_mat = gathered[0]
    key_mat = gathered[1]
    value_mat = gathered[2]
    out_mat = gathered[5]
    gain_one = gathered[7]
    up_mat = gathered[9]
    down_mat = gathered[11]
    gain_two = gathered[13]
    incoming = widened(cotangent.reshape(total_rows, model_width))
    grad_two_sum, grad_second_gain, grad_second_shift = norm_backward(
        incoming, normed_two, inv_two, widened(gain_two)
    )
    grad_ffn = rounded(grad_two_sum)
    grad_b_down = jnp.sum(widened(grad_ffn), axis=0)
    grad_w_down = row_inner(activated, grad_ffn)
    grad_act = widened(rounded(right_inner(grad_ffn, down_mat)))
    grad_pre = rounded(grad_act * plain_gelu_slope(pre_act))
    grad_b_up = jnp.sum(widened(grad_pre), axis=0)
    grad_w_up = row_inner(middle_low, grad_pre)
    grad_middle = grad_two_sum + widened(rounded(right_inner(grad_pre, up_mat)))
    grad_one_sum, grad_first_gain, grad_first_shift = norm_backward(
        grad_middle, normed_one, inv_one, widened(gain_one)
    )
    grad_branch = rounded(grad_one_sum)
    grad_b_out = jnp.sum(widened(grad_branch), axis=0)
    grad_w_out = row_inner(attended_low, grad_branch)
    grad_att = rounded(right_inner(grad_branch, out_mat)).reshape(block_shape)
    grad_att_heads = split_heads(grad_att)
    delta = jnp.einsum("sqhd,sqhd->shq", widened(grad_att_heads), attended_f32)

    def grad_terms(query4, key4, value4, att4, row_log, row_delta, query_start, key_start):
        scores, allowed = score_block(query4, key4, query_start, key_start, seq_info)
        probs = jnp.where(allowed, jnp.exp(scores - row_log[..., None]), 0.0)
        slope = jnp.einsum("sqhd,skhd->shqk", att4, value4, preferred_element_type=jnp.float32)
        return (rounded(probs), rounded(probs * (slope - row_delta[..., None])))

    def query_step(running, sliced, anchor):
        key4 = split_heads(sliced[0])
        value4 = split_heads(sliced[1])
        probs_low, score_grad = grad_terms(
            query_heads, key4, value4, grad_att_heads, log_total, delta, own_start, anchor
        )
        return (
            running
            + jnp.einsum("shqk,skhd->sqhd", score_grad, key4, preferred_element_type=jnp.float32)
            * score_scale
        )

    grad_q = over_blocks(
        query_step,
        jnp.zeros(query_heads.shape, jnp.float32),
        (
            lax.all_gather(key_rows, "ctx", axis=1, tiled=True),
            lax.all_gather(value_rows, "ctx", axis=1, tiled=True),
        ),
    )
    log_all, delta_all = (
        lax.all_gather(log_total, "ctx", axis=2, tiled=True),
        lax.all_gather(delta, "ctx", axis=2, tiled=True),
    )
    own_keys = split_heads(key_rows)
    own_values = split_heads(value_rows)

    def owner_step(running, sliced, anchor):
        query4 = split_heads(sliced[0])
        att4 = split_heads(sliced[1])
        count_here = sliced[0].shape[1]
        row_log = lax.dynamic_slice_in_dim(log_all, anchor, count_here, 2)
        row_delta = lax.dynamic_slice_in_dim(delta_all, anchor, count_here, 2)
        probs_low, score_grad = grad_terms(
            query4, own_keys, own_values, att4, row_log, row_delta, anchor, own_start
        )
        grad_k, grad_v = running
        grad_k = (
            grad_k
            + jnp.einsum("shqk,sqhd->skhd", score_grad, query4, preferred_element_type=jnp.float32)
            * score_scale
        )
        grad_v = grad_v + jnp.einsum(
            "shqk,sqhd->skhd", probs_low, att4, preferred_element_type=jnp.float32
        )
        return (grad_k, grad_v)

    owner_start = (jnp.zeros(own_keys.shape, jnp.float32), jnp.zeros(own_keys.shape, jnp.float32))
    grad_k_own, grad_v_own = over_blocks(
        owner_step,
        owner_start,
        (
            lax.all_gather(query_low.reshape(block_shape), "ctx", axis=1, tiled=True),
            lax.all_gather(grad_att, "ctx", axis=1, tiled=True),
        ),
    )
    grad_q_low = rounded(grad_q.reshape(total_rows, model_width))
    grad_k_low = rounded(grad_k_own.reshape(total_rows, model_width))
    grad_v_low = rounded(grad_v_own.reshape(total_rows, model_width))
    grad_w_query = row_inner(tokens, grad_q_low)
    grad_b_query = jnp.sum(widened(grad_q_low), axis=0)
    grad_w_key = row_inner(tokens, grad_k_low)
    grad_w_value = row_inner(tokens, grad_v_low)
    grad_b_value = jnp.sum(widened(grad_v_low), axis=0)
    grad_in = (
        grad_one_sum
        + right_inner(grad_q_low, query_mat)
        + right_inner(grad_k_low, key_mat)
        + right_inner(grad_v_low, value_mat)
    )
    owned = (
        lax.psum_scatter(grad_w_query, ("bucket", "ctx"), scatter_dimension=0, tiled=True),
        lax.psum_scatter(grad_w_key, ("bucket", "ctx"), scatter_dimension=0, tiled=True),
        lax.psum_scatter(grad_w_value, ("bucket", "ctx"), scatter_dimension=0, tiled=True),
        lax.psum_scatter(grad_b_query, ("bucket", "ctx"), scatter_dimension=0, tiled=True),
        lax.psum_scatter(grad_b_value, ("bucket", "ctx"), scatter_dimension=0, tiled=True),
        lax.psum_scatter(grad_w_out, ("bucket", "ctx"), scatter_dimension=0, tiled=True),
        lax.psum_scatter(grad_b_out, ("bucket", "ctx"), scatter_dimension=0, tiled=True),
        lax.psum_scatter(grad_first_gain, ("bucket", "ctx"), scatter_dimension=0, tiled=True),
        lax.psum_scatter(grad_first_shift, ("bucket", "ctx"), scatter_dimension=0, tiled=True),
        lax.psum_scatter(grad_w_up, ("bucket", "ctx"), scatter_dimension=0, tiled=True),
        lax.psum_scatter(grad_b_up, ("bucket", "ctx"), scatter_dimension=0, tiled=True),
        lax.psum_scatter(grad_w_down, ("bucket", "ctx"), scatter_dimension=0, tiled=True),
        lax.psum_scatter(grad_b_down, ("bucket", "ctx"), scatter_dimension=0, tiled=True),
        lax.psum_scatter(grad_second_gain, ("bucket", "ctx"), scatter_dimension=0, tiled=True),
        lax.psum_scatter(grad_second_shift, ("bucket", "ctx"), scatter_dimension=0, tiled=True),
    )
    return (hidden_out, grad_in.reshape(hidden_in.shape)) + tuple(owned)


def solution(mesh):
    placed = (
        P("bucket", None, "ctx", None),
        P("bucket", None, None),
        P(("bucket", "ctx"), None),
        P(("bucket", "ctx"), None),
        P(("bucket", "ctx"), None),
        P(("bucket", "ctx")),
        P(("bucket", "ctx")),
        P(("bucket", "ctx"), None),
        P(("bucket", "ctx")),
        P(("bucket", "ctx")),
        P(("bucket", "ctx")),
        P(("bucket", "ctx"), None),
        P(("bucket", "ctx")),
        P(("bucket", "ctx"), None),
        P(("bucket", "ctx")),
        P(("bucket", "ctx")),
        P(("bucket", "ctx")),
        P("bucket", None, "ctx", None),
    )
    def body(*arguments):
        here = dict(mesh.shape) == {"bucket": 4, "ctx": 8}
        shapes = arguments[0].shape == (1, 1, 128, 1024) and arguments[11].shape == (32, 4096)
        return (fast_body if here and shapes else general_body)(*arguments)

    return jax.shard_map(
        body,
        mesh=mesh,
        in_specs=placed,
        out_specs=(
            P("bucket", None, "ctx", None),
            P("bucket", None, "ctx", None),
            P(("bucket", "ctx"), None),
            P(("bucket", "ctx"), None),
            P(("bucket", "ctx"), None),
            P(("bucket", "ctx")),
            P(("bucket", "ctx")),
            P(("bucket", "ctx"), None),
            P(("bucket", "ctx")),
            P(("bucket", "ctx")),
            P(("bucket", "ctx")),
            P(("bucket", "ctx"), None),
            P(("bucket", "ctx")),
            P(("bucket", "ctx"), None),
            P(("bucket", "ctx")),
            P(("bucket", "ctx")),
            P(("bucket", "ctx")),
        ),
        check_vma=False,
    )
```

```python
import math

import jax
import jax.numpy as jnp
from jax import lax
from jax.experimental import pallas as pl
from jax.experimental.pallas import tpu as pltpu
from jax.sharding import PartitionSpec as P

HEAD_DIM = 64
EPSILON = 1e-05
NEG_FILL = -1e30
MESH_ID = pl.DeviceIdType.MESH
F32, BF16 = jnp.float32, jnp.bfloat16
ROWS = 32
PIECES = 12
VMEM_LIMIT = 63 * 2**20


def when(condition):
    return pl.when(condition)


def place():
    bucket, ctx = lax.axis_index("bucket"), lax.axis_index("ctx")
    return bucket // 2, ctx % 2, ctx // 2, bucket % 2


def device(x, y, z, core):
    return (x * 2 + core, z * 2 + y)


def owner(x, y, z, core):
    return (x * 2 + core) * 8 + z * 2 + y


def remote(src, dst, send_sem, recv_sem, target):
    return pltpu.make_async_remote_copy(
        src_ref=src, dst_ref=dst, send_sem=send_sem, recv_sem=recv_sem,
        device_id=target, device_id_type=MESH_ID,
    )


def bytes_of(ref, sem):
    return pltpu.make_async_copy(ref, ref, sem)


class Roles:
    def __init__(self, route, b_along_x):
        x, y, z, core = route.x, route.y, route.z, route.core
        self.ax, self.ay = jnp.where(b_along_x, x, 1 - x), jnp.where(b_along_x, 1 - y, y)
        self.bx, self.by = jnp.where(b_along_x, 1 - x, x), jnp.where(b_along_x, y, 1 - y)
        self.a = device(self.ax, self.ay, z, core)
        self.b = device(self.bx, self.by, z, core)


class Route:
    def __init__(self):
        self.x, self.y, self.z, self.core = x, y, z, core = place()
        self.across = (device(1 - x, y, z, core), device(x, 1 - y, z, core))
        self.sibling = device(x, y, z, 1 - core)
        self.up = device(x, y, jnp.minimum(z + 1, 3), core)
        self.down = device(x, y, jnp.maximum(z - 1, 0), core)

    def roles(self, turned):
        return Roles(self, (self.core == 1) | turned)

    def greet(self):
        z = self.z
        bucket, ctx = lax.axis_index("bucket"), lax.axis_index("ctx")
        barrier = pltpu.get_barrier_semaphore()
        pack = [(bucket, (ctx + off) % 8) for off in range(1, 8)]
        for target in [*self.across, self.sibling] + pack:
            pl.semaphore_signal(barrier, inc=1, device_id=target, device_id_type=MESH_ID)

        @when(z < 3)
        def _():
            pl.semaphore_signal(barrier, inc=1, device_id=self.up, device_id_type=MESH_ID)

        @when(z > 0)
        def _():
            pl.semaphore_signal(barrier, inc=1, device_id=self.down, device_id_type=MESH_ID)

        pl.semaphore_wait(barrier, 10 + (z < 3).astype(jnp.int32) + (z > 0).astype(jnp.int32))


class Plan:
    def __init__(self, count, mixed, turned, direct):
        self.count, self.which_mixed, self.which_turned, self.which_direct = count, mixed, turned, direct

    def direct(self, c):
        return self.member(c, self.which_direct)

    def chained(self, c):
        return ~(self.mixed(c) | self.direct(c))

    def mixed(self, c):
        return self.member(c, self.which_mixed)

    def turned(self, c):
        return self.member(c, self.which_turned)

    def mixed_before(self, c):
        return sum((c > item).astype(jnp.int32) for item in self.which_mixed)

    @staticmethod
    def member(c, items):
        hit = jnp.bool_(False)
        for item in items:
            hit = hit | (c == item)
        return hit


class Gatherer:
    stages = 7

    def __init__(self, route, plan, own, block, span, sems):
        self.rt, self.plan, self.own, self.block, self.span = route, plan, own, block, span
        (self.zs, self.zr, self.ps, self.ar, self.br, self.dr, self.ls) = sems

    def spread(self, c, src, j, jz, ro, to_a, to_b, z_dirs):
        rt, dst = self.rt, self.block(c, j)
        which, directions = z_dirs
        if "line" in directions:
            for slot in range(3):
                target = device(rt.x, rt.y, (rt.z + slot + 1) % 4, rt.core)
                remote(src, dst, self.zs.at[0, c, which, slot], self.zr.at[c, which, jz], target).start()

        if "up" in directions:

            @when(rt.z < 3)
            def _():
                remote(src, dst, self.zs.at[0, c, which, jz], self.zr.at[c, which, jz], rt.up).start()

        if "down" in directions:

            @when(rt.z > 0)
            def _():
                remote(src, dst, self.zs.at[1, c, which, jz], self.zr.at[c, which, jz], rt.down).start()

        if to_b is not None:
            remote(src, dst, self.ps, self.br.at[c, to_b * 4 + jz], ro.b).start()
        if to_a is not None:

            @when(to_a)
            def _():
                remote(src, dst, self.ps, self.ar.at[c, jz], ro.a).start()

        remote(src, dst, self.ps, self.dr.at[c], rt.sibling).start()

    def near(self, k, action):
        for sign in (0,) if k == 0 else (-1, 1):
            zz = self.rt.z + sign * k

            @when((zz >= 0) & (zz <= 3))
            def _():
                action(zz, "up" if sign < 0 else "down")

    def own_stage(self, c):
        rt, ro = self.rt, self.rt.roles(self.plan.turned(c))
        j = owner(rt.x, rt.y, rt.z, rt.core)
        pltpu.make_async_copy(self.own(c), self.block(c, j), self.ls.at[c]).start()
        direct = self.plan.direct(c)

        @when(direct)
        def _():
            self.spread(c, self.own(c), j, rt.z, ro, jnp.bool_(True), 0, (0, ("line",)))

        @when(~direct)
        def _():
            self.spread(c, self.own(c), j, rt.z, ro, jnp.bool_(True), 0, (0, ("up", "down")))

    def z_stage(self, c, k):
        rt, ro = self.rt, self.rt.roles(self.plan.turned(c))

        def action(zz, direction):
            j = owner(rt.x, rt.y, zz, rt.core)
            bytes_of(self.block(c, j), self.zr.at[c, 0, zz]).wait()

            @when(self.plan.direct(c))
            def _():
                self.spread(c, self.block(c, j), j, zz, ro, jnp.bool_(True), 0, (0, ()))

            @when(~self.plan.direct(c))
            def _():
                self.spread(c, self.block(c, j), j, zz, ro, ~self.plan.mixed(c), 0, (0, (direction,)))


        self.near(k, action)

    def z_stage_of_a(self, c, k):
        rt, ro = self.rt, self.rt.roles(self.plan.turned(c))

        def action(zz, direction):
            j = owner(ro.ax, ro.ay, zz, rt.core)
            bytes_of(self.block(c, j), self.zr.at[c, 1, zz]).wait()
            self.spread(c, self.block(c, j), j, zz, ro, None, 1, (1, (direction,)))

        self.near(k, action)

    def a_stage(self, c, k, directions=()):
        rt, ro = self.rt, self.rt.roles(self.plan.turned(c))

        def action(zz, _):
            j = owner(ro.ax, ro.ay, zz, rt.core)
            bytes_of(self.block(c, j), self.ar.at[c, zz]).wait()
            self.spread(c, self.block(c, j), j, zz, ro, None, 1, (1, directions))

        self.near(k, action)

    def b_stage(self, c, k):
        rt, ro = self.rt, self.rt.roles(self.plan.turned(c))

        def action(zz, _):
            for which, (xx, yy) in enumerate(((ro.bx, ro.by), (1 - rt.x, 1 - rt.y))):
                j = owner(xx, yy, zz, rt.core)
                bytes_of(self.block(c, j), self.br.at[c, which * 4 + zz]).wait()
                self.spread(c, self.block(c, j), j, zz, ro, None, None, (0, ()))

        self.near(k, action)

    def stage(self, s, c):
        mixed, direct = self.plan.mixed(c), self.plan.direct(c)
        if s == 0:
            self.own_stage(c)

        @when(direct)
        def _():
            for k in range(1, 4):
                if s == 1:
                    self.z_stage(c, k)
            for k in range(4):
                if s == 2:
                    self.a_stage(c, k)
                if s == 3:
                    self.b_stage(c, k)

        @when(~direct)
        def _():
            if 1 <= s <= 3:
                self.z_stage(c, s)
            if s == 1:

                @when(mixed)
                def _():
                    self.a_stage(c, 0, ("up", "down"))

                @when(~mixed)
                def _():
                    self.a_stage(c, 0)

            if 2 <= s <= 4:

                @when(mixed)
                def _():
                    self.z_stage_of_a(c, s - 1)

                @when(~mixed)
                def _():
                    self.a_stage(c, s - 1)

            if 3 <= s <= 6:
                self.b_stage(c, s - 3)

    def arrived(self, c):
        bytes_of(self.span(16), self.dr.at[c]).wait()
        bytes_of(self.span(1), self.ls.at[c]).wait()

    def finish(self):
        bytes_of(self.span(28 * self.plan.count - 3 * len(self.plan.which_mixed)), self.ps).wait()

    def finish_z(self, c):
        rt = self.rt

        def sent(which):
            for zz in range(4):

                @when((rt.z < 3) & (rt.z >= zz))
                def _():
                    bytes_of(self.span(1), self.zs.at[0, c, which, zz]).wait()

                @when((rt.z > 0) & (rt.z <= zz))
                def _():
                    bytes_of(self.span(1), self.zs.at[1, c, which, zz]).wait()

        @when(self.plan.direct(c))
        def _():
            for slot in range(3):
                bytes_of(self.span(1), self.zs.at[0, c, 0, slot]).wait()

        @when(~self.plan.direct(c))
        def _():
            sent(0)

        @when(self.plan.mixed(c))
        def _():
            sent(1)


def gather_sems(count):
    dma = pltpu.SemaphoreType.DMA
    return [dma((2, count, 2, 4)), dma((count, 2, 4)), dma(()), dma((count, 4)), dma((count, 8)), dma((count,)), dma((count,))]


def outer(left, right):
    return lax.dot_general(left, right, (((0,), (0,)), ((), ())), preferred_element_type=F32)


def inner(left, right):
    return lax.dot_general(left, right, (((1,), (1,)), ((), ())), preferred_element_type=F32)


def dense(left, right):
    return jnp.dot(left, right, preferred_element_type=F32)


def head_mask(shape, head):
    lane = lax.broadcasted_iota(jnp.int32, shape, len(shape) - 1)
    return (lane // HEAD_DIM) == head


def only_head(values, head):
    return jnp.where(head_mask(values.shape, head), values, jnp.zeros_like(values))


def key_sequences(len_ref, shift, keys):
    pos = lax.broadcasted_iota(jnp.int32, (keys, 128), 0)
    seq = lax.shift_right_logical(pos, shift)
    at = pos - lax.shift_left(seq, shift)
    limit = jnp.zeros((keys, 128), jnp.int32)
    for s in range(8):
        limit = jnp.where(seq == s, len_ref[s], limit)
    return jnp.where(at < limit, seq, -1)


def key_bias(kseq, shift, start, width):
    keys = kseq.shape[0]
    qseq = lax.shift_right_logical(start + lax.broadcasted_iota(jnp.int32, (1, 128), 1), shift)
    parts = []
    for w in range(width // 128):
        qs = lax.shift_right_logical(start + w * 128 + lax.broadcasted_iota(jnp.int32, (1, 128), 1), shift)
        parts.append(jnp.where(kseq == qs, 0.0, NEG_FILL))
    return jnp.concatenate(parts, axis=1)


class Swap:
    def __init__(self):
        self.bucket, self.me = lax.axis_index("bucket"), lax.axis_index("ctx")

    def heads_out(self, tokens, heads, send_sem, recv_sem, local_sem):
        rows = pl.ds(pl.multiple_of(self.me * 128, 128), 128)
        for off in (4, 3, 5, 2, 6, 1, 7):
            d = (self.me + off) % 8
            remote(tokens.at[:, pl.ds(pl.multiple_of(d * 128, 128), 128)], heads.at[rows], send_sem, recv_sem, (self.bucket, d)).start()
        pltpu.make_async_copy(tokens.at[:, pl.ds(pl.multiple_of(self.me * 128, 128), 128)], heads.at[rows], local_sem).start()

    def heads_back(self, heads, tokens, send_sem, recv_sem, local_sem):
        cols = pl.ds(pl.multiple_of(self.me * 128, 128), 128)
        for off in (4, 3, 5, 2, 6, 1, 7):
            d = (self.me + off) % 8
            remote(heads.at[pl.ds(pl.multiple_of(d * 128, 128), 128)], tokens.at[:, cols], send_sem, recv_sem, (self.bucket, d)).start()
        pltpu.make_async_copy(heads.at[pl.ds(pl.multiple_of(self.me * 128, 128), 128)], tokens.at[:, cols], local_sem).start()

    def wait(self, heads, send_sem, recv_sem, local_sem):
        seven = heads.at[pl.ds(0, 7 * 128)]
        bytes_of(seven, recv_sem).wait()
        bytes_of(seven, send_sem).wait()
        bytes_of(heads.at[pl.ds(0, 128)], local_sem).wait()


Q_BLOCK = 256


def attend_block(i, shift, kseq, q, k, v, o_ref, lse_ref):
    start = i * Q_BLOCK
    rows = pl.ds(pl.multiple_of(start, Q_BLOCK), Q_BLOCK)
    bias = key_bias(kseq[...], shift, start, Q_BLOCK)
    scaled = q[rows] * jnp.asarray(HEAD_DIM ** (-0.5), BF16)
    result = []
    for h in range(2):
        s = inner(k[...], only_head(scaled, h)) + bias
        m = jnp.max(s, axis=0, keepdims=True)
        e = jnp.exp(s - m)
        total = jnp.sum(e, axis=0, keepdims=True)
        w = (e * (1.0 / total)).astype(BF16)
        lse_ref[h:h + 1, rows] = m + jnp.log(total)
        o = outer(v[...], w)
        result.append(o[h * HEAD_DIM:(h + 1) * HEAD_DIM])
    o_ref[rows] = jnp.concatenate(result, axis=0).T.astype(BF16)


def attend_back_block(i, shift, kseq, q, k, v, do, lse, dq, dk, dv):
    start = i * Q_BLOCK
    rows = pl.ds(pl.multiple_of(start, Q_BLOCK), Q_BLOCK)
    bias = key_bias(kseq[...], shift, start, Q_BLOCK)
    scaled = q[rows] * jnp.asarray(HEAD_DIM ** (-0.5), BF16)
    back = do[rows]
    result = []
    for h in range(2):
        qm, dm = only_head(scaled, h), only_head(back, h)
        p = jnp.exp(inner(k[...], qm) + bias - lse[h:h + 1, rows])
        slope = inner(v[...], dm)
        product = p * slope
        delta = jnp.sum(product, axis=0, keepdims=True)
        ds = (product - p * delta).astype(BF16)
        dv[...] += dense(p.astype(BF16), dm)
        dk[...] += dense(ds, qm)
        g = outer(k[...], ds) * (HEAD_DIM ** (-0.5))
        result.append(g[h * HEAD_DIM:(h + 1) * HEAD_DIM])
    dq[rows] = jnp.concatenate(result, axis=0).T.astype(BF16)


def table_of(t_ref):
    groups = []
    for g in range(8):
        groups.append(sum(t_ref[4 * g + i].astype(F32) for i in range(4)))
    return jnp.concatenate(groups, axis=1)


def gelu_value(values):
    return 0.5 * values * (1.0 + lax.erf(values * 0.7071067811865476))


def gelu_slope(values):
    return 0.5 * (1.0 + lax.erf(values * 0.7071067811865476)) + values * jnp.exp(-0.5 * values * values) * 0.3989422804014327


def row_mean(values):
    return jnp.mean(values, axis=-1, keepdims=True)


def column_sum(values):
    return jnp.sum(values, axis=0, keepdims=True)


def norm_parts(summed):
    centred = summed - row_mean(summed)
    inv_std = lax.rsqrt(row_mean(centred * centred) + EPSILON)
    return centred * inv_std, inv_std


def norm_back(incoming, normed, inv_std, gain):
    scaled = incoming * gain
    return inv_std * (scaled - row_mean(scaled) - normed * row_mean(scaled * normed))


V_QUERY, V_VALUE, V_OUT, V_GAIN1, V_SHIFT1, V_DOWN, V_GAIN2, V_SHIFT2 = range(8)
V_UP = 8
W_DOWN, W_UP = 4096, 8192
GATHER = Plan(PIECES, (1, 3, 4, 6, 8, 10), (4,), ())
REDUCE = Plan(PIECES, (1, 3, 6, 9), (6,), (11,))
ONE_PIECE = Plan(1, (), (), ())


def piece_row(c, j):
    tall = (c >= 4) & (c < 8)
    return pl.multiple_of(jnp.where(tall, W_DOWN + 128 * j + ROWS * (c - 4), c * 1024 + ROWS * j), ROWS)


def add_f32(left, right):
    return left.astype(F32) + right.astype(F32)


class Reducer:
    stages = 7

    def __init__(self, route, plan, own, rb, ra, ru, rn, out, sems):
        self.rt, self.plan = route, plan
        self.own, self.rb, self.ra, self.ru, self.rn, self.out = own, rb, ra, ru, rn, out
        (self.sb_s, self.sb_r, self.sa_s, self.sa_r, self.sz_s, self.su_r, self.sn_r) = sems

    @staticmethod
    def slot(xx, yy, zz):
        return xx * 8 + zz * 2 + yy

    def add(self, c, k, other):
        at = self.own(c, k)
        at[...] = add_f32(at[...], other).astype(at.dtype)

    def roles(self, c):
        return self.rt.roles(self.plan.turned(c))

    def b_blocks(self, c):
        rt, ro = self.rt, self.roles(c)
        blocks = []
        for same_a in (0, 1):
            for zz in range(4):
                xx, yy = (ro.bx, ro.by) if same_a else (1 - rt.x, 1 - rt.y)
                blocks.append((self.slot(xx, yy, zz), same_a * 4 + zz))
        return blocks

    def send_b(self, c, k, at):
        remote(self.own(c, k), self.rb.at[c, at], self.sb_s.at[c], self.sb_r.at[c, at], self.roles(c).b).start()

    def to_b(self, c):
        for k, at in self.b_blocks(c):
            self.send_b(c, k, at)

    def add_b(self, c, k, at):
        bytes_of(self.rb.at[c, at], self.sb_r.at[c, at]).wait()
        self.add(c, k, self.rb[c, at])

    def to_a(self, c):
        rt, ro = self.rt, self.roles(c)
        for zz in range(4):
            k = self.slot(ro.ax, ro.ay, zz)
            self.add_b(c, k, zz)
            remote(self.own(c, k), self.ra(c, zz), self.sa_s.at[c], self.sa_r.at[c, zz], ro.a).start()
        for zz in range(4):
            self.add_b(c, self.slot(rt.x, rt.y, zz), 4 + zz)

    def keep_b(self, c):
        rt, ro = self.rt, self.roles(c)
        for zz in range(4):
            self.add_b(c, self.slot(ro.ax, ro.ay, zz), zz)
        for zz in range(4):
            self.add_b(c, self.slot(rt.x, rt.y, zz), 4 + zz)

    def from_a(self, c):
        rt = self.rt
        for zz in range(4):
            bytes_of(self.ra(c, zz), self.sa_r.at[c, zz]).wait()
            self.add(c, self.slot(rt.x, rt.y, zz), self.ra(c, zz)[...])

    def to_line(self, c):
        rt = self.rt
        for step in range(4):
            zz = (rt.z + 1 + step) % 4
            k = self.slot(rt.x, rt.y, zz)
            bytes_of(self.ra(c, zz), self.sa_r.at[c, zz]).wait()
            self.add(c, k, self.ra(c, zz)[...])
            if step < 3:
                target = device(rt.x, rt.y, zz, rt.core)
                remote(self.own(c, k), self.ru(c, 0, step), self.sz_s.at[c, 0, step], self.su_r.at[c, 0, step], target).start()

    def total_line(self, c):
        rt = self.rt
        value = self.own(c, self.slot(rt.x, rt.y, rt.z))[...].astype(F32)
        for step in range(3):
            bytes_of(self.ru(c, 0, step), self.su_r.at[c, 0, step]).wait()
            value = value + self.ru(c, 0, step)[...].astype(F32)
        self.out[c] = value

    def along_z(self, c, hop, which):
        rt, ro = self.rt, self.roles(c)
        x, y = (ro.ax, ro.ay) if which else (rt.x, rt.y)

        @when(rt.z == hop)
        def _():
            for d in range(3, hop, -1):
                k = self.slot(x, y, d)
                at, sem = self.ru(c, which, d - 1), self.su_r.at[c, which, d - 1]
                if hop > 0:
                    bytes_of(at, sem).wait()
                    self.add(c, k, at[...])
                remote(self.own(c, k), at, self.sz_s.at[c, which, d], sem, rt.up).start()
            if hop > 0:
                bytes_of(self.ru(c, which, hop - 1), self.su_r.at[c, which, hop - 1]).wait()

        end = 3 - hop

        @when(rt.z == end)
        def _():
            for d in range(end):
                k = self.slot(x, y, d)
                at, sem = self.rn(c, which, d), self.sn_r.at[c, which, d]
                if end < 3:
                    bytes_of(at, sem).wait()
                    self.add(c, k, at[...])
                remote(self.own(c, k), at, self.sz_s.at[c, which, d], sem, rt.down).start()
            if end < 3:
                bytes_of(self.rn(c, which, end), self.sn_r.at[c, which, end]).wait()

    def sum_z(self, c, which, store):
        rt, ro = self.rt, self.roles(c)
        k = self.slot(ro.ax, ro.ay, rt.z) if which else self.slot(rt.x, rt.y, rt.z)

        @when(rt.z == 0)
        def _():
            store(k, add_f32(self.own(c, k)[...], self.rn(c, which, 0)[...]))

        @when(rt.z == 3)
        def _():
            store(k, add_f32(self.own(c, k)[...], self.ru(c, which, 2)[...]))

        for at in (1, 2):

            @when(rt.z == at)
            def _():
                store(k, add_f32(self.own(c, k)[...], self.ru(c, which, at - 1)[...]) + self.rn(c, which, at)[...].astype(F32))

    def close_a(self, c):
        ro = self.roles(c)

        def store(k, value):
            at = self.own(c, k)
            at[...] = value.astype(at.dtype)

        self.sum_z(c, 1, store)
        k = self.slot(ro.ax, ro.ay, self.rt.z)
        remote(self.own(c, k), self.ra(c, 0), self.sa_s.at[c], self.sa_r.at[c, 0], ro.a).start()

    def total(self, c, from_a):
        def store(k, value):
            if from_a:
                bytes_of(self.ra(c, 0), self.sa_r.at[c, 0]).wait()
                value = value + self.ra(c, 0)[...].astype(F32)
            self.out[c] = value

        self.sum_z(c, 0, store)

    def stage(self, s, c):
        mixed = self.plan.mixed(c)

        @when(mixed)
        def _():
            if s == 2:
                self.keep_b(c)
            if 2 <= s <= 5:
                self.along_z(c, s - 2, 1)
                self.along_z(c, s - 2, 0)
            if s == 5:
                self.close_a(c)
            if s == 6:
                self.total(c, True)

        @when(self.plan.direct(c))
        def _():
            if s == 2:
                self.to_a(c)
            if s == 3:
                self.to_line(c)
            if s == 4:
                self.total_line(c)

        @when(self.plan.chained(c))
        def _():
            if s == 2:
                self.to_a(c)
            if s == 3:
                self.from_a(c)
            if s >= 3:
                self.along_z(c, s - 3, 0)
            if s == 6:
                self.total(c, False)

    def finish(self, c):
        rt = self.rt
        bytes_of(self.rb.at[c], self.sb_s.at[c]).wait()

        def sent(which):
            for d in range(4):

                @when(rt.z != d)
                def _():
                    bytes_of(self.ra(c, 0), self.sz_s.at[c, which, d]).wait()

        @when(self.plan.direct(c))
        def _():
            for step in range(3):
                bytes_of(self.ra(c, 0), self.sz_s.at[c, 0, step]).wait()

        @when(~self.plan.direct(c))
        def _():
            sent(0)

        @when(self.plan.mixed(c))
        def _():
            sent(1)
            bytes_of(self.ra(c, 0), self.sa_s.at[c]).wait()

        @when(~self.plan.mixed(c))
        def _():
            bytes_of(self.rb.at[c, pl.ds(0, 4)], self.sa_s.at[c]).wait()


def reducer_sems(count):
    dma = pltpu.SemaphoreType.DMA
    return [dma((count,)), dma((count, 8)), dma((count,)), dma((count, 4)), dma((count, 2, 4)), dma((count, 2, 3)), dma((count, 2, 3))]


class Shared:
    def __init__(self, route, ref, sems, at, start=0):
        cols = pl.ds(start, 1024)
        self.rt, self.mine, self.other = route, ref.at[pl.ds(0, 128), cols], ref.at[pl.ds(128, 128), cols]
        self.send, self.recv = sems.at[0, at], sems.at[1, at]

    def give(self):
        remote(self.mine, self.other, self.send, self.recv, self.rt.sibling).start()

    def wait(self):
        bytes_of(self.mine, self.recv).wait()

    def sent(self):
        bytes_of(self.mine, self.send).wait()


SMALL_AT = 10
GATHER_OFFSETS = (0, 1, 2, 3, 4, 5, 6, 7)
OFFSETS = (0, 0, 3, 5, 7, 9, 11)


def layer_kernel(x_ref, cot_ref, v_ref, len_ref, wq, wk, wv, wo, wu, wd,
                 kept, hid, gin, sums, small_out,
                 w, own, tiles, qkv, oh, kseq, qh, kh, vh, doh, lse, pre, nor1, inv1, gtwo, dk, dv, table, rows2,
                 x2, att2, mid2, act2, gffn2, gpre2, gbr2, dq2, dk2, dv2,
                 rb, ra, ru, rn, v_own, v_rb, v_ra, v_ru, v_rn, v_out,
                 own_sems, kept_sems, swap_sems, shared_sems, row_sems, *sems):
    rt, swap = Route(), Swap()
    shift = 7 + swap.bucket
    g_sems, gv_sems, r_sems, rv_sems = sems[:7], sems[7:14], sems[14:21], sems[21:28]
    loads = [pltpu.make_async_copy(ref, own.at[pl.ds(i * ROWS, ROWS)], own_sems.at[i]) for i, ref in enumerate((wq, wk, wv, wo))]
    loads.append(pltpu.make_async_copy(wd, own.at[pl.ds(4 * ROWS, 4 * ROWS)], own_sems.at[4]))
    for i in range(4):
        loads.append(pltpu.make_async_copy(wu.at[:, pl.ds(i * 1024, 1024)], own.at[pl.ds((8 + i) * ROWS, ROWS)], own_sems.at[5 + i]))
    loads.append(pltpu.make_async_copy(x_ref, x2.at[pl.ds(0, 128)], own_sems.at[9]))
    for load in loads:
        load.start()
    gather = Gatherer(
        rt, GATHER,
        lambda c: own.at[pl.ds(pl.multiple_of(c * ROWS, ROWS), ROWS)],
        lambda c, j: w.at[pl.ds(piece_row(c, j), ROWS)],
        lambda n: w.at[pl.ds(0, n * ROWS)],
        g_sems,
    )
    gather_small = Gatherer(rt, ONE_PIECE, lambda c: v_ref, lambda c, j: tiles.at[j], lambda n: tiles.at[pl.ds(0, n)], gv_sems)

    def own_block(c, k):
        first = jnp.where(c < 6, c * 512, W_DOWN + (c - 6) * 512)
        return w.at[pl.ds(pl.multiple_of(first + k * ROWS, ROWS), ROWS)]

    def ra_block(c, i):
        return ra.at[4 * c - 3 * REDUCE.mixed_before(c) + i]

    def ru_block(c, which, d):
        return ru.at[3 * (c + REDUCE.mixed_before(c) + which) + d]

    def rn_block(c, which, d):
        return rn.at[3 * (c + REDUCE.mixed_before(c) + which) + d]

    reduce = Reducer(rt, REDUCE, own_block, rb, ra_block, ru_block, rn_block, sums, r_sems)
    reduce_small = Reducer(
        rt, ONE_PIECE, lambda c, k: v_own.at[k], v_rb, lambda c, i: v_ra.at[i],
        lambda c, which, d: v_ru.at[d], lambda c, which, d: v_rn.at[d], v_out, rv_sems,
    )
    sx, satt, smid, sgffn, sgbr, sdq, sdk, sdv = (
        Shared(rt, ref, shared_sems, i) for i, ref in enumerate((x2, att2, mid2, gffn2, gbr2, dq2, dk2, dv2))
    )
    sact = [Shared(rt, act2, shared_sems, 8 + i, i * 1024) for i in range(4)]
    sgpre = [Shared(rt, gpre2, shared_sems, 12 + i, i * 1024) for i in range(4)]
    rt.greet()
    for load in loads:
        load.wait()

    def vec(row):
        return table[row:row + 1]

    def trio(at):
        return tuple(swap_sems.at[3 * at + n] for n in range(3))

    def project(i):
        value = dense(x2[0:128], w[i * 1024:(i + 1) * 1024])
        if i != 1:
            value = value + vec(V_QUERY if i == 0 else V_VALUE)
        qkv[i] = value.astype(BF16)
        swap.heads_out(qkv.at[i], (qh, kh, vh)[i], *trio(i))

    def start():
        gather_small.arrived(0)
        sx.give()
        table[...] = table_of(tiles)
        for i in range(4):
            table[V_UP + i:V_UP + i + 1] = jnp.concatenate([tiles[8 * i + j][8:9].astype(F32) for j in range(8)], axis=1)
        kseq[...] = key_sequences(len_ref, shift, kseq.shape[0])
        project(0)

    def score(first):
        if first == 0:
            for i, ref in enumerate((qh, kh, vh)):
                swap.wait(ref, *trio(i))

        def block(i, _):
            attend_block(i, shift, kseq, qh, kh, vh, oh, lse)
            return 0

        lax.fori_loop(first, first + 2, block, 0)
        if first == 2:
            swap.heads_back(oh, att2.at[pl.ds(0, 128)], *trio(3))

    def first_norm():
        swap.wait(oh, *trio(3))
        satt.give()
        normed, inv = norm_parts(x2[0:128].astype(F32) + (dense(att2[0:128], w[3072:4096]) + vec(V_OUT)))
        nor1[...] = normed
        inv1[...] = inv
        mid2[0:128] = (normed * vec(V_GAIN1) + vec(V_SHIFT1)).astype(BF16)
        smid.give()
        gtwo[...] = jnp.zeros_like(gtwo)

    def up(i):
        value = dense(mid2[0:128], w[W_UP + i * 1024:W_UP + (i + 1) * 1024]) + vec(V_UP + i)
        pre[i] = value
        now = gelu_value(value).astype(BF16)
        act2[0:128, i * 1024:(i + 1) * 1024] = now
        sact[i].give()
        gtwo[...] += dense(now, w[W_DOWN + i * 1024:W_DOWN + (i + 1) * 1024])

    items = {
        0: start, 1: lambda: project(1), 2: lambda: project(2), 4: lambda: score(0), 5: lambda: score(2), 7: first_norm,
        8: lambda: up(0), 9: lambda: up(1), 10: lambda: up(2), 11: lambda: up(3),
    }

    def save(i):
        rows_of = pl.ds(pl.multiple_of(i * 1024, 1024), 1024)
        return pltpu.make_async_copy(w.at[rows_of], kept.at[rows_of], kept_sems.at[i])

    def gather_step(t, _):
        for s in range(Gatherer.stages):
            c = t - GATHER_OFFSETS[s]

            @when(c == 0)
            def _():
                gather_small.stage(s, 0)

            @when((c >= 0) & (c < PIECES))
            def _():
                gather.stage(s, c)

        c = t - GATHER_OFFSETS[-1]

        @when(c >= 0)
        def _():
            gather.arrived(c)

            @when(c < 3)
            def _():
                save(c).start()

        for k, item in items.items():

            @when(c == k)
            def _():
                item()

        return 0

    lax.fori_loop(0, PIECES + GATHER_OFFSETS[-1], gather_step, 0)
    middle = nor1[...] * vec(V_GAIN1) + vec(V_SHIFT1)
    normed2, inv2 = norm_parts(middle + (gtwo[...] + vec(V_DOWN)))
    g = cot_ref[...].astype(F32)
    back = norm_back(g, normed2, inv2, vec(V_GAIN2))
    low = back.astype(BF16)
    gffn2[0:128] = low
    sgffn.give()
    gtwo[...] = back
    hid[...] = (normed2 * vec(V_GAIN2) + vec(V_SHIFT2)).astype(BF16)
    rows2[0] = jnp.zeros(table.shape, F32)
    rows2[0, V_GAIN2:V_GAIN2 + 1] = column_sum(g * normed2)
    rows2[0, V_SHIFT2:V_SHIFT2 + 1] = column_sum(g)
    rows2[0, V_DOWN:V_DOWN + 1] = column_sum(low.astype(F32))
    gather_small.finish()
    gather_small.finish_z(0)

    def gathered(c, _):
        gather.finish_z(c)
        return 0

    lax.fori_loop(0, PIECES, gathered, 0)
    gather.finish()
    for i in range(3):
        save(i).wait()

    def tall(first):
        order = [(k, at) for k, at in reduce.b_blocks(first)]
        kept_here = []
        for same_a in (0, 1):
            for zz in range(4):
                ro = reduce.roles(first)
                xx, yy = (rt.x, rt.y) if same_a else (ro.ax, ro.ay)
                kept_here.append(reduce.slot(xx, yy, zz))

        def block(k):
            j = (k // 8) * 16 + rt.core * 8 + k % 8
            part = act2[:, pl.ds(pl.multiple_of(j * 128, 128), 128)]
            grad = outer(part, gffn2[...]).astype(BF16)
            for q in range(4):
                own_block(first + q, k)[...] = grad[q * ROWS:(q + 1) * ROWS]

        for k, at in order:
            block(k)
        for k in kept_here:
            block(k)

    def square(left, right, c):
        for xx in range(2):
            part = left[:, pl.ds(pl.multiple_of((xx * 2 + rt.core) * 256, 256), 256)]
            grad = outer(part, right).astype(BF16)
            for i in range(8):
                own_block(c, xx * 8 + i)[...] = grad[i * ROWS:(i + 1) * ROWS]

    def compute(c):
        @when(c == 0)
        def _():
            for one in sact + [sgffn]:
                one.wait()
            tall(0)

        for i in range(4):

            @when(c == 4 + i)
            def _():
                if i == 0:
                    smid.wait()
                sgpre[i].wait()

        @when((c >= 4) & (c < 8))
        def _():
            square(mid2, gpre2[:, pl.ds(pl.multiple_of((c - 4) * 1024, 1024), 1024)], c)

        for k, (left, right, lw, rw) in enumerate(
            ((att2, gbr2, satt, sgbr), (x2, dq2, sx, sdq), (x2, dk2, None, sdk), (x2, dv2, None, sdv))
        ):

            @when(c == 8 + k)
            def _():
                if lw is not None:
                    lw.wait()
                rw.wait()
                square(left, right[...], c)

        reduce.to_b(c)

    def share_rows():
        return remote(rows2.at[0], rows2.at[1], row_sems.at[0], row_sems.at[1], rt.sibling)

    def compute_small():
        bytes_of(rows2.at[1], row_sems.at[1]).wait()
        rows2[0] = rows2[0] + rows2[1]

        def one(i, _):
            j = (i // 8) * 16 + rt.core * 8 + i % 8
            v_own[i, 0:8] = rows2[0, 0:8, pl.ds(pl.multiple_of((j // 4) * 128, 128), 128)]
            ups = rows2[0, 8:16, pl.ds(pl.multiple_of((j % 8) * 128, 128), 128)]
            row = lax.broadcasted_iota(jnp.int32, (8, 128), 0)
            v_own[i, 8:16] = jnp.where(row == j // 8, ups, 0.0)
            return 0

        lax.fori_loop(0, 16, one, 0)

    def ffn_back(i):
        gact = inner(gffn2[0:128], w[W_DOWN + i * 1024:W_DOWN + (i + 1) * 1024]).astype(BF16).astype(F32)
        gpre = (gact * gelu_slope(pre[i])).astype(BF16)
        gpre2[0:128, i * 1024:(i + 1) * 1024] = gpre
        sgpre[i].give()
        rows2[0, V_UP + i:V_UP + i + 1] = column_sum(gpre.astype(F32))
        part = inner(gpre, w[W_UP + i * 1024:W_UP + (i + 1) * 1024])
        if i == 0:
            gin[...] = part
        else:
            gin[...] += part

    def load(i):
        return pltpu.make_async_copy(kept.at[pl.ds(i * 1024, 1024)], w.at[pl.ds(W_UP + i * 1024, 1024)], kept_sems.at[i])

    def ffn_end():
        for i in range(3):
            load(i).start()
        gmid = gtwo[...] + gin[...].astype(BF16).astype(F32)
        normed1 = nor1[...]
        gone = norm_back(gmid, normed1, inv1[...], vec(V_GAIN1))
        gbr = gone.astype(BF16)
        gbr2[0:128] = gbr
        qkv[0] = inner(gbr, w[3072:4096]).astype(BF16)
        swap.heads_out(qkv.at[0], doh, *trio(4))
        gin[...] = gone
        sgbr.give()
        rows2[0, V_GAIN1:V_GAIN1 + 1] = column_sum(gmid * normed1)
        rows2[0, V_SHIFT1:V_SHIFT1 + 1] = column_sum(gmid)
        rows2[0, V_OUT:V_OUT + 1] = column_sum(gbr.astype(F32))
        dk[...] = jnp.zeros_like(dk)
        dv[...] = jnp.zeros_like(dv)

    def score_back(first, count):
        if first == 0:
            swap.wait(doh, *trio(4))

        def block(i, _):
            attend_back_block(i, shift, kseq, qh, kh, vh, doh, lse, qh, dk, dv)
            return 0

        lax.fori_loop(first, first + count, block, 0)

    back_trio = ((qh, dq2, sdq), (kh, dk2, sdk), (vh, dv2, sdv))

    def score_end():
        kh[...] = dk[...].astype(BF16)
        vh[...] = dv[...].astype(BF16)
        for i, (src, dst, _) in enumerate(back_trio):
            swap.heads_back(src, dst.at[pl.ds(0, 128)], *trio(5 + i))

    def exchange():
        for i, (src, dst, shared) in enumerate(back_trio):
            swap.wait(src, *trio(5 + i))
            shared.give()
        rows2[0, V_QUERY:V_QUERY + 1] = column_sum(dq2[0:128].astype(F32))
        rows2[0, V_VALUE:V_VALUE + 1] = column_sum(dv2[0:128].astype(F32))
        share_rows().start()

    def input_grad():
        total = gin[...]
        for i, ref in enumerate((dq2, dk2, dv2)):
            load(i).wait()
            total = total + inner(ref[0:128], w[W_UP + i * 1024:W_UP + (i + 1) * 1024])
        gin[...] = total
        share_rows().wait_send()

    back_items = {
        0: (lambda: ffn_back(1),),
        1: (lambda: ffn_back(2), lambda: ffn_back(3), ffn_end),
        2: (lambda: score_back(0, 1),), 3: (lambda: score_back(1, 1),), 4: (lambda: score_back(2, 1),),
        5: (lambda: score_back(3, 1), score_end),
        7: (exchange,), 8: (input_grad,),
    }
    ffn_back(0)

    def reduce_step(t, _):
        @when(t < PIECES)
        def _():
            compute(t)

        @when(t == SMALL_AT)
        def _():
            compute_small()
            reduce_small.to_b(0)

        for s in range(Reducer.stages - 1, 1, -1):
            c = t - OFFSETS[s]

            @when((c >= 0) & (c < PIECES))
            def _():
                reduce.stage(s, c)

            @when(c == SMALL_AT)
            def _():
                reduce_small.stage(s, 0)

        for k, parts in back_items.items():

            @when(t == k)
            def _():
                for part in parts:
                    part()

        return 0

    lax.fori_loop(0, PIECES + OFFSETS[-1], reduce_step, 0)

    def reduced(c, _):
        reduce.finish(c)
        return 0

    lax.fori_loop(0, PIECES, reduced, 0)
    reduce_small.finish(0)
    for one in [sx, satt, smid, sgffn, sgbr, sdq, sdk, sdv] + sact + sgpre:
        one.sent()
    mine = v_out[0]
    quarter = owner(rt.x, rt.y, rt.z, rt.core) % 4
    picked = jnp.zeros((16, 32), F32)
    for q in range(4):
        picked = jnp.where(quarter == q, mine[:, q * 32:(q + 1) * 32], picked)
    small_out[:, 0:128] = jnp.broadcast_to(column_sum(mine[8:16]), (16, 128))
    small_out[:, 128:160] = picked


def shaped(shape, dtype):
    return jax.ShapeDtypeStruct(shape, dtype)


def layer(tokens, cotangent, small, lens, weights):
    vmem, anywhere = pl.BlockSpec(memory_space=pltpu.VMEM), pl.BlockSpec(memory_space=pl.ANY)
    dma = pltpu.SemaphoreType.DMA
    narrow, heads = (128, 1024), (1024, 128)
    half, full = pltpu.VMEM(heads, BF16), pltpu.VMEM(heads, F32)
    pair, wide_pair, tokens_f32 = pltpu.VMEM((256, 1024), BF16), pltpu.VMEM((256, 4096), BF16), pltpu.VMEM(narrow, F32)

    mixed = len(REDUCE.which_mixed)

    def blocks(*n):
        return pltpu.VMEM(n + (ROWS, 1024), BF16)

    def tiles(*n):
        return pltpu.VMEM(n + (16, 128), F32)

    return pl.pallas_call(
        layer_kernel,
        out_shape=(
            shaped((3 * 1024, 1024), BF16), shaped(narrow, BF16), shaped(narrow, F32),
            shaped((PIECES, ROWS, 1024), F32), shaped((16, 256), F32),
        ),
        in_specs=[anywhere, vmem, vmem, pl.BlockSpec(memory_space=pltpu.SMEM)] + [anywhere] * 6,
        out_specs=(anywhere,) + (vmem,) * 4,
        scratch_shapes=[
            pltpu.VMEM((PIECES * 1024, 1024), BF16), pltpu.VMEM((PIECES * ROWS, 1024), BF16), pltpu.VMEM((32, 16, 128), BF16),
            pltpu.VMEM((3, 128, 1024), BF16), half, pltpu.VMEM(heads, jnp.int32), half, half, half, half,
            pltpu.VMEM((2, 1024), F32), pltpu.VMEM((4, 128, 1024), F32), tokens_f32, pltpu.VMEM((128, 1), F32), tokens_f32,
            full, full, pltpu.VMEM((16, 1024), F32), pltpu.VMEM((2, 16, 1024), F32),
            pair, pair, pair, wide_pair, pair, wide_pair, pair, pair, pair, pair,
            blocks(PIECES, 8), blocks(4 * PIECES - 3 * mixed), blocks(3 * PIECES + 3 * mixed), blocks(3 * PIECES + 3 * mixed),
            tiles(16), tiles(1, 8), tiles(4), tiles(3), tiles(3), tiles(1),
            dma((10,)), dma((3,)), dma((24,)), dma((2, 16)), dma((2,)),
        ] + gather_sems(PIECES) + gather_sems(1) + reducer_sems(PIECES) + reducer_sems(1),
        compiler_params=pltpu.CompilerParams(collective_id=0, has_side_effects=True, vmem_limit_bytes=VMEM_LIMIT),
    )(tokens, cotangent, small, lens, *weights)


def unpack_kernel(sums, small, hid, gin, *outs):
    (o_hid, o_gin, o_q, o_k, o_v, o_bq, o_bv, o_o, o_bo, o_g1, o_s1, o_up, o_bup, o_down, o_bdown, o_g2, o_s2) = outs
    o_hid[...] = hid[...]
    o_gin[...] = gin[...]
    for ref, c in ((o_q, 9), (o_k, 10), (o_v, 11), (o_o, 8)):
        ref[...] = sums[c]
    for i in range(4):
        o_down[i * ROWS:(i + 1) * ROWS] = sums[i]
        o_up[:, i * 1024:(i + 1) * 1024] = sums[4 + i]
    for i, ref in enumerate((o_bq, o_bv, o_bo, o_g1, o_s1, o_bdown, o_g2, o_s2)):
        ref[...] = small[i, 128:160]
    o_bup[...] = small[8, 0:128]


def unpack(sums, small, hid, gin):
    vmem = pl.BlockSpec(memory_space=pltpu.VMEM)
    block, vector = shaped((ROWS, 1024), F32), shaped((32,), F32)
    return pl.pallas_call(
        unpack_kernel,
        out_shape=(
            shaped(hid.shape, BF16), shaped(gin.shape, F32), block, block, block, vector, vector, block, vector, vector, vector,
            shaped((ROWS, 4096), F32), shaped((128,), F32), shaped((128, 1024), F32), vector, vector, vector,
        ),
        in_specs=[vmem] * 4,
        out_specs=(vmem,) * 17,
        compiler_params=pltpu.CompilerParams(vmem_limit_bytes=VMEM_LIMIT),
    )(sums, small, hid, gin)


def fast_body(hidden_in, lengths, w_query, w_key, w_value, b_query, b_value, w_out, b_out, first_gain, first_shift,
              w_up, b_up, w_down, b_down, second_gain, second_shift, cotangent):
    tokens = hidden_in.reshape(128, 1024)
    me = lax.axis_index("bucket") * 8 + lax.axis_index("ctx")
    rows = jnp.stack([b_query, b_value, b_out, first_gain, first_shift, b_down, second_gain, second_shift])
    spread = jnp.concatenate([jnp.where(me % 4 == q, rows, jnp.zeros_like(rows)) for q in range(4)], axis=1)
    small = jnp.concatenate([spread, b_up[None], jnp.zeros((7, 128), BF16)], axis=0)
    _, hidden_out, grad_in, sums, small_sums = layer(
        tokens, cotangent.reshape(128, 1024), small, lengths.reshape(8), (w_query, w_key, w_value, w_out, w_up, w_down)
    )
    outs = unpack(sums, small_sums, hidden_out, grad_in)
    return (outs[0].reshape(hidden_in.shape), outs[1].reshape(hidden_in.shape)) + tuple(outs[2:])


def matmul(left, right):
    return jnp.dot(left, right, preferred_element_type=jnp.float32)


def row_inner(left, right):
    return lax.dot_general(
        left, right, (((0,), (0,)), ((), ())), preferred_element_type=jnp.float32
    )


def right_inner(left, right):
    return lax.dot_general(
        left, right, (((1,), (1,)), ((), ())), preferred_element_type=jnp.float32
    )


def rounded(values):
    return values.astype(jnp.bfloat16)


def widened(values):
    return values.astype(jnp.float32)


def norm_forward(summed, gain_vec, shift_vec):
    average = jnp.mean(summed, axis=-1, keepdims=True)
    centred = summed - average
    variance = jnp.mean(centred * centred, axis=-1, keepdims=True)
    inv_std = lax.rsqrt(variance + EPSILON)
    normed = centred * inv_std
    return (normed * gain_vec + shift_vec, normed, inv_std)


def norm_backward(incoming, normed, inv_std, gain_vec):
    scaled = incoming * gain_vec
    inner = (
        scaled
        - jnp.mean(scaled, axis=-1, keepdims=True)
        - normed * jnp.mean(scaled * normed, axis=-1, keepdims=True)
    )
    return (inv_std * inner, jnp.sum(incoming * normed, axis=0), jnp.sum(incoming, axis=0))


def plain_gelu_value(values):
    return 0.5 * values * (1.0 + jax.scipy.special.erf(values * 0.7071067811865476))


def plain_gelu_slope(values):
    return (
        0.5 * (1.0 + jax.scipy.special.erf(values * 0.7071067811865476))
        + values * jnp.exp(-0.5 * values * values) * 0.3989422804014327
    )


def split_heads(values):
    return values.reshape(values.shape[0], values.shape[1], values.shape[2] // HEAD_DIM, HEAD_DIM)


def seq_mask(seq_info, query_pos, key_pos):
    seq_lens, slot_len = seq_info
    query_seq = query_pos // slot_len
    key_seq = key_pos // slot_len
    seq_ids = jnp.arange(seq_lens.shape[1], dtype=jnp.int32)
    picked = (key_seq[:, None] == seq_ids[None, :]).astype(jnp.int32)
    key_limit = jnp.sum(picked[None, :, :] * seq_lens[:, None, :], axis=-1)
    key_valid = (key_pos - key_seq * slot_len)[None, :] < key_limit
    same_seq = query_seq[:, None] == key_seq[None, :]
    return (same_seq[None, :, :] & key_valid[:, None, :])[:, None, :, :]


def score_block(query4, key4, query_start, key_start, seq_info):
    raw = jnp.einsum(
        "sqhd,skhd->shqk", query4, key4, preferred_element_type=jnp.float32
    ) * HEAD_DIM ** (-0.5)
    query_pos = query_start + jnp.arange(query4.shape[1], dtype=jnp.int32)
    key_pos = key_start + jnp.arange(key4.shape[1], dtype=jnp.int32)
    allowed = seq_mask(seq_info, query_pos, key_pos)
    return (jnp.where(allowed, raw, NEG_FILL), allowed)


def over_blocks(block_step, running, pieces):
    length_here = pieces[0].shape[1]
    block_len = math.gcd(length_here, 512)
    turn_count = length_here // block_len

    def advance(turn_no, current):
        offset = turn_no * block_len
        sliced = tuple(
            (lax.dynamic_slice_in_dim(piece_arr, offset, block_len, 1) for piece_arr in pieces)
        )
        return block_step(current, sliced, offset)

    return lax.fori_loop(0, turn_count, advance, running)


def general_body(
    hidden_in,
    lengths,
    w_query,
    w_key,
    w_value,
    b_query,
    b_value,
    w_out,
    b_out,
    first_gain,
    first_shift,
    w_up,
    b_up,
    w_down,
    b_down,
    second_gain,
    second_shift,
    cotangent,
):
    shards = (
        w_query,
        w_key,
        w_value,
        b_query,
        b_value,
        w_out,
        b_out,
        first_gain,
        first_shift,
        w_up,
        b_up,
        w_down,
        b_down,
        second_gain,
        second_shift,
    )
    gathered = (
        lax.all_gather(shards[0], ("bucket", "ctx"), axis=0, tiled=True),
        lax.all_gather(shards[1], ("bucket", "ctx"), axis=0, tiled=True),
        lax.all_gather(shards[2], ("bucket", "ctx"), axis=0, tiled=True),
        lax.all_gather(shards[3], ("bucket", "ctx"), axis=0, tiled=True),
        lax.all_gather(shards[4], ("bucket", "ctx"), axis=0, tiled=True),
        lax.all_gather(shards[5], ("bucket", "ctx"), axis=0, tiled=True),
        lax.all_gather(shards[6], ("bucket", "ctx"), axis=0, tiled=True),
        lax.all_gather(shards[7], ("bucket", "ctx"), axis=0, tiled=True),
        lax.all_gather(shards[8], ("bucket", "ctx"), axis=0, tiled=True),
        lax.all_gather(shards[9], ("bucket", "ctx"), axis=0, tiled=True),
        lax.all_gather(shards[10], ("bucket", "ctx"), axis=0, tiled=True),
        lax.all_gather(shards[11], ("bucket", "ctx"), axis=0, tiled=True),
        lax.all_gather(shards[12], ("bucket", "ctx"), axis=0, tiled=True),
        lax.all_gather(shards[13], ("bucket", "ctx"), axis=0, tiled=True),
        lax.all_gather(shards[14], ("bucket", "ctx"), axis=0, tiled=True),
    )
    (
        query_mat,
        key_mat,
        value_mat,
        query_bias,
        value_bias,
        out_mat,
        out_bias,
        gain_one,
        shift_one,
        up_mat,
        up_bias,
        down_mat,
        down_bias,
        gain_two,
        shift_two,
    ) = gathered
    seq_count = hidden_in.shape[1]
    local_rows = hidden_in.shape[2]
    model_width = hidden_in.shape[3]
    head_count = model_width // HEAD_DIM
    total_rows = seq_count * local_rows
    block_shape = (seq_count, local_rows, model_width)
    score_scale = HEAD_DIM ** (-0.5)
    seq_total = local_rows * lax.axis_size("ctx")
    group_index = lax.axis_index("bucket")
    seq_slots = jnp.right_shift(jnp.int32(lengths.shape[2]), group_index)
    slot_len = jnp.int32(seq_total) // seq_slots
    seq_info = (lengths[0], slot_len)
    own_start = lax.axis_index("ctx") * local_rows
    tokens = hidden_in.reshape(total_rows, model_width)
    query_low = rounded(matmul(tokens, query_mat) + widened(query_bias))
    key_low = rounded(matmul(tokens, key_mat))
    value_low = rounded(matmul(tokens, value_mat) + widened(value_bias))
    query_heads = split_heads(query_low.reshape(block_shape))
    key_rows = key_low.reshape(block_shape)
    value_rows = value_low.reshape(block_shape)

    def stats_step(running, sliced, anchor):
        scores, allowed = score_block(
            query_heads, split_heads(sliced[0]), own_start, anchor, seq_info
        )
        run_max, run_total = running
        new_max = jnp.maximum(run_max, jnp.max(scores, axis=-1))
        raised = jnp.where(allowed, jnp.exp(scores - new_max[..., None]), 0.0)
        return (new_max, run_total * jnp.exp(run_max - new_max) + jnp.sum(raised, axis=-1))

    stat_shape = (seq_count, head_count, local_rows)
    stats_start = (jnp.full(stat_shape, NEG_FILL, jnp.float32), jnp.zeros(stat_shape, jnp.float32))
    run_max, run_total = over_blocks(
        stats_step, stats_start, (lax.all_gather(key_rows, "ctx", axis=1, tiled=True),)
    )
    log_total = run_max + jnp.log(run_total)

    def output_step(running, sliced, anchor):
        key4 = split_heads(sliced[0])
        value4 = split_heads(sliced[1])
        scores, allowed = score_block(query_heads, key4, own_start, anchor, seq_info)
        probs_low = rounded(jnp.where(allowed, jnp.exp(scores - log_total[..., None]), 0.0))
        return running + jnp.einsum(
            "shqk,skhd->sqhd", probs_low, value4, preferred_element_type=jnp.float32
        )

    attended_f32 = over_blocks(
        output_step,
        jnp.zeros(query_heads.shape, jnp.float32),
        (
            lax.all_gather(key_rows, "ctx", axis=1, tiled=True),
            lax.all_gather(value_rows, "ctx", axis=1, tiled=True),
        ),
    )
    attended_low = rounded(attended_f32.reshape(total_rows, model_width))
    branch = matmul(attended_low, out_mat) + widened(out_bias)
    middle, normed_one, inv_one = norm_forward(
        widened(tokens) + branch, widened(gain_one), widened(shift_one)
    )
    middle_low = rounded(middle)
    pre_act = matmul(middle_low, up_mat) + widened(up_bias)
    activated = rounded(plain_gelu_value(pre_act))
    ffn_out = matmul(activated, down_mat) + widened(down_bias)
    result, normed_two, inv_two = norm_forward(
        middle + ffn_out, widened(gain_two), widened(shift_two)
    )
    hidden_out = rounded(result).reshape(hidden_in.shape)
    gathered = (
        lax.all_gather(shards[0], ("bucket", "ctx"), axis=0, tiled=True),
        lax.all_gather(shards[1], ("bucket", "ctx"), axis=0, tiled=True),
        lax.all_gather(shards[2], ("bucket", "ctx"), axis=0, tiled=True),
        lax.all_gather(shards[3], ("bucket", "ctx"), axis=0, tiled=True),
        lax.all_gather(shards[4], ("bucket", "ctx"), axis=0, tiled=True),
        lax.all_gather(shards[5], ("bucket", "ctx"), axis=0, tiled=True),
        lax.all_gather(shards[6], ("bucket", "ctx"), axis=0, tiled=True),
        lax.all_gather(shards[7], ("bucket", "ctx"), axis=0, tiled=True),
        lax.all_gather(shards[8], ("bucket", "ctx"), axis=0, tiled=True),
        lax.all_gather(shards[9], ("bucket", "ctx"), axis=0, tiled=True),
        lax.all_gather(shards[10], ("bucket", "ctx"), axis=0, tiled=True),
        lax.all_gather(shards[11], ("bucket", "ctx"), axis=0, tiled=True),
        lax.all_gather(shards[12], ("bucket", "ctx"), axis=0, tiled=True),
        lax.all_gather(shards[13], ("bucket", "ctx"), axis=0, tiled=True),
        lax.all_gather(shards[14], ("bucket", "ctx"), axis=0, tiled=True),
    )
    query_mat = gathered[0]
    key_mat = gathered[1]
    value_mat = gathered[2]
    out_mat = gathered[5]
    gain_one = gathered[7]
    up_mat = gathered[9]
    down_mat = gathered[11]
    gain_two = gathered[13]
    incoming = widened(cotangent.reshape(total_rows, model_width))
    grad_two_sum, grad_second_gain, grad_second_shift = norm_backward(
        incoming, normed_two, inv_two, widened(gain_two)
    )
    grad_ffn = rounded(grad_two_sum)
    grad_b_down = jnp.sum(widened(grad_ffn), axis=0)
    grad_w_down = row_inner(activated, grad_ffn)
    grad_act = widened(rounded(right_inner(grad_ffn, down_mat)))
    grad_pre = rounded(grad_act * plain_gelu_slope(pre_act))
    grad_b_up = jnp.sum(widened(grad_pre), axis=0)
    grad_w_up = row_inner(middle_low, grad_pre)
    grad_middle = grad_two_sum + widened(rounded(right_inner(grad_pre, up_mat)))
    grad_one_sum, grad_first_gain, grad_first_shift = norm_backward(
        grad_middle, normed_one, inv_one, widened(gain_one)
    )
    grad_branch = rounded(grad_one_sum)
    grad_b_out = jnp.sum(widened(grad_branch), axis=0)
    grad_w_out = row_inner(attended_low, grad_branch)
    grad_att = rounded(right_inner(grad_branch, out_mat)).reshape(block_shape)
    grad_att_heads = split_heads(grad_att)
    delta = jnp.einsum("sqhd,sqhd->shq", widened(grad_att_heads), attended_f32)

    def grad_terms(query4, key4, value4, att4, row_log, row_delta, query_start, key_start):
        scores, allowed = score_block(query4, key4, query_start, key_start, seq_info)
        probs = jnp.where(allowed, jnp.exp(scores - row_log[..., None]), 0.0)
        slope = jnp.einsum("sqhd,skhd->shqk", att4, value4, preferred_element_type=jnp.float32)
        return (rounded(probs), rounded(probs * (slope - row_delta[..., None])))

    def query_step(running, sliced, anchor):
        key4 = split_heads(sliced[0])
        value4 = split_heads(sliced[1])
        probs_low, score_grad = grad_terms(
            query_heads, key4, value4, grad_att_heads, log_total, delta, own_start, anchor
        )
        return (
            running
            + jnp.einsum("shqk,skhd->sqhd", score_grad, key4, preferred_element_type=jnp.float32)
            * score_scale
        )

    grad_q = over_blocks(
        query_step,
        jnp.zeros(query_heads.shape, jnp.float32),
        (
            lax.all_gather(key_rows, "ctx", axis=1, tiled=True),
            lax.all_gather(value_rows, "ctx", axis=1, tiled=True),
        ),
    )
    log_all, delta_all = (
        lax.all_gather(log_total, "ctx", axis=2, tiled=True),
        lax.all_gather(delta, "ctx", axis=2, tiled=True),
    )
    own_keys = split_heads(key_rows)
    own_values = split_heads(value_rows)

    def owner_step(running, sliced, anchor):
        query4 = split_heads(sliced[0])
        att4 = split_heads(sliced[1])
        count_here = sliced[0].shape[1]
        row_log = lax.dynamic_slice_in_dim(log_all, anchor, count_here, 2)
        row_delta = lax.dynamic_slice_in_dim(delta_all, anchor, count_here, 2)
        probs_low, score_grad = grad_terms(
            query4, own_keys, own_values, att4, row_log, row_delta, anchor, own_start
        )
        grad_k, grad_v = running
        grad_k = (
            grad_k
            + jnp.einsum("shqk,sqhd->skhd", score_grad, query4, preferred_element_type=jnp.float32)
            * score_scale
        )
        grad_v = grad_v + jnp.einsum(
            "shqk,sqhd->skhd", probs_low, att4, preferred_element_type=jnp.float32
        )
        return (grad_k, grad_v)

    owner_start = (jnp.zeros(own_keys.shape, jnp.float32), jnp.zeros(own_keys.shape, jnp.float32))
    grad_k_own, grad_v_own = over_blocks(
        owner_step,
        owner_start,
        (
            lax.all_gather(query_low.reshape(block_shape), "ctx", axis=1, tiled=True),
            lax.all_gather(grad_att, "ctx", axis=1, tiled=True),
        ),
    )
    grad_q_low = rounded(grad_q.reshape(total_rows, model_width))
    grad_k_low = rounded(grad_k_own.reshape(total_rows, model_width))
    grad_v_low = rounded(grad_v_own.reshape(total_rows, model_width))
    grad_w_query = row_inner(tokens, grad_q_low)
    grad_b_query = jnp.sum(widened(grad_q_low), axis=0)
    grad_w_key = row_inner(tokens, grad_k_low)
    grad_w_value = row_inner(tokens, grad_v_low)
    grad_b_value = jnp.sum(widened(grad_v_low), axis=0)
    grad_in = (
        grad_one_sum
        + right_inner(grad_q_low, query_mat)
        + right_inner(grad_k_low, key_mat)
        + right_inner(grad_v_low, value_mat)
    )
    owned = (
        lax.psum_scatter(grad_w_query, ("bucket", "ctx"), scatter_dimension=0, tiled=True),
        lax.psum_scatter(grad_w_key, ("bucket", "ctx"), scatter_dimension=0, tiled=True),
        lax.psum_scatter(grad_w_value, ("bucket", "ctx"), scatter_dimension=0, tiled=True),
        lax.psum_scatter(grad_b_query, ("bucket", "ctx"), scatter_dimension=0, tiled=True),
        lax.psum_scatter(grad_b_value, ("bucket", "ctx"), scatter_dimension=0, tiled=True),
        lax.psum_scatter(grad_w_out, ("bucket", "ctx"), scatter_dimension=0, tiled=True),
        lax.psum_scatter(grad_b_out, ("bucket", "ctx"), scatter_dimension=0, tiled=True),
        lax.psum_scatter(grad_first_gain, ("bucket", "ctx"), scatter_dimension=0, tiled=True),
        lax.psum_scatter(grad_first_shift, ("bucket", "ctx"), scatter_dimension=0, tiled=True),
        lax.psum_scatter(grad_w_up, ("bucket", "ctx"), scatter_dimension=0, tiled=True),
        lax.psum_scatter(grad_b_up, ("bucket", "ctx"), scatter_dimension=0, tiled=True),
        lax.psum_scatter(grad_w_down, ("bucket", "ctx"), scatter_dimension=0, tiled=True),
        lax.psum_scatter(grad_b_down, ("bucket", "ctx"), scatter_dimension=0, tiled=True),
        lax.psum_scatter(grad_second_gain, ("bucket", "ctx"), scatter_dimension=0, tiled=True),
        lax.psum_scatter(grad_second_shift, ("bucket", "ctx"), scatter_dimension=0, tiled=True),
    )
    return (hidden_out, grad_in.reshape(hidden_in.shape)) + tuple(owned)


def solution(mesh):
    placed = (
        P("bucket", None, "ctx", None),
        P("bucket", None, None),
        P(("bucket", "ctx"), None),
        P(("bucket", "ctx"), None),
        P(("bucket", "ctx"), None),
        P(("bucket", "ctx")),
        P(("bucket", "ctx")),
        P(("bucket", "ctx"), None),
        P(("bucket", "ctx")),
        P(("bucket", "ctx")),
        P(("bucket", "ctx")),
        P(("bucket", "ctx"), None),
        P(("bucket", "ctx")),
        P(("bucket", "ctx"), None),
        P(("bucket", "ctx")),
        P(("bucket", "ctx")),
        P(("bucket", "ctx")),
        P("bucket", None, "ctx", None),
    )
    def body(*arguments):
        here = dict(mesh.shape) == {"bucket": 4, "ctx": 8}
        shapes = arguments[0].shape == (1, 1, 128, 1024) and arguments[11].shape == (32, 4096)
        return (fast_body if here and shapes else general_body)(*arguments)

    return jax.shard_map(
        body,
        mesh=mesh,
        in_specs=placed,
        out_specs=(
            P("bucket", None, "ctx", None),
            P("bucket", None, "ctx", None),
            P(("bucket", "ctx"), None),
            P(("bucket", "ctx"), None),
            P(("bucket", "ctx"), None),
            P(("bucket", "ctx")),
            P(("bucket", "ctx")),
            P(("bucket", "ctx"), None),
            P(("bucket", "ctx")),
            P(("bucket", "ctx")),
            P(("bucket", "ctx")),
            P(("bucket", "ctx"), None),
            P(("bucket", "ctx")),
            P(("bucket", "ctx"), None),
            P(("bucket", "ctx")),
            P(("bucket", "ctx")),
            P(("bucket", "ctx")),
        ),
        check_vma=False,
    )
```
